32 devices in a mesh: section: 2 (over core), dp: 8 (over z, y), mp: 2 (over x).
Axes of the slice: x: 2, y: 2, z: 4, core: 2. Of those that a mesh axis runs over, the one named last changes fastest.
Arguments:
- qkv: bfloat16 [1024, 3072], P('dp', ('section', 'mp')), may hold values from -6 to 6
- kv_cache: bfloat16 [512, 8, 2048], P('dp', None, ('section', 'mp')), may hold values from -6 to 6
- residual: bfloat16 [1024, 2048], P('dp'), may hold values from -6 to 6
- out_weight: bfloat16 [1024, 2048], P(('section', 'mp')), may hold values from -0.1875 to 0.1875
- moe_gain: float32 [2048], replicated, may hold values from 0.1 to 1.9
- w_gate: bfloat16 [8, 2048, 1408], P('dp', None, ('section', 'mp')), may hold values from -0.125 to 0.125
- w_up: bfloat16 [8, 2048, 1408], P('dp', None, ('section', 'mp')), may hold values from -0.125 to 0.125
- w_down: bfloat16 [8, 1408, 2048], P('dp', ('section', 'mp')), may hold values from -0.15625 to 0.15625
- seg_ids: int32 [8, 1, 128], P('dp'), may hold values from 0 to 3, never falling along the last dimension, each value on 1 to 64 neighbouring positions
- prefix_blocks: int32 [8, 1, 4], P('dp'), may hold values from 1 to 32, 64 in all within a row
- owners: int32 [8, 1, 64, 1], replicated, may hold values from 0 to 7; in each aligned block of 64 rows (0 to 63, 64 to 127, ..., all dimensions but the last counted through in order) at most 24 rows name the same one
- slot_ids: int32 [8, 1, 64], replicated, may hold values from 0 to 63
- expert_ids: int32 [1024, 4], P('dp'), may hold values from 0 to 7, all different within a row; in each aligned block of 32 rows (0 to 31, 32 to 63, ...) at most 32 rows name the same one
- gate_weights: float32 [1024, 4], P('dp'), may hold values from 0.05 to 0.5
Outputs:
- layer_out: bfloat16 [1024, 2048], P('dp', ('section', 'mp'))
The draws below stay inside these ranges and needn't reach their ends.
Inputs may be any that keep to these rules, and one draw needn't show every extreme that they name: seg_ids[g, m] never falls along the tokens; each of the 4 requests has 1 to 64 tokens, one exactly 64. `prefix_blocks`: the 4 counts of each (g, m) sum to 64, one of them is 32. `owners`: in each block table of 64 entries no owner appears more than 24 times, and some owner appears exactly 24 times in some table. `expert_ids`: each token names 4 different experts; in each aligned block of 32 tokens no expert is named by more than 32 tokens, a bound that some block reaches.
All inputs are finite; a program needn't handle non-finite values.
Results may differ from the reference program's by a relative error of at most 0.009.
Values may be sent and summed in bfloat16 or wider, within the bound.
A program may use at most 64 MiB of HBM per device.

```python
import math
from functools import partial
import jax
import jax.numpy as jnp
import numpy as np
from jax import lax

D = 2048
HEADS = 8
HEAD_DIM = 128
FFE = 1408
TOPK = 4
MICRO = 1
PREF = 64
BLK = 8
SLOTS = 64
SEGS = 4
SPLIT = 4
EXPERTS = 8
TOKENS = 1024
MB = 128
QROWS = 32
CAPQ = 32
OWN_CAP = 24
SEG_MOST = 64
PMOST = 32
N_DP = 8


def draw_qkv(key, part):
    shape = (TOKENS, HEADS, 3, HEAD_DIM)
    base = jnp.clip(jax.random.normal(key, shape, jnp.float32), -6.0, 6.0)
    return base.reshape(TOKENS, HEADS * 3 * HEAD_DIM).astype(jnp.bfloat16)


def set_ends(result, rng, low, top_value):
    spot = [jax.random.randint(jax.random.fold_in(rng, axis), (), 0, length) for axis, length in enumerate(result.shape)]
    longest = result.shape.index(max(result.shape))
    beside = spot[:longest] + [(spot[longest] + 1) % result.shape[longest]] + spot[longest + 1:]
    return result.at[tuple(spot)].set(low).at[tuple(beside)].set(top_value)


def block_levels(own_key, shape, shards, least, largest):
    loudness, own = 1.0, jax.random.fold_in(own_key, 6)
    for dim, shards_of in shards:
        heights = jnp.exp(jax.random.uniform(jax.random.fold_in(own, dim), (shards_of,), jnp.float32, least / len(shards), largest / len(shards)))
        loudness = loudness * jnp.repeat(heights, shape[dim] // shards_of).reshape([-1 if axis == dim else 1 for axis in range(len(shape))])
    return loudness


def profile(number_of, total, bound, slope):
    weights = [(1 << 20) // math.isqrt(grade ** slope) + 1 for grade in range(2, number_of + 1)]
    rest, holding = total - bound - (number_of - 1), [1] * (number_of - 1)
    while rest > 0:
        free = [i for i in range(number_of - 1) if holding[i] < bound]
        whole, left = sum([weights[i] for i in free]), rest
        for i in free:
            extra = min(bound - holding[i], max(1, left * weights[i] // whole), rest)
            holding[i] = holding[i] + extra
            rest = rest - extra
    return np.array([bound] + holding)


def uneven(own_key, amount, total, limit, lean):
    if amount == 2:
        one = jax.random.randint(own_key, (), max(1, total - limit), min(limit, total - 1) + 1)
        return jnp.stack([one, total - one])
    tallies = jnp.asarray(profile(amount, total, limit, lean), jnp.int32)
    couples = (amount - 1) // 2
    donor, receiver = tallies[1:1 + 2 * couples:2], tallies[2:2 + 2 * couples:2]
    margin = jnp.minimum(donor - 1, limit - receiver)
    moved = jax.random.randint(jax.random.fold_in(own_key, 1), (couples,), 0, 1 << 20) % (margin + 1)
    tallies = tallies.at[1:1 + 2 * couples:2].set(donor - moved).at[2:2 + 2 * couples:2].set(receiver + moved)
    return tallies[jax.random.permutation(jax.random.fold_in(own_key, 2), amount)]


def assign_block(own_key, own, number, rows, amount, top, bound, slope):
    order = jax.random.permutation(own_key, amount)
    heavy_load, usual = shares(amount, rows * top, bound, slope, True), shares(amount, rows * top, bound, slope, False)
    places = jnp.arange(amount)

    def named(sizes, offset_by):
        used = int((sizes > 0).sum())
        fixed = max(1, used // 4)
        passed = fixed + (places - fixed + offset_by * (used - fixed)) % max(1, amount - fixed)
        return jnp.zeros((amount,), jnp.int32).at[order[jnp.where(places < fixed, places, passed)]].set(jnp.asarray(sizes, jnp.int32))

    sizes = jnp.where(number % 4 == 0, named(heavy_load, number // 4), named(usual, number - number // 4 - 1))
    mixed = jax.random.permutation(jax.random.fold_in(own, 3), amount)
    donor, taker = mixed[0:amount // 2 * 2:2], mixed[1:amount // 2 * 2:2]
    room = jnp.minimum(sizes[donor] - 1, bound - sizes[taker]) // 2
    room = jnp.where((donor == order[0]) | (taker == order[0]) | (sizes[taker] == 0), 0, jnp.maximum(room, 0))
    passed = jax.random.randint(jax.random.fold_in(own, 4), (amount // 2,), 0, 1 << 20) % (room + 1)
    sizes = sizes.at[donor].add(-passed).at[taker].add(passed)
    labels = jnp.searchsorted(jnp.cumsum(sizes), jnp.arange(rows * top), side="right").astype(jnp.int32)
    listing = labels.reshape(top, rows).T
    listing = listing[jax.random.permutation(jax.random.fold_in(own, 1), rows)]
    offset_by = jax.random.randint(jax.random.fold_in(own, 2), (rows, 1), 0, top)
    return jnp.take_along_axis(listing, (jnp.arange(top)[None, :] + offset_by) % top, axis=1)


def shares(number_of, total, most, slope, full):
    weights = [(1 << 20) // math.isqrt(rank ** slope) + 1 for rank in range(1, number_of + 1)]
    largest = most if full else min(most, max(-(-total // number_of), total * weights[0] // sum(weights)))
    least = 1 if total - largest >= number_of - 1 else 0
    given, rest = [largest] + [least] * (number_of - 1), total - largest - least * (number_of - 1)
    while rest > 0:
        movable = [i for i in range(1, number_of) if given[i] < largest] or [i for i in range(1, number_of) if given[i] < most]
        pool, remaining = sum([weights[i] for i in movable]), rest
        for i in movable:
            addition = min(most - given[i], max(1, remaining * weights[i] // pool), rest)
            given[i] = given[i] + addition
            rest = rest - addition
    return np.array(given)


def gaussian(own_key, shape, deviation, reach, cuts=(), kind=jnp.bfloat16):
    entries = deviation * jax.random.normal(own_key, shape, jnp.float32)
    if cuts:
        entries = entries * block_levels(own_key, shape, cuts, -0.22, 0.18)
    return jnp.clip(entries, -reach, reach).astype(kind)


def setup_inputs(seed: int = 0) -> dict:
    splits = jax.random.split(jax.random.key(seed), 15)
    qkv = draw_qkv(jax.random.fold_in(splits[14], 71), 0)
    kv_cache = gaussian(splits[1], (N_DP * SLOTS, BLK, HEADS * 2 * HEAD_DIM), 1.0, 6.0, ((0, 8), (2, 4)))
    residual = gaussian(splits[2], (TOKENS, D), 1.0, 6.0, ((0, 8),))
    out_weight = gaussian(splits[3], (HEADS * HEAD_DIM, D), (HEADS * HEAD_DIM) ** -0.5, 0.1875, ((0, 4),))
    moe_gain = jnp.clip(1.0 + 0.18 * jax.random.normal(splits[4], (D,), jnp.float32), 0.1, 1.9)
    w_gate = gaussian(splits[5], (EXPERTS, D, FFE), D ** -0.5, 0.125, ((0, 8), (2, 4)))
    w_up = gaussian(splits[6], (EXPERTS, D, FFE), D ** -0.5, 0.125, ((0, 8), (2, 4)))
    w_down = gaussian(splits[7], (EXPERTS, FFE, D), FFE ** -0.5, 0.15625, ((0, 8), (1, 4)))
    seg_ids = jax.vmap(lambda own: jnp.searchsorted(jnp.cumsum(uneven(own, SEGS, MB, SEG_MOST, 2)), jnp.arange(MB), side="right"))(jax.random.split(splits[8], N_DP * MICRO)).reshape((N_DP, MICRO, MB)).astype(jnp.int32)
    prefix_blocks = jax.vmap(lambda own: uneven(own, SEGS, PREF, PMOST, 2))(jax.random.split(splits[9], N_DP * MICRO)).reshape((N_DP, MICRO, SEGS)).astype(jnp.int32)
    owners_keys = jax.random.split(jax.random.fold_in(splits[10], 1), N_DP * MICRO * PREF // PREF)
    owners_turns = jax.random.permutation(jax.random.fold_in(splits[10], 3), N_DP * MICRO * PREF // PREF)
    owners = jax.vmap(lambda own, number: assign_block(jax.random.fold_in(splits[10], 2), own, number, PREF, N_DP, 1, OWN_CAP, 1))(owners_keys, owners_turns).reshape((N_DP, MICRO, PREF, 1))
    slot_ids = set_ends(jax.random.randint(splits[11], (N_DP, MICRO, PREF), 0, SLOTS), jax.random.fold_in(splits[11], 1), 0, SLOTS - 1).astype(jnp.int32)
    expert_ids_keys = jax.random.split(jax.random.fold_in(splits[12], 1), TOKENS // QROWS)
    expert_ids_turns = jax.random.permutation(jax.random.fold_in(splits[12], 3), TOKENS // QROWS)
    expert_ids = jax.vmap(lambda own, number: assign_block(jax.random.fold_in(splits[12], 2), own, number, QROWS, EXPERTS, TOPK, CAPQ, 0))(expert_ids_keys, expert_ids_turns).reshape((TOKENS, TOPK))
    gate_weights = jnp.clip(jnp.exp(math.log(0.5) - 2.3025851 * jax.random.uniform(splits[13], (TOKENS, TOPK), jnp.float32) ** block_levels(splits[13], (TOKENS, TOPK), ((0, 8),), -0.2, 0.2)), 0.05, 0.5)
    return {"qkv": qkv, "kv_cache": kv_cache, "residual": residual, "out_weight": out_weight, "moe_gain": moe_gain, "w_gate": w_gate, "w_up": w_up, "w_down": w_down, "seg_ids": seg_ids, "prefix_blocks": prefix_blocks, "owners": owners, "slot_ids": slot_ids, "expert_ids": expert_ids, "gate_weights": gate_weights}


def normalize(hidden, gain):
    square = lax.optimization_barrier(jnp.mean(hidden * hidden, axis=-1, keepdims=True))
    return (hidden * lax.rsqrt(square + 1e-06) * gain).astype(jnp.bfloat16)

def attend_block(tokens, segments, counts, owner_row, slot_row, cache_view):
    mb_rows = tokens.shape[0]
    blocks = cache_view[owner_row, slot_row]
    prefix = blocks.reshape(PREF * BLK, HEADS, 2, HEAD_DIM)
    key_rows = jnp.concatenate([prefix[:, :, 0], tokens[:, :, 1]], axis=0).astype(jnp.float32)
    value_rows = jnp.concatenate([prefix[:, :, 1], tokens[:, :, 2]], axis=0).astype(jnp.float32)
    query_rows = tokens[:, :, 0].astype(jnp.float32)
    block_ends = jnp.cumsum(counts)
    block_index = jnp.arange(PREF, dtype=jnp.int32)
    block_seg = lax.optimization_barrier(jnp.sum((block_ends[None, :] <= block_index[:, None]).astype(jnp.int32), axis=1))
    prefix_seg = jnp.repeat(block_seg, BLK)
    position = jnp.arange(mb_rows, dtype=jnp.int32)
    same_prefix = prefix_seg[None, :] == segments[:, None]
    same_new = (segments[None, :] == segments[:, None]) & (position[None, :] <= position[:, None])
    visible = jnp.concatenate([same_prefix, same_new], axis=1)
    scores = jnp.einsum('qhd,khd->hqk', query_rows, key_rows) * (1.0 / math.sqrt(HEAD_DIM))
    scores = jnp.where(visible[None], scores, -jnp.inf)
    row_max = lax.optimization_barrier(jnp.max(scores, axis=2, keepdims=True))
    weights = jnp.exp(scores - row_max)
    probs = (weights / lax.optimization_barrier(jnp.sum(weights, axis=2, keepdims=True))).astype(jnp.bfloat16)
    combined = jnp.einsum('hqk,khd->qhd', probs.astype(jnp.float32), value_rows)
    return combined.astype(jnp.bfloat16).reshape(mb_rows, HEADS * HEAD_DIM)

def reference(qkv, kv_cache, residual, out_weight, moe_gain, w_gate, w_up, w_down, seg_ids, prefix_blocks, owners, slot_ids, expert_ids, gate_weights):
    qkv_view = qkv.reshape(N_DP, MICRO, MB, HEADS, 3, HEAD_DIM)
    cache_view = kv_cache.reshape(N_DP, SLOTS, BLK, HEADS, 2, HEAD_DIM)
    attend_one = partial(attend_block, cache_view=cache_view)
    attended = jax.vmap(jax.vmap(attend_one))(qkv_view, seg_ids, prefix_blocks, owners[..., 0], slot_ids)
    attended = attended.reshape(TOKENS, HEADS * HEAD_DIM)
    attn_proj = jnp.dot(attended, out_weight, preferred_element_type=jnp.float32)
    mixed_in = residual.astype(jnp.float32) + attn_proj
    normed = normalize(mixed_in, moe_gain.astype(jnp.float32))
    block_count = TOKENS // QROWS
    block_ids = expert_ids.reshape(block_count, QROWS * TOPK)
    one_hot = (block_ids[:, :, None] == jnp.arange(EXPERTS, dtype=jnp.int32)[None, None, :]).astype(jnp.int32)
    block_rank = lax.optimization_barrier(jnp.sum((jnp.cumsum(one_hot, axis=1) - one_hot) * one_hot, axis=2))
    block_number = jnp.arange(block_count, dtype=jnp.int32)
    quarter_of = block_number % SPLIT
    micro_group = block_number // SPLIT
    capacity = SPLIT * CAPQ
    buffer_rows = N_DP * MICRO * capacity
    slot_of = quarter_of[:, None] * CAPQ + block_rank
    target = (block_ids * (N_DP * MICRO) + micro_group[:, None]) * capacity + slot_of
    token_index = block_number[:, None] * QROWS + jnp.arange(QROWS * TOPK, dtype=jnp.int32)[None, :] // TOPK
    row_table = jnp.full((EXPERTS * buffer_rows,), TOKENS, jnp.int32).at[target.reshape(-1)].set(token_index.reshape(-1))
    gate_table = jnp.zeros((EXPERTS * buffer_rows,), jnp.float32).at[target.reshape(-1)].set(gate_weights.reshape(-1))
    padded = jnp.concatenate([normed, jnp.zeros((1, D), jnp.bfloat16)], axis=0)
    group_width = FFE // SPLIT

    def one_expert(total, inputs):
        gate_w, up_w, down_w, rows_index, row_gates = inputs
        gathered = padded[rows_index]
        gate_rows = jnp.dot(gathered, gate_w, preferred_element_type=jnp.float32)
        up_rows = jnp.dot(gathered, up_w, preferred_element_type=jnp.float32)
        hidden = (jax.nn.silu(gate_rows) * up_rows).astype(jnp.bfloat16)
        output = jnp.zeros((rows_index.shape[0], D), jnp.float32)
        for piece_index in range(SPLIT):
            lower = piece_index * group_width
            piece_out = jnp.dot(hidden[:, lower:lower + group_width], down_w[lower:lower + group_width], preferred_element_type=jnp.float32)
            rounded = lax.optimization_barrier(piece_out.astype(jnp.bfloat16))
            output = output + rounded.astype(jnp.float32)
        total = total.at[rows_index].add(output * row_gates[:, None])
        return (total, None)
    moe_total, unused = lax.scan(one_expert, jnp.zeros((TOKENS + 1, D), jnp.float32), (w_gate, w_up, w_down, row_table.reshape(EXPERTS, buffer_rows), gate_table.reshape(EXPERTS, buffer_rows)))
    return (mixed_in + moe_total[:TOKENS]).astype(jnp.bfloat16)
```

```python
import math
from functools import partial

import jax
import jax.numpy as jnp
from jax import lax
from jax.experimental import pallas as pl
from jax.experimental.pallas import tpu as pltpu
from jax.sharding import PartitionSpec as P

HEAD_DIM = 128
TOPK = 4
PREF = 64
BLK = 8
MESH = pl.DeviceIdType.MESH
DENSE_GROUPS = 8
NEG = -1e30


def normalize(hidden, gain):
    square = jnp.mean(hidden * hidden, axis=-1, keepdims=True)
    return (hidden * lax.rsqrt(square + 1e-06) * gain).astype(jnp.bfloat16)


def expert_rows(inputs, w_gate, w_up, w_down):
    model_width = inputs.shape[-1]
    flat_rows = inputs.reshape(-1, model_width)
    gate_rows = jnp.dot(flat_rows, w_gate[0], preferred_element_type=jnp.float32)
    up_rows = jnp.dot(flat_rows, w_up[0], preferred_element_type=jnp.float32)
    hidden = (jax.nn.silu(gate_rows) * up_rows).astype(jnp.bfloat16)
    result = jnp.dot(hidden, w_down[0], preferred_element_type=jnp.float32).astype(jnp.bfloat16)
    return result.reshape(inputs.shape[:-1] + (result.shape[-1],))


def slot_table(pair_ids, pair_slots, experts, capacity):
    pair_count = pair_ids.shape[0]
    expert_match = pair_ids[None, None, :] == jnp.arange(experts, dtype=jnp.int32)[:, None, None]
    slot_match = pair_slots[None, None, :] == jnp.arange(capacity, dtype=jnp.int32)[None, :, None]
    pair_match = expert_match & slot_match
    token_of = jnp.arange(pair_count, dtype=jnp.int32) // TOPK
    source = jnp.sum(jnp.where(pair_match, token_of[None, None, :], 0), axis=2)
    filled = jnp.any(pair_match, axis=2)
    return (source, filled)


def dispatch_rows(normed, source, filled):
    gathered = jnp.take(normed, source.reshape(-1), axis=0).reshape(
        source.shape + (normed.shape[-1],)
    )
    return jnp.where(filled[:, :, None], gathered, jnp.zeros_like(gathered))


def local_sparse(
    qkv,
    kv_cache,
    residual,
    out_weight,
    moe_gain,
    w_gate,
    w_up,
    w_down,
    seg_ids,
    prefix_blocks,
    owners,
    slot_ids,
    expert_ids,
    gate_weights,
):
    groups = lax.axis_size("dp")
    shards = lax.axis_size("section") * lax.axis_size("mp")
    group_index = lax.axis_index("dp")
    shard_index = lax.axis_index("section") * lax.axis_size("mp") + lax.axis_index("mp")
    mb_rows = seg_ids.shape[2]
    quarter_rows = mb_rows // shards
    model_width = residual.shape[1]
    part_cols = model_width // shards
    head_cols = out_weight.shape[0]
    heads_local = head_cols // HEAD_DIM
    cache_cols = kv_cache.shape[2]
    quarter_cap = min(quarter_rows, max(2, 2 * quarter_rows * TOPK // groups))
    capacity = shards * quarter_cap
    owner_cap = max(3, 3 * PREF // groups)
    score_scale = 1.0 / math.sqrt(HEAD_DIM)
    own_table = owners[:, 0, :, 0]
    slot_table_m = slot_ids[:, 0, :]
    owned_here = own_table == group_index
    local_order = jnp.cumsum(owned_here.astype(jnp.int32), axis=1) - 1
    wanted = owned_here[:, None, :] & (
        local_order[:, None, :] == jnp.arange(owner_cap, dtype=jnp.int32)[None, :, None]
    )
    slot_pick = jnp.sum(jnp.where(wanted, slot_table_m[:, None, :], 0), axis=2)
    filled = jnp.any(wanted, axis=2)
    chosen = jnp.take(kv_cache, slot_pick.reshape(-1), axis=0).reshape(
        groups, owner_cap, BLK, cache_cols
    )
    chosen = jnp.where(filled[:, :, None, None], chosen, jnp.zeros_like(chosen))
    arrived = lax.all_to_all(chosen, "dp", split_axis=0, concat_axis=0, tiled=True)
    my_owner = lax.dynamic_index_in_dim(own_table, group_index, 0, keepdims=False)
    block_index = jnp.arange(PREF, dtype=jnp.int32)
    earlier = (my_owner[None, :] == my_owner[:, None]) & (
        block_index[None, :] < block_index[:, None]
    )
    my_rank = jnp.sum(earlier.astype(jnp.int32), axis=1)
    where_from = my_owner * owner_cap + my_rank
    prefix = jnp.take(arrived.reshape(groups * owner_cap, BLK, cache_cols), where_from, axis=0)
    prefix = prefix.reshape(PREF * BLK, heads_local, 2, HEAD_DIM)
    tokens = qkv
    tokens = tokens.reshape(mb_rows, heads_local, 3, HEAD_DIM)
    query_rows = tokens[:, :, 0]
    key_rows = jnp.concatenate([prefix[:, :, 0], tokens[:, :, 1]], axis=0)
    value_rows = jnp.concatenate([prefix[:, :, 1], tokens[:, :, 2]], axis=0)
    segments = seg_ids[0, 0]
    block_ends = jnp.cumsum(prefix_blocks[0, 0])
    block_seg = jnp.sum((block_ends[None, :] <= block_index[:, None]).astype(jnp.int32), axis=1)
    prefix_seg = jnp.repeat(block_seg, BLK)
    position = jnp.arange(mb_rows, dtype=jnp.int32)
    same_prefix = prefix_seg[None, :] == segments[:, None]
    same_new = (segments[None, :] == segments[:, None]) & (position[None, :] <= position[:, None])
    visible = jnp.concatenate([same_prefix, same_new], axis=1)
    scores = (
        jnp.einsum("qhd,khd->hqk", query_rows, key_rows, preferred_element_type=jnp.float32)
        * score_scale
    )
    scores = jnp.where(visible[None], scores, -jnp.inf)
    row_max = jnp.max(scores, axis=2, keepdims=True)
    weights = jnp.exp(scores - row_max)
    attention = (weights / jnp.sum(weights, axis=2, keepdims=True)).astype(jnp.bfloat16)
    combined = jnp.einsum("hqk,khd->qhd", attention, value_rows, preferred_element_type=jnp.float32)
    attended_now = combined.astype(jnp.bfloat16).reshape(mb_rows, head_cols)
    stream = residual.astype(jnp.float32)
    projected = jnp.dot(attended_now, out_weight, preferred_element_type=jnp.float32)
    quarter_ids = expert_ids.reshape(shards, quarter_rows * TOPK)
    one_hot = (
        quarter_ids[:, :, None] == jnp.arange(groups, dtype=jnp.int32)[None, None, :]
    ).astype(jnp.int32)
    quarter_rank = jnp.sum((jnp.cumsum(one_hot, axis=1) - one_hot) * one_hot, axis=2)
    flat_ids = expert_ids.reshape(-1)
    flat_slot = (quarter_rank + jnp.arange(shards, dtype=jnp.int32)[:, None] * quarter_cap).reshape(
        -1
    )
    mixed_in = stream + lax.psum(projected, ("section", "mp"))
    normed = normalize(mixed_in, moe_gain)
    source, filled = slot_table(flat_ids, flat_slot, groups, capacity)
    outgoing = dispatch_rows(normed, source, filled)
    incoming = lax.all_to_all(outgoing, "dp", split_axis=0, concat_axis=0, tiled=True)
    produced = expert_rows(incoming, w_gate, w_up, w_down)
    returned = lax.all_to_all(produced, "dp", split_axis=0, concat_axis=0, tiled=True)
    position = flat_ids * capacity + flat_slot
    picked = jnp.take(returned.reshape(groups * capacity, model_width), position, axis=0)
    picked = picked.reshape(mb_rows, TOPK, model_width)
    weighted = jnp.einsum("tk,tkd->td", gate_weights, picked.astype(jnp.float32))
    moe_full = lax.psum(weighted.astype(jnp.bfloat16), ("section", "mp")).astype(jnp.float32)
    finished = (mixed_in + moe_full).astype(jnp.bfloat16).reshape(mb_rows, shards, part_cols)
    return lax.dynamic_index_in_dim(finished, shard_index, 1, keepdims=False)


def remote(src, dst, send, recv, device):
    return pltpu.make_async_remote_copy(
        src_ref=src, dst_ref=dst, send_sem=send, recv_sem=recv, device_id=device, device_id_type=MESH
    )


def contract_last(a, b):
    return lax.dot_general(a, b, (((1,), (1,)), ((), ())), preferred_element_type=jnp.float32)


def layer_kernel(
    groups,
    qkv_ref,
    kv_ref,
    res_ref,
    ow_ref,
    gain_ref,
    wg_hbm,
    wu_hbm,
    wd_hbm,
    meta_ref,
    table_ref,
    cw_ref,
    out_ref,
    wg,
    wu,
    wd,
    qb,
    mb,
    os,
    orv,
    mls,
    mlr,
    ps,
    pr,
    ss,
    nb,
    xb,
    yown,
    ys,
    yr,
    rs,
    rb,
    mixed,
    w_local,
    w_send,
    w_recv,
    q_send,
    q_recv,
    m_send,
    m_recv,
    o_send,
    o_recv,
    l_send,
    l_recv,
    p_send,
    p_recv,
    s_send,
    s_recv,
    x_send,
    x_recv,
    f_send,
    y_send,
    y_recv,
    r_send,
    r_recv,
):
    s = lax.axis_index("section")
    g = lax.axis_index("dp")
    m = lax.axis_index("mp")
    q = s * 2 + m
    rows = qkv_ref.shape[0]
    wide = out_ref.shape[1]
    half = groups // 2
    scale = 1.0 / math.sqrt(HEAD_DIM)
    core_peer = (1 - s, g, m)
    x_peer = (s, g, 1 - m)

    barrier = pltpu.get_barrier_semaphore()

    def greet(k, carry):
        other = lax.rem(s * groups + g + k, 2 * groups)
        pl.semaphore_signal(
            barrier, inc=1, device_id=(other // groups, lax.rem(other, groups), m), device_id_type=MESH
        )
        return carry

    lax.fori_loop(1, 2 * groups, greet, 0)
    pl.semaphore_signal(barrier, inc=1, device_id=x_peer, device_id_type=MESH)
    pl.semaphore_signal(barrier, inc=1, device_id=(1 - s, g, 1 - m), device_id_type=MESH)

    for h in range(2):
        qb[g, :, h * HEAD_DIM : (h + 1) * HEAD_DIM] = qkv_ref[:, h * 3 * HEAD_DIM : h * 3 * HEAD_DIM + HEAD_DIM]
    mb[g] = meta_ref[...]
    pl.semaphore_wait(barrier, 2 * groups + 1)

    def send_query(k, carry):
        to = (s, lax.rem(g + k, groups), m)
        remote(mb.at[g], mb.at[g], m_send.at[k], m_recv.at[g], to).start()
        remote(qb.at[g], qb.at[g], q_send.at[k], q_recv.at[g], to).start()
        return carry

    lax.fori_loop(1, groups, send_query, 0)

    weights = ((wg_hbm, wg), (wu_hbm, wu), (wd_hbm, wd))
    for i, (hbm, vmem) in enumerate(weights):
        pltpu.make_async_copy(hbm.at[0], vmem.at[s], w_local.at[i]).start()
        remote(hbm.at[0], vmem.at[s], w_send.at[i], w_recv.at[i], core_peer).start()

    lane = lax.broadcasted_iota(jnp.int32, (rows, HEAD_DIM), 1)
    row = lax.broadcasted_iota(jnp.int32, (rows, HEAD_DIM), 0)

    def same_request(meta, line):
        own = jnp.broadcast_to(meta[0:1, :], (rows, HEAD_DIM)).T
        return own == jnp.broadcast_to(meta[line : line + 1, :], (rows, HEAD_DIM))

    def serve(k, carry):
        asker = lax.rem(g - k + groups, groups)
        back = (s, asker, m)

        @pl.when(k > 0)
        def _():
            remote(mb.at[asker], mb.at[asker], m_send.at[k], m_recv.at[asker], back).wait_recv()
            remote(qb.at[asker], qb.at[asker], q_send.at[k], q_recv.at[asker], back).wait_recv()

        seen = same_request(mb[asker].astype(jnp.float32), 1)
        seen = jnp.where(seen, 1.0, 0.0).astype(jnp.bfloat16)
        count = jnp.dot(seen, table_ref[asker], preferred_element_type=jnp.float32)
        facts = jnp.zeros((rows, HEAD_DIM), jnp.float32)
        for h in range(2):
            query = qb[asker, :, h * HEAD_DIM : (h + 1) * HEAD_DIM]
            key = kv_ref[:, h * 2 * HEAD_DIM : h * 2 * HEAD_DIM + HEAD_DIM]
            value = kv_ref[:, h * 2 * HEAD_DIM + HEAD_DIM : (h + 1) * 2 * HEAD_DIM]
            scores = jnp.where(count > 0.0, contract_last(query, key) * scale, NEG)
            top = jnp.max(scores, axis=1, keepdims=True)
            weight = jnp.exp(scores - top) * count
            total = jnp.sum(weight, axis=1, keepdims=True)
            part = jnp.dot(weight.astype(jnp.bfloat16), value, preferred_element_type=jnp.float32)
            os[asker, :, h * HEAD_DIM : (h + 1) * HEAD_DIM] = part.astype(jnp.bfloat16)
            facts = jnp.where(lane == 2 * h, top, jnp.where(lane == 2 * h + 1, total, facts))
        mls[asker] = facts.T[0:8, :]

        @pl.when(k > 0)
        def _():
            remote(mls.at[asker], mlr.at[g], l_send.at[k], l_recv.at[g], back).start()
            remote(os.at[asker], orv.at[g], o_send.at[k], o_recv.at[g], back).start()

        @pl.when(k == 0)
        def _():
            mlr[g] = mls[g]
            orv[g] = os[g]

        return carry

    lax.fori_loop(0, groups, serve, 0)

    visible = same_request(meta_ref[...].astype(jnp.float32), 0) & (lane <= row)
    fresh = []
    for h in range(2):
        base = h * 3 * HEAD_DIM
        scores = contract_last(qkv_ref[:, base : base + HEAD_DIM], qkv_ref[:, base + HEAD_DIM : base + 2 * HEAD_DIM])
        scores = jnp.where(visible, scores * scale, NEG)
        top = jnp.max(scores, axis=1, keepdims=True)
        weight = jnp.where(visible, jnp.exp(scores - top), 0.0)
        total = jnp.sum(weight, axis=1, keepdims=True)
        part = jnp.dot(
            weight.astype(jnp.bfloat16),
            qkv_ref[:, base + 2 * HEAD_DIM : base + 3 * HEAD_DIM],
            preferred_element_type=jnp.float32,
        )
        fresh.append((top, total, part))

    def arrive_part(k, carry):
        owner = lax.rem(g + k, groups)
        back = (s, owner, m)
        remote(mls.at[owner], mlr.at[owner], l_send.at[k], l_recv.at[owner], back).wait_recv()
        remote(os.at[owner], orv.at[owner], o_send.at[k], o_recv.at[owner], back).wait_recv()
        return carry

    lax.fori_loop(1, groups, arrive_part, 0)

    facts = mlr[...].reshape(groups * 8, HEAD_DIM)
    facts = jnp.concatenate([facts, jnp.zeros((HEAD_DIM - groups * 8, HEAD_DIM), jnp.float32)], axis=0).T
    attended = []
    for h in range(2):
        top, total, part = fresh[h]
        best = top
        for e in range(groups):
            best = jnp.maximum(best, facts[:, e * 8 + 2 * h : e * 8 + 2 * h + 1])
        factor = jnp.exp(top - best)
        mass = factor * total
        mix = factor * part
        for e in range(groups):
            factor = jnp.exp(facts[:, e * 8 + 2 * h : e * 8 + 2 * h + 1] - best)
            mass = mass + factor * facts[:, e * 8 + 2 * h + 1 : e * 8 + 2 * h + 2]
            mix = mix + factor * orv[e, :, h * HEAD_DIM : (h + 1) * HEAD_DIM].astype(jnp.float32)
        attended.append((mix / mass).astype(jnp.bfloat16))
    attended = jnp.concatenate(attended, axis=1)

    def project(to):
        cols = pl.ds(pl.multiple_of(to * wide, wide), wide)
        return jnp.dot(attended, ow_ref[:, cols], preferred_element_type=jnp.float32)

    for j in (1, 3, 2):
        to = lax.rem(q + j, 4)
        ps[to] = project(to).astype(jnp.bfloat16)
        remote(ps.at[to], pr.at[q], p_send.at[j], p_recv.at[q], (to // 2, g, lax.rem(to, 2))).start()
    mine = pl.ds(pl.multiple_of(q * wide, wide), wide)
    stream = res_ref[:, mine].astype(jnp.float32) + project(q)
    for j in (1, 3, 2):
        at = lax.rem(q + j, 4)
        remote(ps.at[at], pr.at[at], p_send.at[j], p_recv.at[at], (at // 2, g, lax.rem(at, 2))).wait_recv()
        stream = stream + pr[at].astype(jnp.float32)
    mixed[...] = stream

    square = jnp.sum(stream * stream, axis=1, keepdims=True)
    ss[q] = jnp.broadcast_to(square, (rows, HEAD_DIM)).T[0:8, :]
    for j in (1, 2, 3):
        to = lax.rem(q + j, 4)
        remote(ss.at[q], ss.at[q], s_send.at[j], s_recv.at[q], (to // 2, g, lax.rem(to, 2))).start()
    for j in (1, 2, 3):
        at = lax.rem(q + j, 4)
        remote(ss.at[at], ss.at[at], s_send.at[j], s_recv.at[at], (at // 2, g, lax.rem(at, 2))).wait_recv()
    square = ss[0] + ss[1] + ss[2] + ss[3]
    square = jnp.broadcast_to(square[0:1, :], (rows, HEAD_DIM)).T[:, 0:1]
    inverse = lax.rsqrt(square * (1.0 / (4 * wide)) + 1e-06)
    nb[...] = (stream * inverse * gain_ref[:, mine]).astype(jnp.bfloat16)

    side = lax.rem(g, 2)
    place = g // 2

    @pl.when(s == side)
    def _():
        xb[place, q] = nb[...]

    @pl.when(s != side)
    def _():
        remote(nb, xb.at[place, q], x_send.at[0], x_recv.at[place, q], core_peer).start()

    def dispatch(k, carry):
        to = (side, lax.rem(g + k, groups), m)
        remote(nb, xb.at[place, q], x_send.at[k], x_recv.at[place, q], to).start()
        return carry

    lax.fori_loop(1, groups, dispatch, 0)

    for i, (hbm, vmem) in enumerate(weights):
        pltpu.make_async_copy(hbm.at[0], vmem.at[s], w_local.at[i]).wait()
        remote(hbm.at[0], vmem.at[1 - s], w_send.at[i], w_recv.at[i], core_peer).wait()

    first = lax.rem(g + s, 2)

    def slot_of(i):
        from_group = lax.rem(g - first - 2 * i + 2 * groups, groups)
        return from_group, from_group // 2

    def forward(i):
        asker, at = slot_of(i)
        for c in range(2):
            piece = 2 * c + m

            @pl.when((asker != g) | (c != s))
            def _():
                remote(nb, xb.at[at, piece], x_send.at[0], x_recv.at[at, piece], core_peer).wait_recv()

            remote(xb.at[at, piece], xb.at[at, piece], f_send.at[at, c], x_recv.at[at, piece], x_peer).start()

    def compute(i):
        asker, at = slot_of(i)
        for c in range(2):
            piece = 2 * c + 1 - m
            remote(xb.at[at, piece], xb.at[at, piece], f_send.at[at, c], x_recv.at[at, piece], x_peer).wait_recv()
        hidden = []
        for c in range(2):
            gate = jnp.zeros((rows, wg.shape[2]), jnp.float32)
            up = jnp.zeros((rows, wg.shape[2]), jnp.float32)
            for piece in range(4):
                rows_in = xb[at, piece]
                gate += jnp.dot(
                    rows_in, wg[c, piece * wide : (piece + 1) * wide, :], preferred_element_type=jnp.float32
                )
                up += jnp.dot(rows_in, wu[c, piece * wide : (piece + 1) * wide, :], preferred_element_type=jnp.float32)
            hidden.append((gate / (1.0 + jnp.exp(-gate)) * up).astype(jnp.bfloat16))

        def down(piece):
            cols = pl.ds(pl.multiple_of(piece * wide, wide), wide)
            return jnp.dot(hidden[0], wd[0, :, cols], preferred_element_type=jnp.float32) + jnp.dot(
                hidden[1], wd[1, :, cols], preferred_element_type=jnp.float32
            )

        for c in range(2):
            ys[at, c] = down(2 * c + 1 - m).astype(jnp.bfloat16)
            remote(ys.at[at, c], yr.at[at, c], y_send.at[at, c], y_recv.at[at, c], x_peer).start()
        for c in range(2):
            yown[at, c] = down(2 * c + m)

    def give_back(i):
        asker, at = slot_of(i)
        for c in range(2):
            remote(ys.at[at, c], yr.at[at, c], y_send.at[at, c], y_recv.at[at, c], x_peer).wait_recv()
            rs[at, c] = (yown[at, c] + yr[at, c].astype(jnp.float32)).astype(jnp.bfloat16)
            is_mine = (asker == g) & (c == s)

            @pl.when(is_mine)
            def _():
                rb[g] = rs[at, c]

            @pl.when(jnp.logical_not(is_mine))
            def _():
                remote(rs.at[at, c], rb.at[g], r_send.at[at, c], r_recv.at[g], (c, asker, m)).start()

    def step(t, carry):
        @pl.when(t < half)
        def _():
            forward(t)

        @pl.when((t >= 1) & (t <= half))
        def _():
            compute(t - 1)

        @pl.when(t >= 2)
        def _():
            give_back(t - 2)

        return carry

    lax.fori_loop(0, half + 2, step, 0)

    stream = mixed[...]
    for e in range(groups):

        @pl.when((e != g) | (s != side))
        def _():
            remote(rs.at[0, 0], rb.at[e], r_send.at[0, 0], r_recv.at[e], core_peer).wait_recv()

        stream = stream + cw_ref[:, e : e + 1] * rb[e].astype(jnp.float32)
    out_ref[...] = stream.astype(jnp.bfloat16)

    def drain(k, carry):
        to = (s, lax.rem(g + k, groups), m)
        remote(mb.at[g], mb.at[g], m_send.at[k], m_recv.at[g], to).wait_send()
        remote(qb.at[g], qb.at[g], q_send.at[k], q_recv.at[g], to).wait_send()
        remote(mls.at[0], mlr.at[g], l_send.at[k], l_recv.at[g], to).wait_send()
        remote(os.at[0], orv.at[g], o_send.at[k], o_recv.at[g], to).wait_send()
        remote(nb, xb.at[place, q], x_send.at[k], x_recv.at[place, q], to).wait_send()
        return carry

    lax.fori_loop(1, groups, drain, 0)

    @pl.when(s != side)
    def _():
        remote(nb, xb.at[place, q], x_send.at[0], x_recv.at[place, q], core_peer).wait_send()

    for j in (1, 2, 3):
        remote(ps.at[0], pr.at[q], p_send.at[j], p_recv.at[q], core_peer).wait_send()
        remote(ss.at[q], ss.at[q], s_send.at[j], s_recv.at[q], core_peer).wait_send()

    def drain_slot(i, carry):
        asker, at = slot_of(i)
        for c in range(2):
            remote(xb.at[at, 0], xb.at[at, 0], f_send.at[at, c], x_recv.at[at, 0], x_peer).wait_send()
            remote(ys.at[at, c], yr.at[at, c], y_send.at[at, c], y_recv.at[at, c], x_peer).wait_send()

            @pl.when((asker != g) | (c != s))
            def _():
                remote(rs.at[at, c], rb.at[g], r_send.at[at, c], r_recv.at[g], core_peer).wait_send()

        return carry

    lax.fori_loop(0, half, drain_slot, 0)


def local_dense(
    qkv,
    kv_cache,
    residual,
    out_weight,
    moe_gain,
    w_gate,
    w_up,
    w_down,
    seg_ids,
    prefix_blocks,
    owners,
    slot_ids,
    expert_ids,
    gate_weights,
):
    groups = lax.axis_size("dp")
    group_index = lax.axis_index("dp")
    rows = qkv.shape[0]
    model_width = residual.shape[1]
    wide = model_width // 4
    half = groups // 2
    hid = w_gate.shape[2]
    slots = kv_cache.shape[0]
    kv = kv_cache.reshape(slots * BLK, kv_cache.shape[2])
    block_ends = jnp.cumsum(prefix_blocks[0, 0])
    block_index = jnp.arange(PREF, dtype=jnp.int32)
    block_seg = jnp.sum((block_ends[None, :] <= block_index[:, None]).astype(jnp.int32), axis=1)
    block_seg = jnp.pad(block_seg, (0, HEAD_DIM - PREF), constant_values=-1)
    meta = jnp.concatenate([seg_ids[0], block_seg[None, :], jnp.zeros((6, HEAD_DIM), jnp.int32)], axis=0)
    mine = jnp.where(owners[:, 0, :, 0] == group_index, slot_ids[:, 0, :], -1)
    mine = jnp.pad(mine, ((0, 0), (0, HEAD_DIM - PREF)), constant_values=-1)
    row_slot = jnp.arange(slots * BLK, dtype=jnp.int32) // BLK
    table = (mine[:, :, None] == row_slot[None, None, :]).astype(jnp.bfloat16)
    chosen = expert_ids[:, :, None] == jnp.arange(groups, dtype=jnp.int32)[None, None, :]
    combine = jnp.sum(jnp.where(chosen, gate_weights[:, :, None], 0.0), axis=1)
    bf, f32 = jnp.bfloat16, jnp.float32
    dma = pltpu.SemaphoreType.DMA
    vmem = pl.BlockSpec(memory_space=pltpu.VMEM)
    anywhere = pl.BlockSpec(memory_space=pl.ANY)
    return pl.pallas_call(
        partial(layer_kernel, groups),
        out_shape=jax.ShapeDtypeStruct((rows, wide), bf),
        in_specs=[vmem] * 5 + [anywhere] * 3 + [vmem] * 3,
        out_specs=vmem,
        scratch_shapes=[
            pltpu.VMEM((2, model_width, hid), bf),
            pltpu.VMEM((2, model_width, hid), bf),
            pltpu.VMEM((2, hid, model_width), bf),
            pltpu.VMEM((groups, rows, 2 * HEAD_DIM), bf),
            pltpu.VMEM((groups, 8, HEAD_DIM), jnp.int32),
            pltpu.VMEM((groups, rows, 2 * HEAD_DIM), bf),
            pltpu.VMEM((groups, rows, 2 * HEAD_DIM), bf),
            pltpu.VMEM((groups, 8, HEAD_DIM), f32),
            pltpu.VMEM((groups, 8, HEAD_DIM), f32),
            pltpu.VMEM((4, rows, wide), bf),
            pltpu.VMEM((4, rows, wide), bf),
            pltpu.VMEM((4, 8, HEAD_DIM), f32),
            pltpu.VMEM((rows, wide), bf),
            pltpu.VMEM((half, 4, rows, wide), bf),
            pltpu.VMEM((half, 2, rows, wide), f32),
            pltpu.VMEM((half, 2, rows, wide), bf),
            pltpu.VMEM((half, 2, rows, wide), bf),
            pltpu.VMEM((half, 2, rows, wide), bf),
            pltpu.VMEM((groups, rows, wide), bf),
            pltpu.VMEM((rows, wide), f32),
            dma((3,)),
            dma((3,)),
            dma((3,)),
            dma((groups,)),
            dma((groups,)),
            dma((groups,)),
            dma((groups,)),
            dma((groups,)),
            dma((groups,)),
            dma((groups,)),
            dma((groups,)),
            dma((4,)),
            dma((4,)),
            dma((4,)),
            dma((4,)),
            dma((groups,)),
            dma((half, 4)),
            dma((half, 2)),
            dma((half, 2)),
            dma((half, 2)),
            dma((half, 2)),
            dma((groups,)),
        ],
        compiler_params=pltpu.CompilerParams(
            collective_id=0, has_side_effects=True, vmem_limit_bytes=48 * 1024 * 1024
        ),
    )(
        qkv,
        kv,
        residual,
        out_weight,
        moe_gain.reshape(1, -1),
        w_gate,
        w_up,
        w_down,
        meta,
        table,
        combine,
    )


def solution(mesh):
    dense = mesh.shape["dp"] <= DENSE_GROUPS
    return jax.shard_map(
        local_dense if dense else local_sparse,
        mesh=mesh,
        in_specs=(
            P("dp", ("section", "mp")),
            P("dp", None, ("section", "mp")),
            P("dp", None),
            P(("section", "mp"), None),
            P(),
            P("dp", None, ("section", "mp")),
            P("dp", None, ("section", "mp")),
            P("dp", ("section", "mp"), None),
            P("dp", None, None),
            P("dp", None, None),
            P(),
            P(),
            P("dp", None),
            P("dp", None),
        ),
        out_specs=P("dp", ("section", "mp")),
        check_vma=False,
    )
```

```python
import math
from functools import partial

import jax
import jax.numpy as jnp
from jax import lax
from jax.experimental import pallas as pl
from jax.experimental.pallas import tpu as pltpu
from jax.sharding import PartitionSpec as P

HEAD_DIM = 128
TOPK = 4
PREF = 64
BLK = 8
MESH = pl.DeviceIdType.MESH
DENSE_GROUPS = 8
NEG = -1e30


def normalize(hidden, gain):
    square = jnp.mean(hidden * hidden, axis=-1, keepdims=True)
    return (hidden * lax.rsqrt(square + 1e-06) * gain).astype(jnp.bfloat16)


def expert_rows(inputs, w_gate, w_up, w_down):
    model_width = inputs.shape[-1]
    flat_rows = inputs.reshape(-1, model_width)
    gate_rows = jnp.dot(flat_rows, w_gate[0], preferred_element_type=jnp.float32)
    up_rows = jnp.dot(flat_rows, w_up[0], preferred_element_type=jnp.float32)
    hidden = (jax.nn.silu(gate_rows) * up_rows).astype(jnp.bfloat16)
    result = jnp.dot(hidden, w_down[0], preferred_element_type=jnp.float32).astype(jnp.bfloat16)
    return result.reshape(inputs.shape[:-1] + (result.shape[-1],))


def slot_table(pair_ids, pair_slots, experts, capacity):
    pair_count = pair_ids.shape[0]
    expert_match = pair_ids[None, None, :] == jnp.arange(experts, dtype=jnp.int32)[:, None, None]
    slot_match = pair_slots[None, None, :] == jnp.arange(capacity, dtype=jnp.int32)[None, :, None]
    pair_match = expert_match & slot_match
    token_of = jnp.arange(pair_count, dtype=jnp.int32) // TOPK
    source = jnp.sum(jnp.where(pair_match, token_of[None, None, :], 0), axis=2)
    filled = jnp.any(pair_match, axis=2)
    return (source, filled)


def dispatch_rows(normed, source, filled):
    gathered = jnp.take(normed, source.reshape(-1), axis=0).reshape(
        source.shape + (normed.shape[-1],)
    )
    return jnp.where(filled[:, :, None], gathered, jnp.zeros_like(gathered))


def local_sparse(
    qkv,
    kv_cache,
    residual,
    out_weight,
    moe_gain,
    w_gate,
    w_up,
    w_down,
    seg_ids,
    prefix_blocks,
    owners,
    slot_ids,
    expert_ids,
    gate_weights,
):
    groups = lax.axis_size("dp")
    shards = lax.axis_size("section") * lax.axis_size("mp")
    group_index = lax.axis_index("dp")
    shard_index = lax.axis_index("section") * lax.axis_size("mp") + lax.axis_index("mp")
    mb_rows = seg_ids.shape[2]
    quarter_rows = mb_rows // shards
    model_width = residual.shape[1]
    part_cols = model_width // shards
    head_cols = out_weight.shape[0]
    heads_local = head_cols // HEAD_DIM
    cache_cols = kv_cache.shape[2]
    quarter_cap = min(quarter_rows, max(2, 2 * quarter_rows * TOPK // groups))
    capacity = shards * quarter_cap
    owner_cap = max(3, 3 * PREF // groups)
    score_scale = 1.0 / math.sqrt(HEAD_DIM)
    own_table = owners[:, 0, :, 0]
    slot_table_m = slot_ids[:, 0, :]
    owned_here = own_table == group_index
    local_order = jnp.cumsum(owned_here.astype(jnp.int32), axis=1) - 1
    wanted = owned_here[:, None, :] & (
        local_order[:, None, :] == jnp.arange(owner_cap, dtype=jnp.int32)[None, :, None]
    )
    slot_pick = jnp.sum(jnp.where(wanted, slot_table_m[:, None, :], 0), axis=2)
    filled = jnp.any(wanted, axis=2)
    chosen = jnp.take(kv_cache, slot_pick.reshape(-1), axis=0).reshape(
        groups, owner_cap, BLK, cache_cols
    )
    chosen = jnp.where(filled[:, :, None, None], chosen, jnp.zeros_like(chosen))
    arrived = lax.all_to_all(chosen, "dp", split_axis=0, concat_axis=0, tiled=True)
    my_owner = lax.dynamic_index_in_dim(own_table, group_index, 0, keepdims=False)
    block_index = jnp.arange(PREF, dtype=jnp.int32)
    earlier = (my_owner[None, :] == my_owner[:, None]) & (
        block_index[None, :] < block_index[:, None]
    )
    my_rank = jnp.sum(earlier.astype(jnp.int32), axis=1)
    where_from = my_owner * owner_cap + my_rank
    prefix = jnp.take(arrived.reshape(groups * owner_cap, BLK, cache_cols), where_from, axis=0)
    prefix = prefix.reshape(PREF * BLK, heads_local, 2, HEAD_DIM)
    tokens = qkv
    tokens = tokens.reshape(mb_rows, heads_local, 3, HEAD_DIM)
    query_rows = tokens[:, :, 0]
    key_rows = jnp.concatenate([prefix[:, :, 0], tokens[:, :, 1]], axis=0)
    value_rows = jnp.concatenate([prefix[:, :, 1], tokens[:, :, 2]], axis=0)
    segments = seg_ids[0, 0]
    block_ends = jnp.cumsum(prefix_blocks[0, 0])
    block_seg = jnp.sum((block_ends[None, :] <= block_index[:, None]).astype(jnp.int32), axis=1)
    prefix_seg = jnp.repeat(block_seg, BLK)
    position = jnp.arange(mb_rows, dtype=jnp.int32)
    same_prefix = prefix_seg[None, :] == segments[:, None]
    same_new = (segments[None, :] == segments[:, None]) & (position[None, :] <= position[:, None])
    visible = jnp.concatenate([same_prefix, same_new], axis=1)
    scores = (
        jnp.einsum("qhd,khd->hqk", query_rows, key_rows, preferred_element_type=jnp.float32)
        * score_scale
    )
    scores = jnp.where(visible[None], scores, -jnp.inf)
    row_max = jnp.max(scores, axis=2, keepdims=True)
    weights = jnp.exp(scores - row_max)
    attention = (weights / jnp.sum(weights, axis=2, keepdims=True)).astype(jnp.bfloat16)
    combined = jnp.einsum("hqk,khd->qhd", attention, value_rows, preferred_element_type=jnp.float32)
    attended_now = combined.astype(jnp.bfloat16).reshape(mb_rows, head_cols)
    stream = residual.astype(jnp.float32)
    projected = jnp.dot(attended_now, out_weight, preferred_element_type=jnp.float32)
    quarter_ids = expert_ids.reshape(shards, quarter_rows * TOPK)
    one_hot = (
        quarter_ids[:, :, None] == jnp.arange(groups, dtype=jnp.int32)[None, None, :]
    ).astype(jnp.int32)
    quarter_rank = jnp.sum((jnp.cumsum(one_hot, axis=1) - one_hot) * one_hot, axis=2)
    flat_ids = expert_ids.reshape(-1)
    flat_slot = (quarter_rank + jnp.arange(shards, dtype=jnp.int32)[:, None] * quarter_cap).reshape(
        -1
    )
    mixed_in = stream + lax.psum(projected, ("section", "mp"))
    normed = normalize(mixed_in, moe_gain)
    source, filled = slot_table(flat_ids, flat_slot, groups, capacity)
    outgoing = dispatch_rows(normed, source, filled)
    incoming = lax.all_to_all(outgoing, "dp", split_axis=0, concat_axis=0, tiled=True)
    produced = expert_rows(incoming, w_gate, w_up, w_down)
    returned = lax.all_to_all(produced, "dp", split_axis=0, concat_axis=0, tiled=True)
    position = flat_ids * capacity + flat_slot
    picked = jnp.take(returned.reshape(groups * capacity, model_width), position, axis=0)
    picked = picked.reshape(mb_rows, TOPK, model_width)
    weighted = jnp.einsum("tk,tkd->td", gate_weights, picked.astype(jnp.float32))
    moe_full = lax.psum(weighted.astype(jnp.bfloat16), ("section", "mp")).astype(jnp.float32)
    finished = (mixed_in + moe_full).astype(jnp.bfloat16).reshape(mb_rows, shards, part_cols)
    return lax.dynamic_index_in_dim(finished, shard_index, 1, keepdims=False)


def remote(src, dst, send, recv, device):
    return pltpu.make_async_remote_copy(
        src_ref=src, dst_ref=dst, send_sem=send, recv_sem=recv, device_id=device, device_id_type=MESH
    )


def contract_last(a, b):
    return lax.dot_general(a, b, (((1,), (1,)), ((), ())), preferred_element_type=jnp.float32)


def layer_kernel(
    groups,
    qkv_hbm,
    kv_hbm,
    res_hbm,
    ow_hbm,
    gain_ref,
    wg_hbm,
    wu_hbm,
    wd_hbm,
    seg_ref,
    count_ref,
    owner_ref,
    slot_ref,
    ids_ref,
    gates_ref,
    out_ref,
    qkv_ref,
    kv_ref,
    res_ref,
    ow_ref,
    wg,
    wu,
    wd,
    qb,
    mb,
    os,
    orv,
    mls,
    mlr,
    ps,
    pr,
    ss,
    nb,
    xb,
    yown,
    ys,
    yr,
    rs,
    rb,
    mixed,
    in_sem,
    w_local,
    w_send,
    w_recv,
    q_send,
    q_recv,
    m_send,
    m_recv,
    o_send,
    o_recv,
    l_send,
    l_recv,
    p_send,
    p_recv,
    s_send,
    s_recv,
    n_send,
    x_send,
    x_recv,
    f_send,
    y_send,
    y_recv,
    r_send,
    r_recv,
):
    loads = []
    for i, (hbm, vmem) in enumerate(((qkv_hbm, qkv_ref), (kv_hbm, kv_ref), (ow_hbm, ow_ref), (res_hbm, res_ref))):
        loads.append(pltpu.make_async_copy(hbm, vmem, in_sem.at[i]))
        loads[-1].start()
    s = lax.axis_index("section")
    g = lax.axis_index("dp")
    m = lax.axis_index("mp")
    q = s * 2 + m
    z, y = g // 2, lax.rem(g, 2)
    across = g + 1 - 2 * y
    rows = qkv_ref.shape[0]
    wide = out_ref.shape[1]
    half = groups // 2
    half_line = half // 2
    scale = 1.0 / math.sqrt(HEAD_DIM)
    core_peer = (1 - s, g, m)
    x_peer = (s, g, 1 - m)

    barrier = pltpu.get_barrier_semaphore()

    def greet(k, carry):
        other = lax.rem(s * groups + g + k, 2 * groups)
        pl.semaphore_signal(
            barrier, inc=1, device_id=(other // groups, lax.rem(other, groups), m), device_id_type=MESH
        )
        return carry

    lax.fori_loop(1, 2 * groups, greet, 0)
    pl.semaphore_signal(barrier, inc=1, device_id=x_peer, device_id_type=MESH)
    pl.semaphore_signal(barrier, inc=1, device_id=(1 - s, g, 1 - m), device_id_type=MESH)

    def near(i):
        upper = z // half_line
        edge = z + upper * (3 - 2 * z)
        pick = (i // 2) * i + (1 - i // 2) * lax.rem(i + edge, 2)
        return pick + upper * (3 - 2 * pick)

    def relay(at, piece, sends, recv, sec, mine):
        @pl.when((at <= z) & (z < half - 1))
        def _():
            remote(piece, piece, sends.at[0], recv, (sec, g + 2, mine)).start()

        @pl.when((at >= z) & (z > 0))
        def _():
            remote(piece, piece, sends.at[1], recv, (sec, g - 2, mine)).start()

        remote(piece, piece, sends.at[2], recv, (sec, across, mine)).start()

    def relay_done(at, piece, sends, recv):
        @pl.when((at <= z) & (z < half - 1))
        def _():
            remote(piece, piece, sends.at[0], recv, x_peer).wait_send()

        @pl.when((at >= z) & (z > 0))
        def _():
            remote(piece, piece, sends.at[1], recv, x_peer).wait_send()

        remote(piece, piece, sends.at[2], recv, x_peer).wait_send()

    lane = lax.broadcasted_iota(jnp.int32, (rows, HEAD_DIM), 1)
    row = lax.broadcasted_iota(jnp.int32, (rows, HEAD_DIM), 0)
    ends = count_ref[0, 0]
    block_seg = jnp.zeros((8, HEAD_DIM), jnp.int32)
    for r in range(count_ref.shape[1] - 1):
        block_seg += jnp.where(lane[0:8] >= ends, 1, 0)
        ends = ends + count_ref[0, r + 1]
    meta = jnp.where(row[0:8] == 0, jnp.broadcast_to(seg_ref[...], (8, HEAD_DIM)), block_seg)
    mb[g] = meta
    loads[0].wait()
    for h in range(2):
        qb[g, :, h * HEAD_DIM : (h + 1) * HEAD_DIM] = qkv_ref[:, h * 3 * HEAD_DIM : h * 3 * HEAD_DIM + HEAD_DIM]
    pl.semaphore_wait(barrier, 2 * groups + 1)

    def take_query(src):
        remote(mb.at[src], mb.at[src], m_send.at[src, 0], m_recv.at[src], x_peer).wait_recv()
        remote(qb.at[src], qb.at[src], q_send.at[src, 0], q_recv.at[src], x_peer).wait_recv()

    def forward_query(i):
        at = near(i)
        src = at * 2 + y

        @pl.when(at != z)
        def _():
            take_query(src)

        relay(at, mb.at[src], m_send.at[src], m_recv.at[src], s, m)
        relay(at, qb.at[src], q_send.at[src], q_recv.at[src], s, m)

    forward_query(0)

    weights = ((wg_hbm, wg), (wu_hbm, wu), (wd_hbm, wd))
    for i, (hbm, vmem) in enumerate(weights):
        pltpu.make_async_copy(hbm.at[0], vmem.at[s], w_local.at[i]).start()
        remote(hbm.at[0], vmem.at[s], w_send.at[i], w_recv.at[i], core_peer).start()

    key_slot = lax.broadcasted_iota(jnp.int32, (kv_ref.shape[0], PREF), 0) // BLK

    def same_request(meta, line):
        own = jnp.broadcast_to(meta[0:1, :], (rows, HEAD_DIM)).T
        return own == jnp.broadcast_to(meta[line : line + 1, :], (rows, HEAD_DIM))

    def serve(asker):
        back = (s, asker, m)
        seen = same_request(mb[asker].astype(jnp.float32), 1)
        seen = jnp.where(seen, 1.0, 0.0).astype(jnp.bfloat16)[:, :PREF]
        held = jnp.where(owner_ref[pl.ds(asker, 1), :] == g, slot_ref[pl.ds(asker, 1), :], -1)
        held = jnp.broadcast_to(held, key_slot.shape) == key_slot
        count = contract_last(seen, jnp.where(held, 1.0, 0.0).astype(jnp.bfloat16))
        facts = jnp.zeros((rows, HEAD_DIM), jnp.float32)
        for h in range(2):
            query = qb[asker, :, h * HEAD_DIM : (h + 1) * HEAD_DIM]
            key = kv_ref[:, h * 2 * HEAD_DIM : h * 2 * HEAD_DIM + HEAD_DIM]
            value = kv_ref[:, h * 2 * HEAD_DIM + HEAD_DIM : (h + 1) * 2 * HEAD_DIM]
            scores = jnp.where(count > 0.0, contract_last(query, key) * scale, NEG)
            top = jnp.max(scores, axis=1, keepdims=True)
            weight = jnp.exp(scores - top) * count
            total = jnp.sum(weight, axis=1, keepdims=True)
            part = jnp.dot(weight.astype(jnp.bfloat16), value, preferred_element_type=jnp.float32)
            os[asker, :, h * HEAD_DIM : (h + 1) * HEAD_DIM] = part.astype(jnp.bfloat16)
            facts = jnp.where(lane == 2 * h, top, jnp.where(lane == 2 * h + 1, total, facts))
        mls[asker] = facts.T[0:8, :]

        @pl.when(asker != g)
        def _():
            remote(mls.at[asker], mlr.at[g], l_send.at[asker], l_recv.at[g], back).start()
            remote(os.at[asker], orv.at[g], o_send.at[asker], o_recv.at[g], back).start()

        @pl.when(asker == g)
        def _():
            mlr[g] = mls[g]
            orv[g] = os[g]

    loads[1].wait()

    def attend_step(t, carry):
        @pl.when(t < half)
        def _():
            forward_query(t)

        @pl.when(t <= half)
        def _():
            serve(near(t - 1) * 2 + y)

        @pl.when(t >= 2)
        def _():
            src = near(t - 2) * 2 + 1 - y
            take_query(src)
            serve(src)

        return carry

    lax.fori_loop(1, half + 2, attend_step, 0)

    visible = same_request(meta.astype(jnp.float32), 0) & (lane <= row)
    fresh = []
    for h in range(2):
        base = h * 3 * HEAD_DIM
        scores = contract_last(qkv_ref[:, base : base + HEAD_DIM], qkv_ref[:, base + HEAD_DIM : base + 2 * HEAD_DIM])
        scores = jnp.where(visible, scores * scale, NEG)
        top = jnp.max(scores, axis=1, keepdims=True)
        weight = jnp.where(visible, jnp.exp(scores - top), 0.0)
        total = jnp.sum(weight, axis=1, keepdims=True)
        part = jnp.dot(
            weight.astype(jnp.bfloat16),
            qkv_ref[:, base + 2 * HEAD_DIM : base + 3 * HEAD_DIM],
            preferred_element_type=jnp.float32,
        )
        fresh.append((top, total, part))

    def arrive_part(k, carry):
        owner = lax.rem(g + k, groups)
        back = (s, owner, m)
        remote(mls.at[owner], mlr.at[owner], l_send.at[owner], l_recv.at[owner], back).wait_recv()
        remote(os.at[owner], orv.at[owner], o_send.at[owner], o_recv.at[owner], back).wait_recv()
        return carry

    lax.fori_loop(1, groups, arrive_part, 0)

    facts = mlr[...].reshape(groups * 8, HEAD_DIM)
    facts = jnp.concatenate([facts, jnp.zeros((HEAD_DIM - groups * 8, HEAD_DIM), jnp.float32)], axis=0).T
    attended = []
    for h in range(2):
        top, total, part = fresh[h]
        best = top
        for e in range(groups):
            best = jnp.maximum(best, facts[:, e * 8 + 2 * h : e * 8 + 2 * h + 1])
        factor = jnp.exp(top - best)
        mass = factor * total
        mix = factor * part
        for e in range(groups):
            factor = jnp.exp(facts[:, e * 8 + 2 * h : e * 8 + 2 * h + 1] - best)
            mass = mass + factor * facts[:, e * 8 + 2 * h + 1 : e * 8 + 2 * h + 2]
            mix = mix + factor * orv[e, :, h * HEAD_DIM : (h + 1) * HEAD_DIM].astype(jnp.float32)
        attended.append((mix / mass).astype(jnp.bfloat16))
    attended = jnp.concatenate(attended, axis=1)

    loads[2].wait()

    def project(to):
        cols = pl.ds(pl.multiple_of(to * wide, wide), wide)
        return jnp.dot(attended, ow_ref[:, cols], preferred_element_type=jnp.float32)

    for j in (1, 3, 2):
        to = lax.rem(q + j, 4)
        ps[to] = project(to).astype(jnp.bfloat16)
        remote(ps.at[to], pr.at[q], p_send.at[j], p_recv.at[q], (to // 2, g, lax.rem(to, 2))).start()
    mine = pl.ds(pl.multiple_of(q * wide, wide), wide)
    loads[3].wait()
    stream = res_ref[:, mine].astype(jnp.float32) + project(q)
    for j in (1, 3, 2):
        at = lax.rem(q + j, 4)
        remote(ps.at[at], pr.at[at], p_send.at[j], p_recv.at[at], (at // 2, g, lax.rem(at, 2))).wait_recv()
        stream = stream + pr[at].astype(jnp.float32)
    mixed[...] = stream

    square = jnp.sum(stream * stream, axis=1, keepdims=True)
    ss[q] = jnp.broadcast_to(square, (rows, HEAD_DIM)).T[0:8, :]
    for j in (1, 2, 3):
        to = lax.rem(q + j, 4)
        remote(ss.at[q], ss.at[q], s_send.at[j], s_recv.at[q], (to // 2, g, lax.rem(to, 2))).start()
    for j in (1, 2, 3):
        at = lax.rem(q + j, 4)
        remote(ss.at[at], ss.at[at], s_send.at[j], s_recv.at[at], (at // 2, g, lax.rem(at, 2))).wait_recv()
    square = ss[0] + ss[1] + ss[2] + ss[3]
    square = jnp.broadcast_to(square[0:1, :], (rows, HEAD_DIM)).T[:, 0:1]
    inverse = lax.rsqrt(square * (1.0 / (4 * wide)) + 1e-06)
    nb[...] = (stream * inverse * gain_ref[:, mine]).astype(jnp.bfloat16)

    @pl.when(s == y)
    def _():
        xb[z, q] = nb[...]

    @pl.when(s != y)
    def _():
        remote(nb, xb.at[z, q], n_send.at[0], x_recv.at[z, q], core_peer).start()

    @pl.when(s == 1)
    def _():
        remote(nb, xb.at[z, q], n_send.at[1], x_recv.at[z, q], (y, g, 1 - m)).start()

    for i, (hbm, vmem) in enumerate(weights):
        pltpu.make_async_copy(hbm.at[0], vmem.at[s], w_local.at[i]).wait()
        remote(hbm.at[0], vmem.at[1 - s], w_send.at[i], w_recv.at[i], core_peer).wait()

    def slot_of(i):
        at = near(i)
        return at * 2 + s, at

    def take_tokens(at, piece):
        remote(nb, xb.at[at, piece], n_send.at[0], x_recv.at[at, piece], x_peer).wait_recv()

    def forward(i):
        asker, at = slot_of(i)
        for piece in (m, 2, 3):

            @pl.when((asker != g) | (piece != q))
            def _():
                take_tokens(at, piece)

            @pl.when(s == y)
            def _():
                relay(at, xb.at[at, piece], x_send.at[at, piece], x_recv.at[at, piece], s, m)

        remote(xb.at[at, m], xb.at[at, m], f_send.at[at], x_recv.at[at, m], x_peer).start()

    def compute(i):
        asker, at = slot_of(i)
        take_tokens(at, 1 - m)
        hidden = []
        for c in range(2):
            gate = jnp.zeros((rows, wg.shape[1]), jnp.float32)
            up = jnp.zeros((rows, wg.shape[1]), jnp.float32)
            for piece in range(4):
                rows_in = xb[at, piece]
                gate += contract_last(rows_in, wg[c, :, piece * wide : (piece + 1) * wide])
                up += contract_last(rows_in, wu[c, :, piece * wide : (piece + 1) * wide])
            hidden.append((gate / (1.0 + jnp.exp(-gate)) * up).astype(jnp.bfloat16))

        def down(piece):
            cols = pl.ds(pl.multiple_of(piece * wide, wide), wide)
            return jnp.dot(hidden[0], wd[0, :, cols], preferred_element_type=jnp.float32) + jnp.dot(
                hidden[1], wd[1, :, cols], preferred_element_type=jnp.float32
            )

        for c in range(2):
            ys[at, c] = down(2 * c + 1 - m).astype(jnp.bfloat16)
            remote(ys.at[at, c], yr.at[at, c], y_send.at[at, c], y_recv.at[at, c], x_peer).start()
        for c in range(2):
            yown[at, c] = down(2 * c + m)

    def give_back(i):
        asker, at = slot_of(i)
        for c in range(2):
            remote(ys.at[at, c], yr.at[at, c], y_send.at[at, c], y_recv.at[at, c], x_peer).wait_recv()
            rs[at, c] = (yown[at, c] + yr[at, c].astype(jnp.float32)).astype(jnp.bfloat16)
            is_mine = (asker == g) & (c == s)

            @pl.when(is_mine)
            def _():
                rb[g] = rs[at, c]

            @pl.when(jnp.logical_not(is_mine))
            def _():
                remote(rs.at[at, c], rb.at[g], r_send.at[at, c], r_recv.at[g], (c, asker, m)).start()

    def step(t, carry):
        @pl.when(t < half)
        def _():
            forward(t)

        @pl.when((t >= 1) & (t <= half))
        def _():
            compute(t - 1)

        @pl.when(t >= 2)
        def _():
            give_back(t - 2)

        return carry

    lax.fori_loop(0, half + 2, step, 0)

    share = jnp.zeros((groups, rows), jnp.float32)
    expert = lax.broadcasted_iota(jnp.int32, (groups, rows), 0)
    for k in range(TOPK):
        named = jnp.broadcast_to(ids_ref[k : k + 1, :], (groups, rows)) == expert
        share += jnp.where(named, jnp.broadcast_to(gates_ref[k : k + 1, :], (groups, rows)), 0.0)
    share = jnp.concatenate([share, jnp.zeros((HEAD_DIM - groups, rows), jnp.float32)], axis=0).T
    stream = mixed[...]
    for e in range(groups):

        @pl.when((e != g) | (s != y))
        def _():
            remote(rs.at[0, 0], rb.at[e], r_send.at[0, 0], r_recv.at[e], core_peer).wait_recv()

        stream = stream + share[:, e : e + 1] * rb[e].astype(jnp.float32)
    out_ref[...] = stream.astype(jnp.bfloat16)

    def drain(k, carry):
        other = lax.rem(g + k, groups)
        remote(mls.at[0], mlr.at[g], l_send.at[other], l_recv.at[g], x_peer).wait_send()
        remote(os.at[0], orv.at[g], o_send.at[other], o_recv.at[g], x_peer).wait_send()
        return carry

    lax.fori_loop(1, groups, drain, 0)

    @pl.when(s != y)
    def _():
        remote(nb, xb.at[z, q], n_send.at[0], x_recv.at[z, q], core_peer).wait_send()

    @pl.when(s == 1)
    def _():
        remote(nb, xb.at[z, q], n_send.at[1], x_recv.at[z, q], x_peer).wait_send()

    for j in (1, 2, 3):
        remote(ps.at[0], pr.at[q], p_send.at[j], p_recv.at[q], core_peer).wait_send()
        remote(ss.at[q], ss.at[q], s_send.at[j], s_recv.at[q], core_peer).wait_send()

    def drain_slot(i, carry):
        asker, at = slot_of(i)
        src = at * 2 + y
        relay_done(at, mb.at[src], m_send.at[src], m_recv.at[src])
        relay_done(at, qb.at[src], q_send.at[src], q_recv.at[src])
        for piece in (m, 2, 3):

            @pl.when(s == y)
            def _():
                relay_done(at, xb.at[at, piece], x_send.at[at, piece], x_recv.at[at, piece])

        remote(xb.at[at, m], xb.at[at, m], f_send.at[at], x_recv.at[at, m], x_peer).wait_send()
        for c in range(2):
            remote(ys.at[at, c], yr.at[at, c], y_send.at[at, c], y_recv.at[at, c], x_peer).wait_send()

            @pl.when((asker != g) | (c != s))
            def _():
                remote(rs.at[at, c], rb.at[g], r_send.at[at, c], r_recv.at[g], core_peer).wait_send()

        return carry

    lax.fori_loop(0, half, drain_slot, 0)


def local_dense(
    qkv,
    kv_cache,
    residual,
    out_weight,
    moe_gain,
    w_gate,
    w_up,
    w_down,
    seg_ids,
    prefix_blocks,
    owners,
    slot_ids,
    expert_ids,
    gate_weights,
):
    groups = lax.axis_size("dp")
    rows = qkv.shape[0]
    model_width = residual.shape[1]
    wide = model_width // 4
    half = groups // 2
    hid = w_gate.shape[2]
    slots = kv_cache.shape[0]
    kv = kv_cache.reshape(slots * BLK, kv_cache.shape[2])
    bf, f32 = jnp.bfloat16, jnp.float32
    dma = pltpu.SemaphoreType.DMA
    vmem = pl.BlockSpec(memory_space=pltpu.VMEM)
    smem = pl.BlockSpec(memory_space=pltpu.SMEM)
    anywhere = pl.BlockSpec(memory_space=pl.ANY)
    return pl.pallas_call(
        partial(layer_kernel, groups),
        out_shape=jax.ShapeDtypeStruct((rows, wide), bf),
        in_specs=[anywhere] * 4 + [vmem] + [anywhere] * 3 + [vmem, smem, vmem, vmem, vmem, vmem],
        out_specs=vmem,
        scratch_shapes=[
            pltpu.VMEM(qkv.shape, bf),
            pltpu.VMEM(kv.shape, bf),
            pltpu.VMEM(residual.shape, bf),
            pltpu.VMEM(out_weight.shape, bf),
            pltpu.VMEM((2, hid, model_width), bf),
            pltpu.VMEM((2, hid, model_width), bf),
            pltpu.VMEM((2, hid, model_width), bf),
            pltpu.VMEM((groups, rows, 2 * HEAD_DIM), bf),
            pltpu.VMEM((groups, 8, HEAD_DIM), jnp.int32),
            pltpu.VMEM((groups, rows, 2 * HEAD_DIM), bf),
            pltpu.VMEM((groups, rows, 2 * HEAD_DIM), bf),
            pltpu.VMEM((groups, 8, HEAD_DIM), f32),
            pltpu.VMEM((groups, 8, HEAD_DIM), f32),
            pltpu.VMEM((4, rows, wide), bf),
            pltpu.VMEM((4, rows, wide), bf),
            pltpu.VMEM((4, 8, HEAD_DIM), f32),
            pltpu.VMEM((rows, wide), bf),
            pltpu.VMEM((half, 4, rows, wide), bf),
            pltpu.VMEM((half, 2, rows, wide), f32),
            pltpu.VMEM((half, 2, rows, wide), bf),
            pltpu.VMEM((half, 2, rows, wide), bf),
            pltpu.VMEM((half, 2, rows, wide), bf),
            pltpu.VMEM((groups, rows, wide), bf),
            pltpu.VMEM((rows, wide), f32),
            dma((4,)),
            dma((3,)),
            dma((3,)),
            dma((3,)),
            dma((groups, 3)),
            dma((groups,)),
            dma((groups, 3)),
            dma((groups,)),
            dma((groups,)),
            dma((groups,)),
            dma((groups,)),
            dma((groups,)),
            dma((4,)),
            dma((4,)),
            dma((4,)),
            dma((4,)),
            dma((2,)),
            dma((half, 4, 3)),
            dma((half, 4)),
            dma((half,)),
            dma((half, 2)),
            dma((half, 2)),
            dma((half, 2)),
            dma((groups,)),
        ],
        compiler_params=pltpu.CompilerParams(
            collective_id=0, has_side_effects=True, vmem_limit_bytes=60 * 1024 * 1024
        ),
    )(
        qkv,
        kv,
        residual,
        out_weight,
        moe_gain.reshape(1, -1),
        jnp.swapaxes(w_gate, 1, 2),
        jnp.swapaxes(w_up, 1, 2),
        w_down,
        seg_ids[0],
        prefix_blocks[0],
        owners[:, 0, :, 0],
        slot_ids[:, 0, :],
        expert_ids.T,
        gate_weights.T,
    )


def solution(mesh):
    dense = mesh.shape["dp"] <= DENSE_GROUPS
    return jax.shard_map(
        local_dense if dense else local_sparse,
        mesh=mesh,
        in_specs=(
            P("dp", ("section", "mp")),
            P("dp", None, ("section", "mp")),
            P("dp", None),
            P(("section", "mp"), None),
            P(),
            P("dp", None, ("section", "mp")),
            P("dp", None, ("section", "mp")),
            P("dp", ("section", "mp"), None),
            P("dp", None, None),
            P("dp", None, None),
            P(),
            P(),
            P("dp", None),
            P("dp", None),
        ),
        out_specs=P("dp", ("section", "mp")),
        check_vma=False,
    )
```

```python
import math
from functools import partial

import jax
import jax.numpy as jnp
from jax import lax
from jax.experimental import pallas as pl
from jax.experimental.pallas import tpu as pltpu
from jax.sharding import PartitionSpec as P

HEAD_DIM = 128
TOPK = 4
PREF = 64
BLK = 8
MESH = pl.DeviceIdType.MESH
DENSE_GROUPS = 8
NEG = -1e30


def normalize(hidden, gain):
    square = jnp.mean(hidden * hidden, axis=-1, keepdims=True)
    return (hidden * lax.rsqrt(square + 1e-06) * gain).astype(jnp.bfloat16)


def expert_rows(inputs, w_gate, w_up, w_down):
    model_width = inputs.shape[-1]
    flat_rows = inputs.reshape(-1, model_width)
    gate_rows = jnp.dot(flat_rows, w_gate[0], preferred_element_type=jnp.float32)
    up_rows = jnp.dot(flat_rows, w_up[0], preferred_element_type=jnp.float32)
    hidden = (jax.nn.silu(gate_rows) * up_rows).astype(jnp.bfloat16)
    result = jnp.dot(hidden, w_down[0], preferred_element_type=jnp.float32).astype(jnp.bfloat16)
    return result.reshape(inputs.shape[:-1] + (result.shape[-1],))


def slot_table(pair_ids, pair_slots, experts, capacity):
    pair_count = pair_ids.shape[0]
    expert_match = pair_ids[None, None, :] == jnp.arange(experts, dtype=jnp.int32)[:, None, None]
    slot_match = pair_slots[None, None, :] == jnp.arange(capacity, dtype=jnp.int32)[None, :, None]
    pair_match = expert_match & slot_match
    token_of = jnp.arange(pair_count, dtype=jnp.int32) // TOPK
    source = jnp.sum(jnp.where(pair_match, token_of[None, None, :], 0), axis=2)
    filled = jnp.any(pair_match, axis=2)
    return (source, filled)


def dispatch_rows(normed, source, filled):
    gathered = jnp.take(normed, source.reshape(-1), axis=0).reshape(
        source.shape + (normed.shape[-1],)
    )
    return jnp.where(filled[:, :, None], gathered, jnp.zeros_like(gathered))


def local_sparse(
    qkv,
    kv_cache,
    residual,
    out_weight,
    moe_gain,
    w_gate,
    w_up,
    w_down,
    seg_ids,
    prefix_blocks,
    owners,
    slot_ids,
    expert_ids,
    gate_weights,
):
    groups = lax.axis_size("dp")
    shards = lax.axis_size("section") * lax.axis_size("mp")
    group_index = lax.axis_index("dp")
    shard_index = lax.axis_index("section") * lax.axis_size("mp") + lax.axis_index("mp")
    mb_rows = seg_ids.shape[2]
    quarter_rows = mb_rows // shards
    model_width = residual.shape[1]
    part_cols = model_width // shards
    head_cols = out_weight.shape[0]
    heads_local = head_cols // HEAD_DIM
    cache_cols = kv_cache.shape[2]
    quarter_cap = min(quarter_rows, max(2, 2 * quarter_rows * TOPK // groups))
    capacity = shards * quarter_cap
    owner_cap = max(3, 3 * PREF // groups)
    score_scale = 1.0 / math.sqrt(HEAD_DIM)
    own_table = owners[:, 0, :, 0]
    slot_table_m = slot_ids[:, 0, :]
    owned_here = own_table == group_index
    local_order = jnp.cumsum(owned_here.astype(jnp.int32), axis=1) - 1
    wanted = owned_here[:, None, :] & (
        local_order[:, None, :] == jnp.arange(owner_cap, dtype=jnp.int32)[None, :, None]
    )
    slot_pick = jnp.sum(jnp.where(wanted, slot_table_m[:, None, :], 0), axis=2)
    filled = jnp.any(wanted, axis=2)
    chosen = jnp.take(kv_cache, slot_pick.reshape(-1), axis=0).reshape(
        groups, owner_cap, BLK, cache_cols
    )
    chosen = jnp.where(filled[:, :, None, None], chosen, jnp.zeros_like(chosen))
    arrived = lax.all_to_all(chosen, "dp", split_axis=0, concat_axis=0, tiled=True)
    my_owner = lax.dynamic_index_in_dim(own_table, group_index, 0, keepdims=False)
    block_index = jnp.arange(PREF, dtype=jnp.int32)
    earlier = (my_owner[None, :] == my_owner[:, None]) & (
        block_index[None, :] < block_index[:, None]
    )
    my_rank = jnp.sum(earlier.astype(jnp.int32), axis=1)
    where_from = my_owner * owner_cap + my_rank
    prefix = jnp.take(arrived.reshape(groups * owner_cap, BLK, cache_cols), where_from, axis=0)
    prefix = prefix.reshape(PREF * BLK, heads_local, 2, HEAD_DIM)
    tokens = qkv
    tokens = tokens.reshape(mb_rows, heads_local, 3, HEAD_DIM)
    query_rows = tokens[:, :, 0]
    key_rows = jnp.concatenate([prefix[:, :, 0], tokens[:, :, 1]], axis=0)
    value_rows = jnp.concatenate([prefix[:, :, 1], tokens[:, :, 2]], axis=0)
    segments = seg_ids[0, 0]
    block_ends = jnp.cumsum(prefix_blocks[0, 0])
    block_seg = jnp.sum((block_ends[None, :] <= block_index[:, None]).astype(jnp.int32), axis=1)
    prefix_seg = jnp.repeat(block_seg, BLK)
    position = jnp.arange(mb_rows, dtype=jnp.int32)
    same_prefix = prefix_seg[None, :] == segments[:, None]
    same_new = (segments[None, :] == segments[:, None]) & (position[None, :] <= position[:, None])
    visible = jnp.concatenate([same_prefix, same_new], axis=1)
    scores = (
        jnp.einsum("qhd,khd->hqk", query_rows, key_rows, preferred_element_type=jnp.float32)
        * score_scale
    )
    scores = jnp.where(visible[None], scores, -jnp.inf)
    row_max = jnp.max(scores, axis=2, keepdims=True)
    weights = jnp.exp(scores - row_max)
    attention = (weights / jnp.sum(weights, axis=2, keepdims=True)).astype(jnp.bfloat16)
    combined = jnp.einsum("hqk,khd->qhd", attention, value_rows, preferred_element_type=jnp.float32)
    attended_now = combined.astype(jnp.bfloat16).reshape(mb_rows, head_cols)
    stream = residual.astype(jnp.float32)
    projected = jnp.dot(attended_now, out_weight, preferred_element_type=jnp.float32)
    quarter_ids = expert_ids.reshape(shards, quarter_rows * TOPK)
    one_hot = (
        quarter_ids[:, :, None] == jnp.arange(groups, dtype=jnp.int32)[None, None, :]
    ).astype(jnp.int32)
    quarter_rank = jnp.sum((jnp.cumsum(one_hot, axis=1) - one_hot) * one_hot, axis=2)
    flat_ids = expert_ids.reshape(-1)
    flat_slot = (quarter_rank + jnp.arange(shards, dtype=jnp.int32)[:, None] * quarter_cap).reshape(
        -1
    )
    mixed_in = stream + lax.psum(projected, ("section", "mp"))
    normed = normalize(mixed_in, moe_gain)
    source, filled = slot_table(flat_ids, flat_slot, groups, capacity)
    outgoing = dispatch_rows(normed, source, filled)
    incoming = lax.all_to_all(outgoing, "dp", split_axis=0, concat_axis=0, tiled=True)
    produced = expert_rows(incoming, w_gate, w_up, w_down)
    returned = lax.all_to_all(produced, "dp", split_axis=0, concat_axis=0, tiled=True)
    position = flat_ids * capacity + flat_slot
    picked = jnp.take(returned.reshape(groups * capacity, model_width), position, axis=0)
    picked = picked.reshape(mb_rows, TOPK, model_width)
    weighted = jnp.einsum("tk,tkd->td", gate_weights, picked.astype(jnp.float32))
    moe_full = lax.psum(weighted.astype(jnp.bfloat16), ("section", "mp")).astype(jnp.float32)
    finished = (mixed_in + moe_full).astype(jnp.bfloat16).reshape(mb_rows, shards, part_cols)
    return lax.dynamic_index_in_dim(finished, shard_index, 1, keepdims=False)


def remote(src, dst, send, recv, device):
    return pltpu.make_async_remote_copy(
        src_ref=src, dst_ref=dst, send_sem=send, recv_sem=recv, device_id=device, device_id_type=MESH
    )


def contract_last(a, b):
    return lax.dot_general(a, b, (((1,), (1,)), ((), ())), preferred_element_type=jnp.float32)


def layer_kernel(
    groups,
    qkv_hbm,
    kv_hbm,
    res_hbm,
    ow_hbm,
    gain_ref,
    wg_hbm,
    wu_hbm,
    wd_hbm,
    seg_ref,
    count_ref,
    owner_ref,
    slot_ref,
    ids_ref,
    gates_ref,
    out_ref,
    qkv_ref,
    kv_ref,
    res_ref,
    ow_ref,
    wg,
    wu,
    wd,
    hb,
    qb,
    mb,
    os,
    orv,
    mls,
    mlr,
    ps,
    pr,
    ss,
    nb,
    xb,
    yown,
    ys,
    yr,
    rs,
    rb,
    mixed,
    in_sem,
    w_local,
    w_send,
    w_recv,
    q_send,
    q_recv,
    m_send,
    m_recv,
    o_send,
    o_recv,
    l_send,
    l_recv,
    p_send,
    p_recv,
    s_send,
    s_recv,
    n_send,
    x_send,
    x_recv,
    f_send,
    y_send,
    y_recv,
    r_send,
    r_recv,
):
    loads = []
    for i, (hbm, vmem) in enumerate(((qkv_hbm, qkv_ref), (kv_hbm, kv_ref), (ow_hbm, ow_ref), (res_hbm, res_ref))):
        loads.append(pltpu.make_async_copy(hbm, vmem, in_sem.at[i]))
        loads[-1].start()
    s = lax.axis_index("section")
    g = lax.axis_index("dp")
    m = lax.axis_index("mp")
    q = s * 2 + m
    z, y = g // 2, lax.rem(g, 2)
    across = g + 1 - 2 * y
    rows = qkv_ref.shape[0]
    wide = out_ref.shape[1]
    half = groups // 2
    half_line = half // 2
    scale = 1.0 / math.sqrt(HEAD_DIM)
    core_peer = (1 - s, g, m)
    x_peer = (s, g, 1 - m)

    barrier = pltpu.get_barrier_semaphore()

    def greet(k, carry):
        other = lax.rem(s * groups + g + k, 2 * groups)
        pl.semaphore_signal(
            barrier, inc=1, device_id=(other // groups, lax.rem(other, groups), m), device_id_type=MESH
        )
        return carry

    lax.fori_loop(1, 2 * groups, greet, 0)
    pl.semaphore_signal(barrier, inc=1, device_id=x_peer, device_id_type=MESH)
    pl.semaphore_signal(barrier, inc=1, device_id=(1 - s, g, 1 - m), device_id_type=MESH)

    def near(i):
        upper = z // half_line
        edge = z + upper * (3 - 2 * z)
        pick = (i // 2) * i + (1 - i // 2) * lax.rem(i + edge, 2)
        return pick + upper * (3 - 2 * pick)

    def relay(at, piece, sends, recv, sec, mine):
        @pl.when((at <= z) & (z < half - 1))
        def _():
            remote(piece, piece, sends.at[0], recv, (sec, g + 2, mine)).start()

        @pl.when((at >= z) & (z > 0))
        def _():
            remote(piece, piece, sends.at[1], recv, (sec, g - 2, mine)).start()

        remote(piece, piece, sends.at[2], recv, (sec, across, mine)).start()

    def relay_done(at, piece, sends, recv):
        @pl.when((at <= z) & (z < half - 1))
        def _():
            remote(piece, piece, sends.at[0], recv, x_peer).wait_send()

        @pl.when((at >= z) & (z > 0))
        def _():
            remote(piece, piece, sends.at[1], recv, x_peer).wait_send()

        remote(piece, piece, sends.at[2], recv, x_peer).wait_send()

    lane = lax.broadcasted_iota(jnp.int32, (rows, HEAD_DIM), 1)
    row = lax.broadcasted_iota(jnp.int32, (rows, HEAD_DIM), 0)
    ends = count_ref[0, 0]
    block_seg = jnp.zeros((8, HEAD_DIM), jnp.int32)
    for r in range(count_ref.shape[1] - 1):
        block_seg += jnp.where(lane[0:8] >= ends, 1, 0)
        ends = ends + count_ref[0, r + 1]
    meta = jnp.where(row[0:8] == 0, jnp.broadcast_to(seg_ref[...], (8, HEAD_DIM)), block_seg)
    mb[g] = meta
    loads[0].wait()
    for h in range(2):
        qb[g, :, h * HEAD_DIM : (h + 1) * HEAD_DIM] = qkv_ref[:, h * 3 * HEAD_DIM : h * 3 * HEAD_DIM + HEAD_DIM]
    pl.semaphore_wait(barrier, 2 * groups + 1)

    def take_query(src):
        remote(mb.at[src], mb.at[src], m_send.at[src, 0], m_recv.at[src], x_peer).wait_recv()
        remote(qb.at[src], qb.at[src], q_send.at[src, 0], q_recv.at[src], x_peer).wait_recv()

    def forward_query(i):
        at = near(i)
        src = at * 2 + y

        @pl.when(at != z)
        def _():
            take_query(src)

        relay(at, mb.at[src], m_send.at[src], m_recv.at[src], s, m)
        relay(at, qb.at[src], q_send.at[src], q_recv.at[src], s, m)

    forward_query(0)

    hid = wg_hbm.shape[1]
    own_hidden = pl.ds(pl.multiple_of(s * hid, 16), hid)
    peer_hidden = pl.ds(pl.multiple_of((1 - s) * hid, 16), hid)
    weights = ((wg_hbm, wg), (wu_hbm, wu), (wd_hbm, wd))
    for i, (hbm, vmem) in enumerate(weights):
        pltpu.make_async_copy(hbm.at[0], vmem.at[own_hidden], w_local.at[i]).start()
        remote(hbm.at[0], vmem.at[own_hidden], w_send.at[i], w_recv.at[i], core_peer).start()

    key_slot = lax.broadcasted_iota(jnp.int32, (kv_ref.shape[0], PREF), 0) // BLK

    def same_request(meta, line):
        own = jnp.broadcast_to(meta[0:1, :], (rows, HEAD_DIM)).T
        return own == jnp.broadcast_to(meta[line : line + 1, :], (rows, HEAD_DIM))

    def serve(asker):
        back = (s, asker, m)
        seen = same_request(mb[asker].astype(jnp.float32), 1)
        seen = jnp.where(seen, 1.0, 0.0).astype(jnp.bfloat16)[:, :PREF]
        held = jnp.where(owner_ref[pl.ds(asker, 1), :] == g, slot_ref[pl.ds(asker, 1), :], -1)
        held = jnp.broadcast_to(held, key_slot.shape) == key_slot
        count = contract_last(seen, jnp.where(held, 1.0, 0.0).astype(jnp.bfloat16))
        facts = jnp.zeros((rows, HEAD_DIM), jnp.float32)
        for h in range(2):
            query = qb[asker, :, h * HEAD_DIM : (h + 1) * HEAD_DIM]
            key = kv_ref[:, h * 2 * HEAD_DIM : h * 2 * HEAD_DIM + HEAD_DIM]
            value = kv_ref[:, h * 2 * HEAD_DIM + HEAD_DIM : (h + 1) * 2 * HEAD_DIM]
            scores = jnp.where(count > 0.0, contract_last(query, key) * scale, NEG)
            top = jnp.max(scores, axis=1, keepdims=True)
            weight = jnp.exp(scores - top) * count
            total = jnp.sum(weight, axis=1, keepdims=True)
            part = jnp.dot(weight.astype(jnp.bfloat16), value, preferred_element_type=jnp.float32)
            os[asker, :, h * HEAD_DIM : (h + 1) * HEAD_DIM] = part.astype(jnp.bfloat16)
            facts = jnp.where(lane == 2 * h, top, jnp.where(lane == 2 * h + 1, total, facts))
        mls[asker] = facts.T[0:8, :]

        @pl.when(asker != g)
        def _():
            remote(mls.at[asker], mlr.at[g], l_send.at[asker], l_recv.at[g], back).start()
            remote(os.at[asker], orv.at[g], o_send.at[asker], o_recv.at[g], back).start()

        @pl.when(asker == g)
        def _():
            mlr[g] = mls[g]
            orv[g] = os[g]

    loads[1].wait()

    def attend_step(t, carry):
        @pl.when(t < half)
        def _():
            forward_query(t)

        @pl.when(t <= half)
        def _():
            serve(near(t - 1) * 2 + y)

        @pl.when(t >= 2)
        def _():
            src = near(t - 2) * 2 + 1 - y
            take_query(src)
            serve(src)

        return carry

    lax.fori_loop(1, half + 2, attend_step, 0)

    visible = same_request(meta.astype(jnp.float32), 0) & (lane <= row)
    fresh = []
    for h in range(2):
        base = h * 3 * HEAD_DIM
        scores = contract_last(qkv_ref[:, base : base + HEAD_DIM], qkv_ref[:, base + HEAD_DIM : base + 2 * HEAD_DIM])
        scores = jnp.where(visible, scores * scale, NEG)
        top = jnp.max(scores, axis=1, keepdims=True)
        weight = jnp.where(visible, jnp.exp(scores - top), 0.0)
        total = jnp.sum(weight, axis=1, keepdims=True)
        part = jnp.dot(
            weight.astype(jnp.bfloat16),
            qkv_ref[:, base + 2 * HEAD_DIM : base + 3 * HEAD_DIM],
            preferred_element_type=jnp.float32,
        )
        fresh.append((top, total, part))

    def arrive_part(k, carry):
        owner = lax.rem(g + k, groups)
        back = (s, owner, m)
        remote(mls.at[owner], mlr.at[owner], l_send.at[owner], l_recv.at[owner], back).wait_recv()
        remote(os.at[owner], orv.at[owner], o_send.at[owner], o_recv.at[owner], back).wait_recv()
        return carry

    lax.fori_loop(1, groups, arrive_part, 0)

    facts = mlr[...].reshape(groups * 8, HEAD_DIM)
    facts = jnp.concatenate([facts, jnp.zeros((HEAD_DIM - groups * 8, HEAD_DIM), jnp.float32)], axis=0).T
    attended = []
    for h in range(2):
        top, total, part = fresh[h]
        best = top
        for e in range(groups):
            best = jnp.maximum(best, facts[:, e * 8 + 2 * h : e * 8 + 2 * h + 1])
        factor = jnp.exp(top - best)
        mass = factor * total
        mix = factor * part
        for e in range(groups):
            factor = jnp.exp(facts[:, e * 8 + 2 * h : e * 8 + 2 * h + 1] - best)
            mass = mass + factor * facts[:, e * 8 + 2 * h + 1 : e * 8 + 2 * h + 2]
            mix = mix + factor * orv[e, :, h * HEAD_DIM : (h + 1) * HEAD_DIM].astype(jnp.float32)
        attended.append((mix / mass).astype(jnp.bfloat16))
    attended = jnp.concatenate(attended, axis=1)

    loads[2].wait()

    def project(to):
        cols = pl.ds(pl.multiple_of(to * wide, wide), wide)
        return jnp.dot(attended, ow_ref[:, cols], preferred_element_type=jnp.float32)

    for j in (1, 3, 2):
        to = lax.rem(q + j, 4)
        ps[to] = project(to).astype(jnp.bfloat16)
        remote(ps.at[to], pr.at[q], p_send.at[j], p_recv.at[q], (to // 2, g, lax.rem(to, 2))).start()
    mine = pl.ds(pl.multiple_of(q * wide, wide), wide)
    loads[3].wait()
    stream = res_ref[:, mine].astype(jnp.float32) + project(q)
    for j in (1, 3, 2):
        at = lax.rem(q + j, 4)
        remote(ps.at[at], pr.at[at], p_send.at[j], p_recv.at[at], (at // 2, g, lax.rem(at, 2))).wait_recv()
        stream = stream + pr[at].astype(jnp.float32)
    mixed[...] = stream

    square = jnp.sum(stream * stream, axis=1, keepdims=True)
    ss[q] = jnp.broadcast_to(square, (rows, HEAD_DIM)).T[0:8, :]
    for j in (1, 2, 3):
        to = lax.rem(q + j, 4)
        remote(ss.at[q], ss.at[q], s_send.at[j], s_recv.at[q], (to // 2, g, lax.rem(to, 2))).start()
    for j in (1, 2, 3):
        at = lax.rem(q + j, 4)
        remote(ss.at[at], ss.at[at], s_send.at[j], s_recv.at[at], (at // 2, g, lax.rem(at, 2))).wait_recv()
    square = ss[0] + ss[1] + ss[2] + ss[3]
    square = jnp.broadcast_to(square[0:1, :], (rows, HEAD_DIM)).T[:, 0:1]
    inverse = lax.rsqrt(square * (1.0 / (4 * wide)) + 1e-06)
    nb[...] = (stream * inverse * gain_ref[:, mine]).astype(jnp.bfloat16)

    @pl.when(s == y)
    def _():
        xb[z, q] = nb[...]

    @pl.when(s != y)
    def _():
        remote(nb, xb.at[z, q], n_send.at[0], x_recv.at[z, q], core_peer).start()

    @pl.when(s == 1)
    def _():
        remote(nb, xb.at[z, q], n_send.at[1], x_recv.at[z, q], (y, g, 1 - m)).start()

    for i, (hbm, vmem) in enumerate(weights):
        pltpu.make_async_copy(hbm.at[0], vmem.at[own_hidden], w_local.at[i]).wait()
        remote(hbm.at[0], vmem.at[peer_hidden], w_send.at[i], w_recv.at[i], core_peer).wait()

    def slot_of(i):
        at = near(i)
        return at * 2 + s, at

    def take_tokens(at, piece):
        remote(nb, xb.at[at, piece], n_send.at[0], x_recv.at[at, piece], x_peer).wait_recv()

    def forward(i):
        asker, at = slot_of(i)
        for piece in (m, 2, 3):

            @pl.when((asker != g) | (piece != q))
            def _():
                take_tokens(at, piece)

            @pl.when(s == y)
            def _():
                relay(at, xb.at[at, piece], x_send.at[at, piece], x_recv.at[at, piece], s, m)

        remote(xb.at[at, m], xb.at[at, m], f_send.at[at], x_recv.at[at, m], x_peer).start()

    def raise_pair(j):
        tokens = []
        for i in range(2):
            asker, at = slot_of(2 * j + i)
            take_tokens(at, 1 - m)
            tokens.append(jnp.concatenate([xb[at, piece] for piece in range(4)], axis=1))
        tokens = jnp.concatenate(tokens, axis=0)
        gate = contract_last(tokens, wg[...])
        up = contract_last(tokens, wu[...])
        hb[...] = (gate / (1.0 + jnp.exp(-gate)) * up).astype(jnp.bfloat16)

    def lower_pair(j):
        def down(piece):
            cols = pl.ds(pl.multiple_of(piece * wide, wide), wide)
            return jnp.dot(hb[...], wd[:, cols], preferred_element_type=jnp.float32)

        for c in range(2):
            result = down(2 * c + 1 - m).astype(jnp.bfloat16)
            for i in range(2):
                asker, at = slot_of(2 * j + i)
                ys[at, c] = result[i * rows : (i + 1) * rows]
                remote(ys.at[at, c], yr.at[at, c], y_send.at[at, c], y_recv.at[at, c], x_peer).start()
        for c in range(2):
            result = down(2 * c + m)
            for i in range(2):
                asker, at = slot_of(2 * j + i)
                yown[at, c] = result[i * rows : (i + 1) * rows]

    def give_back(i):
        asker, at = slot_of(i)
        for c in range(2):
            remote(ys.at[at, c], yr.at[at, c], y_send.at[at, c], y_recv.at[at, c], x_peer).wait_recv()
            rs[at, c] = (yown[at, c] + yr[at, c].astype(jnp.float32)).astype(jnp.bfloat16)
            is_mine = (asker == g) & (c == s)

            @pl.when(is_mine)
            def _():
                rb[g] = rs[at, c]

            @pl.when(jnp.logical_not(is_mine))
            def _():
                remote(rs.at[at, c], rb.at[g], r_send.at[at, c], r_recv.at[g], (c, asker, m)).start()

    pairs = half // 2
    forward(0)
    forward(1)

    def step(j, carry):
        raise_pair(j)

        @pl.when(j < pairs - 1)
        def _():
            forward(2 * j + 2)

        @pl.when(j > 0)
        def _():
            give_back(2 * j - 2)

        lower_pair(j)

        @pl.when(j < pairs - 1)
        def _():
            forward(2 * j + 3)

        @pl.when(j > 0)
        def _():
            give_back(2 * j - 1)

        return carry

    lax.fori_loop(0, pairs, step, 0)
    give_back(half - 2)
    give_back(half - 1)

    share = jnp.zeros((groups, rows), jnp.float32)
    expert = lax.broadcasted_iota(jnp.int32, (groups, rows), 0)
    for k in range(TOPK):
        named = jnp.broadcast_to(ids_ref[k : k + 1, :], (groups, rows)) == expert
        share += jnp.where(named, jnp.broadcast_to(gates_ref[k : k + 1, :], (groups, rows)), 0.0)
    share = jnp.concatenate([share, jnp.zeros((HEAD_DIM - groups, rows), jnp.float32)], axis=0).T
    stream = mixed[...]
    for e in range(groups):

        @pl.when((e != g) | (s != y))
        def _():
            remote(rs.at[0, 0], rb.at[e], r_send.at[0, 0], r_recv.at[e], core_peer).wait_recv()

        stream = stream + share[:, e : e + 1] * rb[e].astype(jnp.float32)
    out_ref[...] = stream.astype(jnp.bfloat16)

    def drain(k, carry):
        other = lax.rem(g + k, groups)
        remote(mls.at[0], mlr.at[g], l_send.at[other], l_recv.at[g], x_peer).wait_send()
        remote(os.at[0], orv.at[g], o_send.at[other], o_recv.at[g], x_peer).wait_send()
        return carry

    lax.fori_loop(1, groups, drain, 0)

    @pl.when(s != y)
    def _():
        remote(nb, xb.at[z, q], n_send.at[0], x_recv.at[z, q], core_peer).wait_send()

    @pl.when(s == 1)
    def _():
        remote(nb, xb.at[z, q], n_send.at[1], x_recv.at[z, q], x_peer).wait_send()

    for j in (1, 2, 3):
        remote(ps.at[0], pr.at[q], p_send.at[j], p_recv.at[q], core_peer).wait_send()
        remote(ss.at[q], ss.at[q], s_send.at[j], s_recv.at[q], core_peer).wait_send()

    def drain_slot(i, carry):
        asker, at = slot_of(i)
        src = at * 2 + y
        relay_done(at, mb.at[src], m_send.at[src], m_recv.at[src])
        relay_done(at, qb.at[src], q_send.at[src], q_recv.at[src])
        for piece in (m, 2, 3):

            @pl.when(s == y)
            def _():
                relay_done(at, xb.at[at, piece], x_send.at[at, piece], x_recv.at[at, piece])

        remote(xb.at[at, m], xb.at[at, m], f_send.at[at], x_recv.at[at, m], x_peer).wait_send()
        for c in range(2):
            remote(ys.at[at, c], yr.at[at, c], y_send.at[at, c], y_recv.at[at, c], x_peer).wait_send()

            @pl.when((asker != g) | (c != s))
            def _():
                remote(rs.at[at, c], rb.at[g], r_send.at[at, c], r_recv.at[g], core_peer).wait_send()

        return carry

    lax.fori_loop(0, half, drain_slot, 0)


def local_dense(
    qkv,
    kv_cache,
    residual,
    out_weight,
    moe_gain,
    w_gate,
    w_up,
    w_down,
    seg_ids,
    prefix_blocks,
    owners,
    slot_ids,
    expert_ids,
    gate_weights,
):
    groups = lax.axis_size("dp")
    rows = qkv.shape[0]
    model_width = residual.shape[1]
    wide = model_width // 4
    half = groups // 2
    hid = w_gate.shape[2]
    slots = kv_cache.shape[0]
    kv = kv_cache.reshape(slots * BLK, kv_cache.shape[2])
    bf, f32 = jnp.bfloat16, jnp.float32
    dma = pltpu.SemaphoreType.DMA
    vmem = pl.BlockSpec(memory_space=pltpu.VMEM)
    smem = pl.BlockSpec(memory_space=pltpu.SMEM)
    anywhere = pl.BlockSpec(memory_space=pl.ANY)
    return pl.pallas_call(
        partial(layer_kernel, groups),
        out_shape=jax.ShapeDtypeStruct((rows, wide), bf),
        in_specs=[anywhere] * 4 + [vmem] + [anywhere] * 3 + [vmem, smem, vmem, vmem, vmem, vmem],
        out_specs=vmem,
        scratch_shapes=[
            pltpu.VMEM(qkv.shape, bf),
            pltpu.VMEM(kv.shape, bf),
            pltpu.VMEM(residual.shape, bf),
            pltpu.VMEM(out_weight.shape, bf),
            pltpu.VMEM((2 * hid, model_width), bf),
            pltpu.VMEM((2 * hid, model_width), bf),
            pltpu.VMEM((2 * hid, model_width), bf),
            pltpu.VMEM((2 * rows, 2 * hid), bf),
            pltpu.VMEM((groups, rows, 2 * HEAD_DIM), bf),
            pltpu.VMEM((groups, 8, HEAD_DIM), jnp.int32),
            pltpu.VMEM((groups, rows, 2 * HEAD_DIM), bf),
            pltpu.VMEM((groups, rows, 2 * HEAD_DIM), bf),
            pltpu.VMEM((groups, 8, HEAD_DIM), f32),
            pltpu.VMEM((groups, 8, HEAD_DIM), f32),
            pltpu.VMEM((4, rows, wide), bf),
            pltpu.VMEM((4, rows, wide), bf),
            pltpu.VMEM((4, 8, HEAD_DIM), f32),
            pltpu.VMEM((rows, wide), bf),
            pltpu.VMEM((half, 4, rows, wide), bf),
            pltpu.VMEM((half, 2, rows, wide), f32),
            pltpu.VMEM((half, 2, rows, wide), bf),
            pltpu.VMEM((half, 2, rows, wide), bf),
            pltpu.VMEM((half, 2, rows, wide), bf),
            pltpu.VMEM((groups, rows, wide), bf),
            pltpu.VMEM((rows, wide), f32),
            dma((4,)),
            dma((3,)),
            dma((3,)),
            dma((3,)),
            dma((groups, 3)),
            dma((groups,)),
            dma((groups, 3)),
            dma((groups,)),
            dma((groups,)),
            dma((groups,)),
            dma((groups,)),
            dma((groups,)),
            dma((4,)),
            dma((4,)),
            dma((4,)),
            dma((4,)),
            dma((2,)),
            dma((half, 4, 3)),
            dma((half, 4)),
            dma((half,)),
            dma((half, 2)),
            dma((half, 2)),
            dma((half, 2)),
            dma((groups,)),
        ],
        compiler_params=pltpu.CompilerParams(
            collective_id=0, has_side_effects=True, vmem_limit_bytes=60 * 1024 * 1024
        ),
    )(
        qkv,
        kv,
        residual,
        out_weight,
        moe_gain.reshape(1, -1),
        jnp.swapaxes(w_gate, 1, 2),
        jnp.swapaxes(w_up, 1, 2),
        w_down,
        seg_ids[0],
        prefix_blocks[0],
        owners[:, 0, :, 0],
        slot_ids[:, 0, :],
        expert_ids.T,
        gate_weights.T,
    )


def solution(mesh):
    dense = mesh.shape["dp"] <= DENSE_GROUPS
    return jax.shard_map(
        local_dense if dense else local_sparse,
        mesh=mesh,
        in_specs=(
            P("dp", ("section", "mp")),
            P("dp", None, ("section", "mp")),
            P("dp", None),
            P(("section", "mp"), None),
            P(),
            P("dp", None, ("section", "mp")),
            P("dp", None, ("section", "mp")),
            P("dp", ("section", "mp"), None),
            P("dp", None, None),
            P("dp", None, None),
            P(),
            P(),
            P("dp", None),
            P("dp", None),
        ),
        out_specs=P("dp", ("section", "mp")),
        check_vma=False,
    )
```

```python
import math
from functools import partial

import jax
import jax.numpy as jnp
from jax import lax
from jax.experimental import pallas as pl
from jax.experimental.pallas import tpu as pltpu
from jax.sharding import PartitionSpec as P

HEAD_DIM = 128
TOPK = 4
PREF = 64
BLK = 8
MESH = pl.DeviceIdType.MESH
DENSE_GROUPS = 8
NEG = -1e30


def normalize(hidden, gain):
    square = jnp.mean(hidden * hidden, axis=-1, keepdims=True)
    return (hidden * lax.rsqrt(square + 1e-06) * gain).astype(jnp.bfloat16)


def expert_rows(inputs, w_gate, w_up, w_down):
    model_width = inputs.shape[-1]
    flat_rows = inputs.reshape(-1, model_width)
    gate_rows = jnp.dot(flat_rows, w_gate[0], preferred_element_type=jnp.float32)
    up_rows = jnp.dot(flat_rows, w_up[0], preferred_element_type=jnp.float32)
    hidden = (jax.nn.silu(gate_rows) * up_rows).astype(jnp.bfloat16)
    result = jnp.dot(hidden, w_down[0], preferred_element_type=jnp.float32).astype(jnp.bfloat16)
    return result.reshape(inputs.shape[:-1] + (result.shape[-1],))


def slot_table(pair_ids, pair_slots, experts, capacity):
    pair_count = pair_ids.shape[0]
    expert_match = pair_ids[None, None, :] == jnp.arange(experts, dtype=jnp.int32)[:, None, None]
    slot_match = pair_slots[None, None, :] == jnp.arange(capacity, dtype=jnp.int32)[None, :, None]
    pair_match = expert_match & slot_match
    token_of = jnp.arange(pair_count, dtype=jnp.int32) // TOPK
    source = jnp.sum(jnp.where(pair_match, token_of[None, None, :], 0), axis=2)
    filled = jnp.any(pair_match, axis=2)
    return (source, filled)


def dispatch_rows(normed, source, filled):
    gathered = jnp.take(normed, source.reshape(-1), axis=0).reshape(
        source.shape + (normed.shape[-1],)
    )
    return jnp.where(filled[:, :, None], gathered, jnp.zeros_like(gathered))


def local_sparse(
    qkv,
    kv_cache,
    residual,
    out_weight,
    moe_gain,
    w_gate,
    w_up,
    w_down,
    seg_ids,
    prefix_blocks,
    owners,
    slot_ids,
    expert_ids,
    gate_weights,
):
    groups = lax.axis_size("dp")
    shards = lax.axis_size("section") * lax.axis_size("mp")
    group_index = lax.axis_index("dp")
    shard_index = lax.axis_index("section") * lax.axis_size("mp") + lax.axis_index("mp")
    mb_rows = seg_ids.shape[2]
    quarter_rows = mb_rows // shards
    model_width = residual.shape[1]
    part_cols = model_width // shards
    head_cols = out_weight.shape[0]
    heads_local = head_cols // HEAD_DIM
    cache_cols = kv_cache.shape[2]
    quarter_cap = min(quarter_rows, max(2, 2 * quarter_rows * TOPK // groups))
    capacity = shards * quarter_cap
    owner_cap = max(3, 3 * PREF // groups)
    score_scale = 1.0 / math.sqrt(HEAD_DIM)
    own_table = owners[:, 0, :, 0]
    slot_table_m = slot_ids[:, 0, :]
    owned_here = own_table == group_index
    local_order = jnp.cumsum(owned_here.astype(jnp.int32), axis=1) - 1
    wanted = owned_here[:, None, :] & (
        local_order[:, None, :] == jnp.arange(owner_cap, dtype=jnp.int32)[None, :, None]
    )
    slot_pick = jnp.sum(jnp.where(wanted, slot_table_m[:, None, :], 0), axis=2)
    filled = jnp.any(wanted, axis=2)
    chosen = jnp.take(kv_cache, slot_pick.reshape(-1), axis=0).reshape(
        groups, owner_cap, BLK, cache_cols
    )
    chosen = jnp.where(filled[:, :, None, None], chosen, jnp.zeros_like(chosen))
    arrived = lax.all_to_all(chosen, "dp", split_axis=0, concat_axis=0, tiled=True)
    my_owner = lax.dynamic_index_in_dim(own_table, group_index, 0, keepdims=False)
    block_index = jnp.arange(PREF, dtype=jnp.int32)
    earlier = (my_owner[None, :] == my_owner[:, None]) & (
        block_index[None, :] < block_index[:, None]
    )
    my_rank = jnp.sum(earlier.astype(jnp.int32), axis=1)
    where_from = my_owner * owner_cap + my_rank
    prefix = jnp.take(arrived.reshape(groups * owner_cap, BLK, cache_cols), where_from, axis=0)
    prefix = prefix.reshape(PREF * BLK, heads_local, 2, HEAD_DIM)
    tokens = qkv
    tokens = tokens.reshape(mb_rows, heads_local, 3, HEAD_DIM)
    query_rows = tokens[:, :, 0]
    key_rows = jnp.concatenate([prefix[:, :, 0], tokens[:, :, 1]], axis=0)
    value_rows = jnp.concatenate([prefix[:, :, 1], tokens[:, :, 2]], axis=0)
    segments = seg_ids[0, 0]
    block_ends = jnp.cumsum(prefix_blocks[0, 0])
    block_seg = jnp.sum((block_ends[None, :] <= block_index[:, None]).astype(jnp.int32), axis=1)
    prefix_seg = jnp.repeat(block_seg, BLK)
    position = jnp.arange(mb_rows, dtype=jnp.int32)
    same_prefix = prefix_seg[None, :] == segments[:, None]
    same_new = (segments[None, :] == segments[:, None]) & (position[None, :] <= position[:, None])
    visible = jnp.concatenate([same_prefix, same_new], axis=1)
    scores = (
        jnp.einsum("qhd,khd->hqk", query_rows, key_rows, preferred_element_type=jnp.float32)
        * score_scale
    )
    scores = jnp.where(visible[None], scores, -jnp.inf)
    row_max = jnp.max(scores, axis=2, keepdims=True)
    weights = jnp.exp(scores - row_max)
    attention = (weights / jnp.sum(weights, axis=2, keepdims=True)).astype(jnp.bfloat16)
    combined = jnp.einsum("hqk,khd->qhd", attention, value_rows, preferred_element_type=jnp.float32)
    attended_now = combined.astype(jnp.bfloat16).reshape(mb_rows, head_cols)
    stream = residual.astype(jnp.float32)
    projected = jnp.dot(attended_now, out_weight, preferred_element_type=jnp.float32)
    quarter_ids = expert_ids.reshape(shards, quarter_rows * TOPK)
    one_hot = (
        quarter_ids[:, :, None] == jnp.arange(groups, dtype=jnp.int32)[None, None, :]
    ).astype(jnp.int32)
    quarter_rank = jnp.sum((jnp.cumsum(one_hot, axis=1) - one_hot) * one_hot, axis=2)
    flat_ids = expert_ids.reshape(-1)
    flat_slot = (quarter_rank + jnp.arange(shards, dtype=jnp.int32)[:, None] * quarter_cap).reshape(
        -1
    )
    mixed_in = stream + lax.psum(projected, ("section", "mp"))
    normed = normalize(mixed_in, moe_gain)
    source, filled = slot_table(flat_ids, flat_slot, groups, capacity)
    outgoing = dispatch_rows(normed, source, filled)
    incoming = lax.all_to_all(outgoing, "dp", split_axis=0, concat_axis=0, tiled=True)
    produced = expert_rows(incoming, w_gate, w_up, w_down)
    returned = lax.all_to_all(produced, "dp", split_axis=0, concat_axis=0, tiled=True)
    position = flat_ids * capacity + flat_slot
    picked = jnp.take(returned.reshape(groups * capacity, model_width), position, axis=0)
    picked = picked.reshape(mb_rows, TOPK, model_width)
    weighted = jnp.einsum("tk,tkd->td", gate_weights, picked.astype(jnp.float32))
    moe_full = lax.psum(weighted.astype(jnp.bfloat16), ("section", "mp")).astype(jnp.float32)
    finished = (mixed_in + moe_full).astype(jnp.bfloat16).reshape(mb_rows, shards, part_cols)
    return lax.dynamic_index_in_dim(finished, shard_index, 1, keepdims=False)


def remote(src, dst, send, recv, device):
    return pltpu.make_async_remote_copy(
        src_ref=src, dst_ref=dst, send_sem=send, recv_sem=recv, device_id=device, device_id_type=MESH
    )


def contract_last(a, b):
    return lax.dot_general(a, b, (((1,), (1,)), ((), ())), preferred_element_type=jnp.float32)


def layer_kernel(
    groups,
    qkv_hbm,
    kv_hbm,
    res_hbm,
    ow_hbm,
    gain_ref,
    wg_hbm,
    wu_hbm,
    wd_hbm,
    seg_ref,
    count_ref,
    owner_ref,
    slot_ref,
    ids_ref,
    gates_ref,
    out_ref,
    qkv_ref,
    kv_ref,
    res_ref,
    ow_ref,
    wg,
    wu,
    wd,
    qb,
    mb,
    os,
    orv,
    mls,
    mlr,
    ps,
    pr,
    ss,
    nb,
    xb,
    yown,
    ys,
    yr,
    rs,
    rb,
    mixed,
    in_sem,
    w_local,
    w_send,
    w_recv,
    q_send,
    q_recv,
    m_send,
    m_recv,
    o_send,
    o_recv,
    l_send,
    l_recv,
    p_send,
    p_recv,
    s_send,
    s_recv,
    n_send,
    x_send,
    x_recv,
    f_send,
    y_send,
    y_recv,
    r_send,
    r_recv,
):
    loads = []
    for i, (hbm, vmem) in enumerate(((qkv_hbm, qkv_ref), (kv_hbm, kv_ref), (ow_hbm, ow_ref), (res_hbm, res_ref))):
        loads.append(pltpu.make_async_copy(hbm, vmem, in_sem.at[i]))
        loads[-1].start()
    s = lax.axis_index("section")
    g = lax.axis_index("dp")
    m = lax.axis_index("mp")
    q = s * 2 + m
    z, y = g // 2, lax.rem(g, 2)
    across = g + 1 - 2 * y
    rows = qkv_ref.shape[0]
    wide = out_ref.shape[1]
    half = groups // 2
    half_line = half // 2
    scale = 1.0 / math.sqrt(HEAD_DIM)
    core_peer = (1 - s, g, m)
    x_peer = (s, g, 1 - m)

    barrier = pltpu.get_barrier_semaphore()

    def greet(k, carry):
        other = lax.rem(s * groups + g + k, 2 * groups)
        pl.semaphore_signal(
            barrier, inc=1, device_id=(other // groups, lax.rem(other, groups), m), device_id_type=MESH
        )
        return carry

    lax.fori_loop(1, 2 * groups, greet, 0)
    pl.semaphore_signal(barrier, inc=1, device_id=x_peer, device_id_type=MESH)
    pl.semaphore_signal(barrier, inc=1, device_id=(1 - s, g, 1 - m), device_id_type=MESH)

    def near(i):
        upper = z // half_line
        edge = z + upper * (3 - 2 * z)
        pick = (i // 2) * i + (1 - i // 2) * lax.rem(i + edge, 2)
        return pick + upper * (3 - 2 * pick)

    def relay(at, piece, sends, recv, sec, mine):
        @pl.when((at <= z) & (z < half - 1))
        def _():
            remote(piece, piece, sends.at[0], recv, (sec, g + 2, mine)).start()

        @pl.when((at >= z) & (z > 0))
        def _():
            remote(piece, piece, sends.at[1], recv, (sec, g - 2, mine)).start()

        remote(piece, piece, sends.at[2], recv, (sec, across, mine)).start()

    def relay_done(at, piece, sends, recv):
        @pl.when((at <= z) & (z < half - 1))
        def _():
            remote(piece, piece, sends.at[0], recv, x_peer).wait_send()

        @pl.when((at >= z) & (z > 0))
        def _():
            remote(piece, piece, sends.at[1], recv, x_peer).wait_send()

        remote(piece, piece, sends.at[2], recv, x_peer).wait_send()

    lane = lax.broadcasted_iota(jnp.int32, (rows, HEAD_DIM), 1)
    row = lax.broadcasted_iota(jnp.int32, (rows, HEAD_DIM), 0)
    ends = count_ref[0, 0]
    block_seg = jnp.zeros((8, HEAD_DIM), jnp.int32)
    for r in range(count_ref.shape[1] - 1):
        block_seg += jnp.where(lane[0:8] >= ends, 1, 0)
        ends = ends + count_ref[0, r + 1]
    meta = jnp.where(row[0:8] == 0, jnp.broadcast_to(seg_ref[...], (8, HEAD_DIM)), block_seg)
    mb[g] = meta
    loads[0].wait()
    for h in range(2):
        qb[g, :, h * HEAD_DIM : (h + 1) * HEAD_DIM] = qkv_ref[:, h * 3 * HEAD_DIM : h * 3 * HEAD_DIM + HEAD_DIM]
    pl.semaphore_wait(barrier, 2 * groups + 1)

    def take_query(src):
        remote(mb.at[src], mb.at[src], m_send.at[src, 0], m_recv.at[src], x_peer).wait_recv()
        remote(qb.at[src], qb.at[src], q_send.at[src, 0], q_recv.at[src], x_peer).wait_recv()

    def forward_query(i):
        at = near(i)
        src = at * 2 + y

        @pl.when(at != z)
        def _():
            take_query(src)

        relay(at, mb.at[src], m_send.at[src], m_recv.at[src], s, m)
        relay(at, qb.at[src], q_send.at[src], q_recv.at[src], s, m)

    forward_query(0)

    hid = wg_hbm.shape[1]
    own_hidden = pl.ds(pl.multiple_of(s * hid, 16), hid)
    peer_hidden = pl.ds(pl.multiple_of((1 - s) * hid, 16), hid)
    weights = ((wg_hbm, wg), (wu_hbm, wu), (wd_hbm, wd))
    for i, (hbm, vmem) in enumerate(weights):
        pltpu.make_async_copy(hbm.at[0], vmem.at[own_hidden], w_local.at[i]).start()

    key_slot = lax.broadcasted_iota(jnp.int32, (kv_ref.shape[0], PREF), 0) // BLK

    def same_request(meta, line):
        own = jnp.broadcast_to(meta[0:1, :], (rows, HEAD_DIM)).T
        return own == jnp.broadcast_to(meta[line : line + 1, :], (rows, HEAD_DIM))

    def serve(asker):
        back = (s, asker, m)
        seen = same_request(mb[asker].astype(jnp.float32), 1)
        seen = jnp.where(seen, 1.0, 0.0).astype(jnp.bfloat16)[:, :PREF]
        held = jnp.where(owner_ref[pl.ds(asker, 1), :] == g, slot_ref[pl.ds(asker, 1), :], -1)
        held = jnp.broadcast_to(held, key_slot.shape) == key_slot
        count = contract_last(seen, jnp.where(held, 1.0, 0.0).astype(jnp.bfloat16))
        facts = jnp.zeros((rows, HEAD_DIM), jnp.float32)
        for h in range(2):
            query = qb[asker, :, h * HEAD_DIM : (h + 1) * HEAD_DIM]
            key = kv_ref[:, h * 2 * HEAD_DIM : h * 2 * HEAD_DIM + HEAD_DIM]
            value = kv_ref[:, h * 2 * HEAD_DIM + HEAD_DIM : (h + 1) * 2 * HEAD_DIM]
            scores = jnp.where(count > 0.0, contract_last(query, key) * scale, NEG)
            top = jnp.max(scores, axis=1, keepdims=True)
            weight = jnp.exp(scores - top) * count
            total = jnp.sum(weight, axis=1, keepdims=True)
            part = jnp.dot(weight.astype(jnp.bfloat16), value, preferred_element_type=jnp.float32)
            os[asker, :, h * HEAD_DIM : (h + 1) * HEAD_DIM] = part.astype(jnp.bfloat16)
            facts = jnp.where(lane == 2 * h, top, jnp.where(lane == 2 * h + 1, total, facts))
        mls[asker] = facts.T[0:8, :]

        @pl.when(asker != g)
        def _():
            remote(mls.at[asker], mlr.at[g], l_send.at[asker], l_recv.at[g], back).start()
            remote(os.at[asker], orv.at[g], o_send.at[asker], o_recv.at[g], back).start()

        @pl.when(asker == g)
        def _():
            mlr[g] = mls[g]
            orv[g] = os[g]

    loads[1].wait()

    def attend_step(t, carry):
        @pl.when(t < half)
        def _():
            forward_query(t)

        @pl.when(t <= half)
        def _():
            serve(near(t - 1) * 2 + y)

        @pl.when(t >= 2)
        def _():
            src = near(t - 2) * 2 + 1 - y
            take_query(src)
            serve(src)

        for i, (hbm, vmem) in enumerate(weights):

            @pl.when(t == i + 2)
            def _():
                remote(hbm.at[0], vmem.at[own_hidden], w_send.at[i], w_recv.at[i], core_peer).start()

        return carry

    lax.fori_loop(1, half + 2, attend_step, 0)

    visible = same_request(meta.astype(jnp.float32), 0) & (lane <= row)
    fresh = []
    for h in range(2):
        base = h * 3 * HEAD_DIM
        scores = contract_last(qkv_ref[:, base : base + HEAD_DIM], qkv_ref[:, base + HEAD_DIM : base + 2 * HEAD_DIM])
        scores = jnp.where(visible, scores * scale, NEG)
        top = jnp.max(scores, axis=1, keepdims=True)
        weight = jnp.where(visible, jnp.exp(scores - top), 0.0)
        total = jnp.sum(weight, axis=1, keepdims=True)
        part = jnp.dot(
            weight.astype(jnp.bfloat16),
            qkv_ref[:, base + 2 * HEAD_DIM : base + 3 * HEAD_DIM],
            preferred_element_type=jnp.float32,
        )
        fresh.append((top, total, part))

    def arrive_part(k, carry):
        owner = lax.rem(g + k, groups)
        back = (s, owner, m)
        remote(mls.at[owner], mlr.at[owner], l_send.at[owner], l_recv.at[owner], back).wait_recv()
        remote(os.at[owner], orv.at[owner], o_send.at[owner], o_recv.at[owner], back).wait_recv()
        return carry

    lax.fori_loop(1, groups, arrive_part, 0)

    facts = mlr[...].reshape(groups * 8, HEAD_DIM)
    facts = jnp.concatenate([facts, jnp.zeros((HEAD_DIM - groups * 8, HEAD_DIM), jnp.float32)], axis=0).T
    attended = []
    for h in range(2):
        top, total, part = fresh[h]
        best = top
        for e in range(groups):
            best = jnp.maximum(best, facts[:, e * 8 + 2 * h : e * 8 + 2 * h + 1])
        factor = jnp.exp(top - best)
        mass = factor * total
        mix = factor * part
        for e in range(groups):
            factor = jnp.exp(facts[:, e * 8 + 2 * h : e * 8 + 2 * h + 1] - best)
            mass = mass + factor * facts[:, e * 8 + 2 * h + 1 : e * 8 + 2 * h + 2]
            mix = mix + factor * orv[e, :, h * HEAD_DIM : (h + 1) * HEAD_DIM].astype(jnp.float32)
        attended.append((mix / mass).astype(jnp.bfloat16))
    attended = jnp.concatenate(attended, axis=1)

    loads[2].wait()

    def project(to):
        cols = pl.ds(pl.multiple_of(to * wide, wide), wide)
        return jnp.dot(attended, ow_ref[:, cols], preferred_element_type=jnp.float32)

    for j in (1, 3, 2):
        to = lax.rem(q + j, 4)
        ps[to] = project(to).astype(jnp.bfloat16)
        remote(ps.at[to], pr.at[q], p_send.at[j], p_recv.at[q], (to // 2, g, lax.rem(to, 2))).start()
    mine = pl.ds(pl.multiple_of(q * wide, wide), wide)
    loads[3].wait()
    stream = res_ref[:, mine].astype(jnp.float32) + project(q)
    for j in (1, 3, 2):
        at = lax.rem(q + j, 4)
        remote(ps.at[at], pr.at[at], p_send.at[j], p_recv.at[at], (at // 2, g, lax.rem(at, 2))).wait_recv()
        stream = stream + pr[at].astype(jnp.float32)
    mixed[...] = stream

    square = jnp.sum(stream * stream, axis=1, keepdims=True)
    ss[q] = jnp.broadcast_to(square, (rows, HEAD_DIM)).T[0:8, :]
    for j in (1, 2, 3):
        to = lax.rem(q + j, 4)
        remote(ss.at[q], ss.at[q], s_send.at[j], s_recv.at[q], (to // 2, g, lax.rem(to, 2))).start()
    for j in (1, 2, 3):
        at = lax.rem(q + j, 4)
        remote(ss.at[at], ss.at[at], s_send.at[j], s_recv.at[at], (at // 2, g, lax.rem(at, 2))).wait_recv()
    square = ss[0] + ss[1] + ss[2] + ss[3]
    square = jnp.broadcast_to(square[0:1, :], (rows, HEAD_DIM)).T[:, 0:1]
    inverse = lax.rsqrt(square * (1.0 / (4 * wide)) + 1e-06)
    nb[...] = (stream * inverse * gain_ref[:, mine]).astype(jnp.bfloat16)

    @pl.when(s == y)
    def _():
        xb[z, q] = nb[...]

    @pl.when(s != y)
    def _():
        remote(nb, xb.at[z, q], n_send.at[0], x_recv.at[z, q], core_peer).start()

    @pl.when(s == 1)
    def _():
        remote(nb, xb.at[z, q], n_send.at[1], x_recv.at[z, q], (y, g, 1 - m)).start()

    for i, (hbm, vmem) in enumerate(weights):
        pltpu.make_async_copy(hbm.at[0], vmem.at[own_hidden], w_local.at[i]).wait()
        remote(hbm.at[0], vmem.at[peer_hidden], w_send.at[i], w_recv.at[i], core_peer).wait()

    def slot_of(i):
        at = near(i)
        return at * 2 + s, at

    def take_tokens(at, piece):
        remote(nb, xb.at[at, piece], n_send.at[0], x_recv.at[at, piece], x_peer).wait_recv()

    def forward(i):
        asker, at = slot_of(i)
        for piece in (m, 2, 3):

            @pl.when((asker != g) | (piece != q))
            def _():
                take_tokens(at, piece)

            if piece is m:
                remote(xb.at[at, m], xb.at[at, m], f_send.at[at], x_recv.at[at, m], x_peer).start()

            @pl.when(s == y)
            def _():
                relay(at, xb.at[at, piece], x_send.at[at, piece], x_recv.at[at, piece], s, m)


    def compute(i):
        asker, at = slot_of(i)
        take_tokens(at, 1 - m)
        tokens = jnp.concatenate([xb[at, piece] for piece in range(4)], axis=1)
        gate = contract_last(tokens, wg[...])
        up = contract_last(tokens, wu[...])
        hidden = (gate / (1.0 + jnp.exp(-gate)) * up).astype(jnp.bfloat16)

        def down(piece):
            cols = pl.ds(pl.multiple_of(piece * wide, wide), wide)
            return jnp.dot(hidden, wd[:, cols], preferred_element_type=jnp.float32)

        for c in range(2):
            ys[at, c] = down(2 * c + 1 - m).astype(jnp.bfloat16)
            remote(ys.at[at, c], yr.at[at, c], y_send.at[at, c], y_recv.at[at, c], x_peer).start()
        for c in range(2):
            yown[at, c] = down(2 * c + m)

    def give_back(i):
        asker, at = slot_of(i)
        for c in range(2):
            remote(ys.at[at, c], yr.at[at, c], y_send.at[at, c], y_recv.at[at, c], x_peer).wait_recv()
            rs[at, c] = (yown[at, c] + yr[at, c].astype(jnp.float32)).astype(jnp.bfloat16)
            is_mine = (asker == g) & (c == s)

            @pl.when(is_mine)
            def _():
                rb[g] = rs[at, c]

            @pl.when(jnp.logical_not(is_mine))
            def _():
                remote(rs.at[at, c], rb.at[g], r_send.at[at, c], r_recv.at[g], (c, asker, m)).start()

    def step(t, carry):
        @pl.when(t < half)
        def _():
            forward(t)

        @pl.when((t >= 1) & (t <= half))
        def _():
            compute(t - 1)

        @pl.when(t >= 2)
        def _():
            give_back(t - 2)

        return carry

    lax.fori_loop(0, half + 2, step, 0)

    share = jnp.zeros((groups, rows), jnp.float32)
    expert = lax.broadcasted_iota(jnp.int32, (groups, rows), 0)
    for k in range(TOPK):
        named = jnp.broadcast_to(ids_ref[k : k + 1, :], (groups, rows)) == expert
        share += jnp.where(named, jnp.broadcast_to(gates_ref[k : k + 1, :], (groups, rows)), 0.0)
    share = jnp.concatenate([share, jnp.zeros((HEAD_DIM - groups, rows), jnp.float32)], axis=0).T
    stream = mixed[...]
    for e in range(groups):

        @pl.when((e != g) | (s != y))
        def _():
            remote(rs.at[0, 0], rb.at[e], r_send.at[0, 0], r_recv.at[e], core_peer).wait_recv()

        stream = stream + share[:, e : e + 1] * rb[e].astype(jnp.float32)
    out_ref[...] = stream.astype(jnp.bfloat16)

    def drain(k, carry):
        other = lax.rem(g + k, groups)
        remote(mls.at[0], mlr.at[g], l_send.at[other], l_recv.at[g], x_peer).wait_send()
        remote(os.at[0], orv.at[g], o_send.at[other], o_recv.at[g], x_peer).wait_send()
        return carry

    lax.fori_loop(1, groups, drain, 0)

    @pl.when(s != y)
    def _():
        remote(nb, xb.at[z, q], n_send.at[0], x_recv.at[z, q], core_peer).wait_send()

    @pl.when(s == 1)
    def _():
        remote(nb, xb.at[z, q], n_send.at[1], x_recv.at[z, q], x_peer).wait_send()

    for j in (1, 2, 3):
        remote(ps.at[0], pr.at[q], p_send.at[j], p_recv.at[q], core_peer).wait_send()
        remote(ss.at[q], ss.at[q], s_send.at[j], s_recv.at[q], core_peer).wait_send()

    def drain_slot(i, carry):
        asker, at = slot_of(i)
        src = at * 2 + y
        relay_done(at, mb.at[src], m_send.at[src], m_recv.at[src])
        relay_done(at, qb.at[src], q_send.at[src], q_recv.at[src])
        for piece in (m, 2, 3):

            @pl.when(s == y)
            def _():
                relay_done(at, xb.at[at, piece], x_send.at[at, piece], x_recv.at[at, piece])

        remote(xb.at[at, m], xb.at[at, m], f_send.at[at], x_recv.at[at, m], x_peer).wait_send()
        for c in range(2):
            remote(ys.at[at, c], yr.at[at, c], y_send.at[at, c], y_recv.at[at, c], x_peer).wait_send()

            @pl.when((asker != g) | (c != s))
            def _():
                remote(rs.at[at, c], rb.at[g], r_send.at[at, c], r_recv.at[g], core_peer).wait_send()

        return carry

    lax.fori_loop(0, half, drain_slot, 0)


def local_dense(
    qkv,
    kv_cache,
    residual,
    out_weight,
    moe_gain,
    w_gate,
    w_up,
    w_down,
    seg_ids,
    prefix_blocks,
    owners,
    slot_ids,
    expert_ids,
    gate_weights,
):
    groups = lax.axis_size("dp")
    rows = qkv.shape[0]
    model_width = residual.shape[1]
    wide = model_width // 4
    half = groups // 2
    hid = w_gate.shape[2]
    slots = kv_cache.shape[0]
    kv = kv_cache.reshape(slots * BLK, kv_cache.shape[2])
    bf, f32 = jnp.bfloat16, jnp.float32
    dma = pltpu.SemaphoreType.DMA
    vmem = pl.BlockSpec(memory_space=pltpu.VMEM)
    smem = pl.BlockSpec(memory_space=pltpu.SMEM)
    anywhere = pl.BlockSpec(memory_space=pl.ANY)
    return pl.pallas_call(
        partial(layer_kernel, groups),
        out_shape=jax.ShapeDtypeStruct((rows, wide), bf),
        in_specs=[anywhere] * 4 + [vmem] + [anywhere] * 3 + [vmem, smem, vmem, vmem, vmem, vmem],
        out_specs=vmem,
        scratch_shapes=[
            pltpu.VMEM(qkv.shape, bf),
            pltpu.VMEM(kv.shape, bf),
            pltpu.VMEM(residual.shape, bf),
            pltpu.VMEM(out_weight.shape, bf),
            pltpu.VMEM((2 * hid, model_width), bf),
            pltpu.VMEM((2 * hid, model_width), bf),
            pltpu.VMEM((2 * hid, model_width), bf),
            pltpu.VMEM((groups, rows, 2 * HEAD_DIM), bf),
            pltpu.VMEM((groups, 8, HEAD_DIM), jnp.int32),
            pltpu.VMEM((groups, rows, 2 * HEAD_DIM), bf),
            pltpu.VMEM((groups, rows, 2 * HEAD_DIM), bf),
            pltpu.VMEM((groups, 8, HEAD_DIM), f32),
            pltpu.VMEM((groups, 8, HEAD_DIM), f32),
            pltpu.VMEM((4, rows, wide), bf),
            pltpu.VMEM((4, rows, wide), bf),
            pltpu.VMEM((4, 8, HEAD_DIM), f32),
            pltpu.VMEM((rows, wide), bf),
            pltpu.VMEM((half, 4, rows, wide), bf),
            pltpu.VMEM((half, 2, rows, wide), f32),
            pltpu.VMEM((half, 2, rows, wide), bf),
            pltpu.VMEM((half, 2, rows, wide), bf),
            pltpu.VMEM((half, 2, rows, wide), bf),
            pltpu.VMEM((groups, rows, wide), bf),
            pltpu.VMEM((rows, wide), f32),
            dma((4,)),
            dma((3,)),
            dma((3,)),
            dma((3,)),
            dma((groups, 3)),
            dma((groups,)),
            dma((groups, 3)),
            dma((groups,)),
            dma((groups,)),
            dma((groups,)),
            dma((groups,)),
            dma((groups,)),
            dma((4,)),
            dma((4,)),
            dma((4,)),
            dma((4,)),
            dma((2,)),
            dma((half, 4, 3)),
            dma((half, 4)),
            dma((half,)),
            dma((half, 2)),
            dma((half, 2)),
            dma((half, 2)),
            dma((groups,)),
        ],
        compiler_params=pltpu.CompilerParams(
            collective_id=0, has_side_effects=True, vmem_limit_bytes=60 * 1024 * 1024
        ),
    )(
        qkv,
        kv,
        residual,
        out_weight,
        moe_gain.reshape(1, -1),
        jnp.swapaxes(w_gate, 1, 2),
        jnp.swapaxes(w_up, 1, 2),
        w_down,
        seg_ids[0],
        prefix_blocks[0],
        owners[:, 0, :, 0],
        slot_ids[:, 0, :],
        expert_ids.T,
        gate_weights.T,
    )


def solution(mesh):
    dense = mesh.shape["dp"] <= DENSE_GROUPS
    return jax.shard_map(
        local_dense if dense else local_sparse,
        mesh=mesh,
        in_specs=(
            P("dp", ("section", "mp")),
            P("dp", None, ("section", "mp")),
            P("dp", None),
            P(("section", "mp"), None),
            P(),
            P("dp", None, ("section", "mp")),
            P("dp", None, ("section", "mp")),
            P("dp", ("section", "mp"), None),
            P("dp", None, None),
            P("dp", None, None),
            P(),
            P(),
            P("dp", None),
            P("dp", None),
        ),
        out_specs=P("dp", ("section", "mp")),
        check_vma=False,
    )
```

```python
import math
from functools import partial

import jax
import jax.numpy as jnp
from jax import lax
from jax.experimental import pallas as pl
from jax.experimental.pallas import tpu as pltpu
from jax.sharding import PartitionSpec as P

HEAD_DIM = 128
TOPK = 4
PREF = 64
BLK = 8
MESH = pl.DeviceIdType.MESH
DENSE_GROUPS = 8
NEG = -1e30


def normalize(hidden, gain):
    square = jnp.mean(hidden * hidden, axis=-1, keepdims=True)
    return (hidden * lax.rsqrt(square + 1e-06) * gain).astype(jnp.bfloat16)


def expert_rows(inputs, w_gate, w_up, w_down):
    model_width = inputs.shape[-1]
    flat_rows = inputs.reshape(-1, model_width)
    gate_rows = jnp.dot(flat_rows, w_gate[0], preferred_element_type=jnp.float32)
    up_rows = jnp.dot(flat_rows, w_up[0], preferred_element_type=jnp.float32)
    hidden = (jax.nn.silu(gate_rows) * up_rows).astype(jnp.bfloat16)
    result = jnp.dot(hidden, w_down[0], preferred_element_type=jnp.float32).astype(jnp.bfloat16)
    return result.reshape(inputs.shape[:-1] + (result.shape[-1],))


def slot_table(pair_ids, pair_slots, experts, capacity):
    pair_count = pair_ids.shape[0]
    expert_match = pair_ids[None, None, :] == jnp.arange(experts, dtype=jnp.int32)[:, None, None]
    slot_match = pair_slots[None, None, :] == jnp.arange(capacity, dtype=jnp.int32)[None, :, None]
    pair_match = expert_match & slot_match
    token_of = jnp.arange(pair_count, dtype=jnp.int32) // TOPK
    source = jnp.sum(jnp.where(pair_match, token_of[None, None, :], 0), axis=2)
    filled = jnp.any(pair_match, axis=2)
    return (source, filled)


def dispatch_rows(normed, source, filled):
    gathered = jnp.take(normed, source.reshape(-1), axis=0).reshape(
        source.shape + (normed.shape[-1],)
    )
    return jnp.where(filled[:, :, None], gathered, jnp.zeros_like(gathered))


def local_sparse(
    qkv,
    kv_cache,
    residual,
    out_weight,
    moe_gain,
    w_gate,
    w_up,
    w_down,
    seg_ids,
    prefix_blocks,
    owners,
    slot_ids,
    expert_ids,
    gate_weights,
):
    groups = lax.axis_size("dp")
    shards = lax.axis_size("section") * lax.axis_size("mp")
    group_index = lax.axis_index("dp")
    shard_index = lax.axis_index("section") * lax.axis_size("mp") + lax.axis_index("mp")
    mb_rows = seg_ids.shape[2]
    quarter_rows = mb_rows // shards
    model_width = residual.shape[1]
    part_cols = model_width // shards
    head_cols = out_weight.shape[0]
    heads_local = head_cols // HEAD_DIM
    cache_cols = kv_cache.shape[2]
    quarter_cap = min(quarter_rows, max(2, 2 * quarter_rows * TOPK // groups))
    capacity = shards * quarter_cap
    owner_cap = max(3, 3 * PREF // groups)
    score_scale = 1.0 / math.sqrt(HEAD_DIM)
    own_table = owners[:, 0, :, 0]
    slot_table_m = slot_ids[:, 0, :]
    owned_here = own_table == group_index
    local_order = jnp.cumsum(owned_here.astype(jnp.int32), axis=1) - 1
    wanted = owned_here[:, None, :] & (
        local_order[:, None, :] == jnp.arange(owner_cap, dtype=jnp.int32)[None, :, None]
    )
    slot_pick = jnp.sum(jnp.where(wanted, slot_table_m[:, None, :], 0), axis=2)
    filled = jnp.any(wanted, axis=2)
    chosen = jnp.take(kv_cache, slot_pick.reshape(-1), axis=0).reshape(
        groups, owner_cap, BLK, cache_cols
    )
    chosen = jnp.where(filled[:, :, None, None], chosen, jnp.zeros_like(chosen))
    arrived = lax.all_to_all(chosen, "dp", split_axis=0, concat_axis=0, tiled=True)
    my_owner = lax.dynamic_index_in_dim(own_table, group_index, 0, keepdims=False)
    block_index = jnp.arange(PREF, dtype=jnp.int32)
    earlier = (my_owner[None, :] == my_owner[:, None]) & (
        block_index[None, :] < block_index[:, None]
    )
    my_rank = jnp.sum(earlier.astype(jnp.int32), axis=1)
    where_from = my_owner * owner_cap + my_rank
    prefix = jnp.take(arrived.reshape(groups * owner_cap, BLK, cache_cols), where_from, axis=0)
    prefix = prefix.reshape(PREF * BLK, heads_local, 2, HEAD_DIM)
    tokens = qkv
    tokens = tokens.reshape(mb_rows, heads_local, 3, HEAD_DIM)
    query_rows = tokens[:, :, 0]
    key_rows = jnp.concatenate([prefix[:, :, 0], tokens[:, :, 1]], axis=0)
    value_rows = jnp.concatenate([prefix[:, :, 1], tokens[:, :, 2]], axis=0)
    segments = seg_ids[0, 0]
    block_ends = jnp.cumsum(prefix_blocks[0, 0])
    block_seg = jnp.sum((block_ends[None, :] <= block_index[:, None]).astype(jnp.int32), axis=1)
    prefix_seg = jnp.repeat(block_seg, BLK)
    position = jnp.arange(mb_rows, dtype=jnp.int32)
    same_prefix = prefix_seg[None, :] == segments[:, None]
    same_new = (segments[None, :] == segments[:, None]) & (position[None, :] <= position[:, None])
    visible = jnp.concatenate([same_prefix, same_new], axis=1)
    scores = (
        jnp.einsum("qhd,khd->hqk", query_rows, key_rows, preferred_element_type=jnp.float32)
        * score_scale
    )
    scores = jnp.where(visible[None], scores, -jnp.inf)
    row_max = jnp.max(scores, axis=2, keepdims=True)
    weights = jnp.exp(scores - row_max)
    attention = (weights / jnp.sum(weights, axis=2, keepdims=True)).astype(jnp.bfloat16)
    combined = jnp.einsum("hqk,khd->qhd", attention, value_rows, preferred_element_type=jnp.float32)
    attended_now = combined.astype(jnp.bfloat16).reshape(mb_rows, head_cols)
    stream = residual.astype(jnp.float32)
    projected = jnp.dot(attended_now, out_weight, preferred_element_type=jnp.float32)
    quarter_ids = expert_ids.reshape(shards, quarter_rows * TOPK)
    one_hot = (
        quarter_ids[:, :, None] == jnp.arange(groups, dtype=jnp.int32)[None, None, :]
    ).astype(jnp.int32)
    quarter_rank = jnp.sum((jnp.cumsum(one_hot, axis=1) - one_hot) * one_hot, axis=2)
    flat_ids = expert_ids.reshape(-1)
    flat_slot = (quarter_rank + jnp.arange(shards, dtype=jnp.int32)[:, None] * quarter_cap).reshape(
        -1
    )
    mixed_in = stream + lax.psum(projected, ("section", "mp"))
    normed = normalize(mixed_in, moe_gain)
    source, filled = slot_table(flat_ids, flat_slot, groups, capacity)
    outgoing = dispatch_rows(normed, source, filled)
    incoming = lax.all_to_all(outgoing, "dp", split_axis=0, concat_axis=0, tiled=True)
    produced = expert_rows(incoming, w_gate, w_up, w_down)
    returned = lax.all_to_all(produced, "dp", split_axis=0, concat_axis=0, tiled=True)
    position = flat_ids * capacity + flat_slot
    picked = jnp.take(returned.reshape(groups * capacity, model_width), position, axis=0)
    picked = picked.reshape(mb_rows, TOPK, model_width)
    weighted = jnp.einsum("tk,tkd->td", gate_weights, picked.astype(jnp.float32))
    moe_full = lax.psum(weighted.astype(jnp.bfloat16), ("section", "mp")).astype(jnp.float32)
    finished = (mixed_in + moe_full).astype(jnp.bfloat16).reshape(mb_rows, shards, part_cols)
    return lax.dynamic_index_in_dim(finished, shard_index, 1, keepdims=False)


def remote(src, dst, send, recv, device):
    return pltpu.make_async_remote_copy(
        src_ref=src, dst_ref=dst, send_sem=send, recv_sem=recv, device_id=device, device_id_type=MESH
    )


def contract_last(a, b):
    return lax.dot_general(a, b, (((1,), (1,)), ((), ())), preferred_element_type=jnp.float32)


def layer_kernel(
    groups,
    qkv_hbm,
    kv_hbm,
    res_hbm,
    ow_hbm,
    gain_ref,
    wg_hbm,
    wu_hbm,
    wd_hbm,
    seg_ref,
    count_ref,
    owner_ref,
    slot_ref,
    ids_ref,
    gates_ref,
    out_ref,
    qkv_ref,
    kv_ref,
    res_ref,
    ow_ref,
    wg,
    wu,
    wd,
    qb,
    mb,
    os,
    orv,
    mls,
    mlr,
    ps,
    pr,
    ss,
    nb,
    xb,
    yown,
    ys,
    yr,
    vs,
    vr,
    rs,
    rb,
    mixed,
    in_sem,
    w_local,
    w_send,
    w_recv,
    q_send,
    q_recv,
    m_send,
    m_recv,
    o_send,
    o_recv,
    l_send,
    l_recv,
    p_send,
    p_recv,
    s_send,
    s_recv,
    n_send,
    x_send,
    x_recv,
    f_send,
    y_send,
    y_recv,
    v_send,
    v_recv,
    r_send,
    r_recv,
):
    loads = []
    for i, (hbm, vmem) in enumerate(((qkv_hbm, qkv_ref), (kv_hbm, kv_ref), (ow_hbm, ow_ref), (res_hbm, res_ref))):
        loads.append(pltpu.make_async_copy(hbm, vmem, in_sem.at[i]))
        loads[-1].start()
    s = lax.axis_index("section")
    g = lax.axis_index("dp")
    m = lax.axis_index("mp")
    q = s * 2 + m
    z, y = g // 2, lax.rem(g, 2)
    across = g + 1 - 2 * y
    rows = qkv_ref.shape[0]
    wide = out_ref.shape[1]
    half = groups // 2
    half_line = half // 2
    scale = 1.0 / math.sqrt(HEAD_DIM)
    core_peer = (1 - s, g, m)
    x_peer = (s, g, 1 - m)

    barrier = pltpu.get_barrier_semaphore()

    def greet(k, carry):
        other = lax.rem(s * groups + g + k, 2 * groups)
        pl.semaphore_signal(
            barrier, inc=1, device_id=(other // groups, lax.rem(other, groups), m), device_id_type=MESH
        )
        return carry

    lax.fori_loop(1, 2 * groups, greet, 0)
    pl.semaphore_signal(barrier, inc=1, device_id=x_peer, device_id_type=MESH)
    pl.semaphore_signal(barrier, inc=1, device_id=(1 - s, g, 1 - m), device_id_type=MESH)

    def near(i):
        upper = z // half_line
        edge = z + upper * (3 - 2 * z)
        pick = (i // 2) * i + (1 - i // 2) * lax.rem(i + edge, 2)
        return pick + upper * (3 - 2 * pick)

    def relay(at, piece, sends, recv, sec, mine):
        @pl.when((at <= z) & (z < half - 1))
        def _():
            remote(piece, piece, sends.at[0], recv, (sec, g + 2, mine)).start()

        @pl.when((at >= z) & (z > 0))
        def _():
            remote(piece, piece, sends.at[1], recv, (sec, g - 2, mine)).start()

        remote(piece, piece, sends.at[2], recv, (sec, across, mine)).start()

    def relay_done(at, piece, sends, recv):
        @pl.when((at <= z) & (z < half - 1))
        def _():
            remote(piece, piece, sends.at[0], recv, x_peer).wait_send()

        @pl.when((at >= z) & (z > 0))
        def _():
            remote(piece, piece, sends.at[1], recv, x_peer).wait_send()

        remote(piece, piece, sends.at[2], recv, x_peer).wait_send()

    lane = lax.broadcasted_iota(jnp.int32, (rows, HEAD_DIM), 1)
    row = lax.broadcasted_iota(jnp.int32, (rows, HEAD_DIM), 0)
    ends = count_ref[0, 0]
    block_seg = jnp.zeros((8, HEAD_DIM), jnp.int32)
    for r in range(count_ref.shape[1] - 1):
        block_seg += jnp.where(lane[0:8] >= ends, 1, 0)
        ends = ends + count_ref[0, r + 1]
    meta = jnp.where(row[0:8] == 0, jnp.broadcast_to(seg_ref[...], (8, HEAD_DIM)), block_seg)
    meta = meta.astype(jnp.float32)
    share = jnp.zeros((groups, rows), jnp.float32)
    expert = lax.broadcasted_iota(jnp.int32, (groups, rows), 0)
    for k in range(TOPK):
        named = jnp.broadcast_to(ids_ref[k : k + 1, :], (groups, rows)) == expert
        share += jnp.where(named, jnp.broadcast_to(gates_ref[k : k + 1, :], (groups, rows)), 0.0)
    mb[g] = jnp.concatenate([meta, share], axis=0)
    loads[0].wait()
    for h in range(2):
        qb[g, :, h * HEAD_DIM : (h + 1) * HEAD_DIM] = qkv_ref[:, h * 3 * HEAD_DIM : h * 3 * HEAD_DIM + HEAD_DIM]
    pl.semaphore_wait(barrier, 2 * groups + 1)

    def take_query(src):
        remote(mb.at[src], mb.at[src], m_send.at[src, 0], m_recv.at[src], x_peer).wait_recv()
        remote(qb.at[src], qb.at[src], q_send.at[src, 0], q_recv.at[src], x_peer).wait_recv()

    def forward_query(i):
        at = near(i)
        src = at * 2 + y

        @pl.when(at != z)
        def _():
            take_query(src)

        relay(at, mb.at[src], m_send.at[src], m_recv.at[src], s, m)
        relay(at, qb.at[src], q_send.at[src], q_recv.at[src], s, m)

    forward_query(0)

    hid = wg_hbm.shape[1]
    own_hidden = pl.ds(pl.multiple_of(s * hid, 16), hid)
    peer_hidden = pl.ds(pl.multiple_of((1 - s) * hid, 16), hid)
    weights = ((wg_hbm, wg), (wu_hbm, wu), (wd_hbm, wd))
    for i, (hbm, vmem) in enumerate(weights):
        pltpu.make_async_copy(hbm.at[0], vmem.at[own_hidden], w_local.at[i]).start()

    key_slot = lax.broadcasted_iota(jnp.int32, (kv_ref.shape[0], PREF), 0) // BLK

    def same_request(meta, line):
        own = jnp.broadcast_to(meta[0:1, :], (rows, HEAD_DIM)).T
        return own == jnp.broadcast_to(meta[line : line + 1, :], (rows, HEAD_DIM))

    def serve(asker):
        back = (s, asker, m)
        seen = same_request(mb[asker], 1)
        seen = jnp.where(seen, 1.0, 0.0).astype(jnp.bfloat16)[:, :PREF]
        held = jnp.where(owner_ref[pl.ds(asker, 1), :] == g, slot_ref[pl.ds(asker, 1), :], -1)
        held = jnp.broadcast_to(held, key_slot.shape) == key_slot
        count = contract_last(seen, jnp.where(held, 1.0, 0.0).astype(jnp.bfloat16))
        facts = jnp.zeros((rows, HEAD_DIM), jnp.float32)
        for h in range(2):
            query = qb[asker, :, h * HEAD_DIM : (h + 1) * HEAD_DIM]
            key = kv_ref[:, h * 2 * HEAD_DIM : h * 2 * HEAD_DIM + HEAD_DIM]
            value = kv_ref[:, h * 2 * HEAD_DIM + HEAD_DIM : (h + 1) * 2 * HEAD_DIM]
            scores = jnp.where(count > 0.0, contract_last(query, key) * scale, NEG)
            top = jnp.max(scores, axis=1, keepdims=True)
            weight = jnp.exp(scores - top) * count
            total = jnp.sum(weight, axis=1, keepdims=True)
            part = jnp.dot(weight.astype(jnp.bfloat16), value, preferred_element_type=jnp.float32)
            os[asker, :, h * HEAD_DIM : (h + 1) * HEAD_DIM] = part.astype(jnp.bfloat16)
            facts = jnp.where(lane == 2 * h, top, jnp.where(lane == 2 * h + 1, total, facts))
        mls[asker] = facts.T[0:8, :]

        @pl.when(asker != g)
        def _():
            remote(mls.at[asker], mlr.at[g], l_send.at[asker], l_recv.at[g], back).start()
            remote(os.at[asker], orv.at[g], o_send.at[asker], o_recv.at[g], back).start()

        @pl.when(asker == g)
        def _():
            mlr[g] = mls[g]
            orv[g] = os[g]

    loads[1].wait()

    def attend_step(t, carry):
        @pl.when(t < half)
        def _():
            forward_query(t)

        @pl.when(t <= half)
        def _():
            serve(near(t - 1) * 2 + y)

        @pl.when(t >= 2)
        def _():
            src = near(t - 2) * 2 + 1 - y
            take_query(src)
            serve(src)

        for i, (hbm, vmem) in enumerate(weights):

            @pl.when(t == i + 2)
            def _():
                remote(hbm.at[0], vmem.at[own_hidden], w_send.at[i], w_recv.at[i], core_peer).start()

        return carry

    lax.fori_loop(1, half + 2, attend_step, 0)

    visible = same_request(meta, 0) & (lane <= row)
    fresh = []
    for h in range(2):
        base = h * 3 * HEAD_DIM
        scores = contract_last(qkv_ref[:, base : base + HEAD_DIM], qkv_ref[:, base + HEAD_DIM : base + 2 * HEAD_DIM])
        scores = jnp.where(visible, scores * scale, NEG)
        top = jnp.max(scores, axis=1, keepdims=True)
        weight = jnp.where(visible, jnp.exp(scores - top), 0.0)
        total = jnp.sum(weight, axis=1, keepdims=True)
        part = jnp.dot(
            weight.astype(jnp.bfloat16),
            qkv_ref[:, base + 2 * HEAD_DIM : base + 3 * HEAD_DIM],
            preferred_element_type=jnp.float32,
        )
        fresh.append((top, total, part))

    def arrive_part(k, carry):
        owner = lax.rem(g + k, groups)
        back = (s, owner, m)
        remote(mls.at[owner], mlr.at[owner], l_send.at[owner], l_recv.at[owner], back).wait_recv()
        remote(os.at[owner], orv.at[owner], o_send.at[owner], o_recv.at[owner], back).wait_recv()
        return carry

    lax.fori_loop(1, groups, arrive_part, 0)

    facts = mlr[...].reshape(groups * 8, HEAD_DIM)
    facts = jnp.concatenate([facts, jnp.zeros((HEAD_DIM - groups * 8, HEAD_DIM), jnp.float32)], axis=0).T
    attended = []
    for h in range(2):
        top, total, part = fresh[h]
        best = top
        for e in range(groups):
            best = jnp.maximum(best, facts[:, e * 8 + 2 * h : e * 8 + 2 * h + 1])
        factor = jnp.exp(top - best)
        mass = factor * total
        mix = factor * part
        for e in range(groups):
            factor = jnp.exp(facts[:, e * 8 + 2 * h : e * 8 + 2 * h + 1] - best)
            mass = mass + factor * facts[:, e * 8 + 2 * h + 1 : e * 8 + 2 * h + 2]
            mix = mix + factor * orv[e, :, h * HEAD_DIM : (h + 1) * HEAD_DIM].astype(jnp.float32)
        attended.append((mix / mass).astype(jnp.bfloat16))
    attended = jnp.concatenate(attended, axis=1)

    loads[2].wait()

    def project(to):
        cols = pl.ds(pl.multiple_of(to * wide, wide), wide)
        return jnp.dot(attended, ow_ref[:, cols], preferred_element_type=jnp.float32)

    for j in (1, 3, 2):
        to = lax.rem(q + j, 4)
        ps[to] = project(to).astype(jnp.bfloat16)
        remote(ps.at[to], pr.at[q], p_send.at[j], p_recv.at[q], (to // 2, g, lax.rem(to, 2))).start()
    mine = pl.ds(pl.multiple_of(q * wide, wide), wide)
    loads[3].wait()
    stream = res_ref[:, mine].astype(jnp.float32) + project(q)
    for j in (1, 3, 2):
        at = lax.rem(q + j, 4)
        remote(ps.at[at], pr.at[at], p_send.at[j], p_recv.at[at], (at // 2, g, lax.rem(at, 2))).wait_recv()
        stream = stream + pr[at].astype(jnp.float32)
    mixed[...] = stream

    square = jnp.sum(stream * stream, axis=1, keepdims=True)
    ss[q] = jnp.broadcast_to(square, (rows, HEAD_DIM)).T[0:8, :]
    for j in (1, 2, 3):
        to = lax.rem(q + j, 4)
        remote(ss.at[q], ss.at[q], s_send.at[j], s_recv.at[q], (to // 2, g, lax.rem(to, 2))).start()
    for j in (1, 2, 3):
        at = lax.rem(q + j, 4)
        remote(ss.at[at], ss.at[at], s_send.at[j], s_recv.at[at], (at // 2, g, lax.rem(at, 2))).wait_recv()
    square = ss[0] + ss[1] + ss[2] + ss[3]
    square = jnp.broadcast_to(square[0:1, :], (rows, HEAD_DIM)).T[:, 0:1]
    inverse = lax.rsqrt(square * (1.0 / (4 * wide)) + 1e-06)
    nb[...] = (stream * inverse * gain_ref[:, mine]).astype(jnp.bfloat16)

    @pl.when(s == y)
    def _():
        xb[z, q] = nb[...]

    @pl.when(s != y)
    def _():
        remote(nb, xb.at[z, q], n_send.at[0], x_recv.at[z, q], core_peer).start()

    @pl.when(s == 1)
    def _():
        remote(nb, xb.at[z, q], n_send.at[1], x_recv.at[z, q], (y, g, 1 - m)).start()

    for i, (hbm, vmem) in enumerate(weights):
        pltpu.make_async_copy(hbm.at[0], vmem.at[own_hidden], w_local.at[i]).wait()
        remote(hbm.at[0], vmem.at[peer_hidden], w_send.at[i], w_recv.at[i], core_peer).wait()

    def slot_of(i):
        at = near(i)
        return at * 2 + s, at

    def take_tokens(at, piece):
        remote(nb, xb.at[at, piece], n_send.at[0], x_recv.at[at, piece], x_peer).wait_recv()

    def forward(i):
        asker, at = slot_of(i)
        for piece in (m, 2, 3):

            @pl.when((asker != g) | (piece != q))
            def _():
                take_tokens(at, piece)

            if piece is m:
                remote(xb.at[at, m], xb.at[at, m], f_send.at[at], x_recv.at[at, m], x_peer).start()

            @pl.when(s == y)
            def _():
                relay(at, xb.at[at, piece], x_send.at[at, piece], x_recv.at[at, piece], s, m)


    def pass_on(at, k):
        return remote(vs.at[at, k], vr.at[at, k], v_send.at[at, k], v_recv.at[at, k], (s, across, m))

    def trade(at, c):
        return remote(ys.at[at, c], yr.at[at, c], y_send.at[at, c], y_recv.at[at, c], x_peer)

    def compute(i):
        asker, at = slot_of(i)
        take_tokens(at, 1 - m)
        tokens = jnp.concatenate([xb[at, piece] for piece in range(4)], axis=1)
        gate = contract_last(tokens, wg[...])
        up = contract_last(tokens, wu[...])
        hidden = (gate / (1.0 + jnp.exp(-gate)) * up).astype(jnp.bfloat16)

        weight = jnp.broadcast_to(mb[asker, pl.ds(8 + g, 1), :], (rows, HEAD_DIM)).T[:, 0:1]

        def down(piece):
            cols = pl.ds(pl.multiple_of(piece * wide, wide), wide)
            return jnp.dot(hidden, wd[:, cols], preferred_element_type=jnp.float32) * weight

        for k in (1, 2):
            yown[at, k] = down(k + 1)

        @pl.when(s != y)
        def _():
            for k in (1, 2):
                vs[at, k] = yown[at, k].astype(jnp.bfloat16)
                pass_on(at, k).start()

        ys[at, 0] = down(1 - m).astype(jnp.bfloat16)
        trade(at, 0).start()
        yown[at, 0] = down(m)

    def gather_half(i):
        asker, at = slot_of(i)
        trade(at, 0).wait_recv()
        yown[at, 0] = yown[at, 0] + yr[at, 0].astype(jnp.float32)

        @pl.when(s != y)
        def _():
            vs[at, 0] = yown[at, 0].astype(jnp.bfloat16)
            pass_on(at, 0).start()

        @pl.when(s == y)
        def _():
            for k in (1, 2):
                pass_on(at, k).wait_recv()
                yown[at, k] = yown[at, k] + vr[at, k].astype(jnp.float32)
            ys[at, 1] = yown[at, 2 - m].astype(jnp.bfloat16)
            trade(at, 1).start()

    def give_back(i):
        asker, at = slot_of(i)
        for c in range(2):
            if c == 0:
                pass_on(at, 0).wait_recv()
                total = yown[at, 0] + vr[at, 0].astype(jnp.float32)
            else:
                trade(at, 1).wait_recv()
                total = yown[at, 1 + m] + yr[at, 1].astype(jnp.float32)
            rs[at, c] = total.astype(jnp.bfloat16)
            is_mine = (asker == g) & (c == s)

            @pl.when(is_mine)
            def _():
                rb[z] = rs[at, c]

            @pl.when(jnp.logical_not(is_mine))
            def _():
                remote(rs.at[at, c], rb.at[z], r_send.at[at, c], r_recv.at[z], (c, asker, m)).start()

    def step(t, carry):
        @pl.when(t < half)
        def _():
            forward(t)

        @pl.when((t >= 1) & (t <= half))
        def _():
            compute(t - 1)

        @pl.when((t >= 2) & (t <= half + 1))
        def _():
            gather_half(t - 2)

        @pl.when((t >= 3) & (s == y))
        def _():
            give_back(t - 3)

        return carry

    lax.fori_loop(0, half + 3, step, 0)

    stream = mixed[...]
    for e in range(half):

        @pl.when((e != z) | (s != y))
        def _():
            remote(rs.at[0, 0], rb.at[e], r_send.at[0, 0], r_recv.at[e], core_peer).wait_recv()

        stream = stream + rb[e].astype(jnp.float32)
    out_ref[...] = stream.astype(jnp.bfloat16)

    def drain(k, carry):
        other = lax.rem(g + k, groups)
        remote(mls.at[0], mlr.at[g], l_send.at[other], l_recv.at[g], x_peer).wait_send()
        remote(os.at[0], orv.at[g], o_send.at[other], o_recv.at[g], x_peer).wait_send()
        return carry

    lax.fori_loop(1, groups, drain, 0)

    @pl.when(s != y)
    def _():
        remote(nb, xb.at[z, q], n_send.at[0], x_recv.at[z, q], core_peer).wait_send()

    @pl.when(s == 1)
    def _():
        remote(nb, xb.at[z, q], n_send.at[1], x_recv.at[z, q], x_peer).wait_send()

    for j in (1, 2, 3):
        remote(ps.at[0], pr.at[q], p_send.at[j], p_recv.at[q], core_peer).wait_send()
        remote(ss.at[q], ss.at[q], s_send.at[j], s_recv.at[q], core_peer).wait_send()

    def drain_slot(i, carry):
        asker, at = slot_of(i)
        src = at * 2 + y
        relay_done(at, mb.at[src], m_send.at[src], m_recv.at[src])
        relay_done(at, qb.at[src], q_send.at[src], q_recv.at[src])
        for piece in (m, 2, 3):

            @pl.when(s == y)
            def _():
                relay_done(at, xb.at[at, piece], x_send.at[at, piece], x_recv.at[at, piece])

        remote(xb.at[at, m], xb.at[at, m], f_send.at[at], x_recv.at[at, m], x_peer).wait_send()
        trade(at, 0).wait_send()

        @pl.when(s != y)
        def _():
            for k in range(3):
                pass_on(at, k).wait_send()

        @pl.when(s == y)
        def _():
            trade(at, 1).wait_send()
            for c in range(2):

                @pl.when((asker != g) | (c != s))
                def _():
                    remote(rs.at[at, c], rb.at[z], r_send.at[at, c], r_recv.at[z], core_peer).wait_send()

        return carry

    lax.fori_loop(0, half, drain_slot, 0)


def local_dense(
    qkv,
    kv_cache,
    residual,
    out_weight,
    moe_gain,
    w_gate,
    w_up,
    w_down,
    seg_ids,
    prefix_blocks,
    owners,
    slot_ids,
    expert_ids,
    gate_weights,
):
    groups = lax.axis_size("dp")
    rows = qkv.shape[0]
    model_width = residual.shape[1]
    wide = model_width // 4
    half = groups // 2
    hid = w_gate.shape[2]
    slots = kv_cache.shape[0]
    kv = kv_cache.reshape(slots * BLK, kv_cache.shape[2])
    bf, f32 = jnp.bfloat16, jnp.float32
    dma = pltpu.SemaphoreType.DMA
    vmem = pl.BlockSpec(memory_space=pltpu.VMEM)
    smem = pl.BlockSpec(memory_space=pltpu.SMEM)
    anywhere = pl.BlockSpec(memory_space=pl.ANY)
    return pl.pallas_call(
        partial(layer_kernel, groups),
        out_shape=jax.ShapeDtypeStruct((rows, wide), bf),
        in_specs=[anywhere] * 4 + [vmem] + [anywhere] * 3 + [vmem, smem, vmem, vmem, vmem, vmem],
        out_specs=vmem,
        scratch_shapes=[
            pltpu.VMEM(qkv.shape, bf),
            pltpu.VMEM(kv.shape, bf),
            pltpu.VMEM(residual.shape, bf),
            pltpu.VMEM(out_weight.shape, bf),
            pltpu.VMEM((2 * hid, model_width), bf),
            pltpu.VMEM((2 * hid, model_width), bf),
            pltpu.VMEM((2 * hid, model_width), bf),
            pltpu.VMEM((groups, rows, 2 * HEAD_DIM), bf),
            pltpu.VMEM((groups, 8 + groups, HEAD_DIM), f32),
            pltpu.VMEM((groups, rows, 2 * HEAD_DIM), bf),
            pltpu.VMEM((groups, rows, 2 * HEAD_DIM), bf),
            pltpu.VMEM((groups, 8, HEAD_DIM), f32),
            pltpu.VMEM((groups, 8, HEAD_DIM), f32),
            pltpu.VMEM((4, rows, wide), bf),
            pltpu.VMEM((4, rows, wide), bf),
            pltpu.VMEM((4, 8, HEAD_DIM), f32),
            pltpu.VMEM((rows, wide), bf),
            pltpu.VMEM((half, 4, rows, wide), bf),
            pltpu.VMEM((half, 3, rows, wide), f32),
            pltpu.VMEM((half, 2, rows, wide), bf),
            pltpu.VMEM((half, 2, rows, wide), bf),
            pltpu.VMEM((half, 3, rows, wide), bf),
            pltpu.VMEM((half, 3, rows, wide), bf),
            pltpu.VMEM((half, 2, rows, wide), bf),
            pltpu.VMEM((half, rows, wide), bf),
            pltpu.VMEM((rows, wide), f32),
            dma((4,)),
            dma((3,)),
            dma((3,)),
            dma((3,)),
            dma((groups, 3)),
            dma((groups,)),
            dma((groups, 3)),
            dma((groups,)),
            dma((groups,)),
            dma((groups,)),
            dma((groups,)),
            dma((groups,)),
            dma((4,)),
            dma((4,)),
            dma((4,)),
            dma((4,)),
            dma((2,)),
            dma((half, 4, 3)),
            dma((half, 4)),
            dma((half,)),
            dma((half, 2)),
            dma((half, 2)),
            dma((half, 3)),
            dma((half, 3)),
            dma((half, 2)),
            dma((half,)),
        ],
        compiler_params=pltpu.CompilerParams(
            collective_id=0, has_side_effects=True, vmem_limit_bytes=60 * 1024 * 1024
        ),
    )(
        qkv,
        kv,
        residual,
        out_weight,
        moe_gain.reshape(1, -1),
        jnp.swapaxes(w_gate, 1, 2),
        jnp.swapaxes(w_up, 1, 2),
        w_down,
        seg_ids[0],
        prefix_blocks[0],
        owners[:, 0, :, 0],
        slot_ids[:, 0, :],
        expert_ids.T,
        gate_weights.T,
    )


def solution(mesh):
    dense = mesh.shape["dp"] <= DENSE_GROUPS
    return jax.shard_map(
        local_dense if dense else local_sparse,
        mesh=mesh,
        in_specs=(
            P("dp", ("section", "mp")),
            P("dp", None, ("section", "mp")),
            P("dp", None),
            P(("section", "mp"), None),
            P(),
            P("dp", None, ("section", "mp")),
            P("dp", None, ("section", "mp")),
            P("dp", ("section", "mp"), None),
            P("dp", None, None),
            P("dp", None, None),
            P(),
            P(),
            P("dp", None),
            P("dp", None),
        ),
        out_specs=P("dp", ("section", "mp")),
        check_vma=False,
    )
```

```python
import math
from functools import partial

import jax
import jax.numpy as jnp
from jax import lax
from jax.experimental import pallas as pl
from jax.experimental.pallas import tpu as pltpu
from jax.sharding import PartitionSpec as P

HEAD_DIM = 128
TOPK = 4
PREF = 64
BLK = 8
MESH = pl.DeviceIdType.MESH
DENSE_GROUPS = 8
NEG = -1e30


def normalize(hidden, gain):
    square = jnp.mean(hidden * hidden, axis=-1, keepdims=True)
    return (hidden * lax.rsqrt(square + 1e-06) * gain).astype(jnp.bfloat16)


def expert_rows(inputs, w_gate, w_up, w_down):
    model_width = inputs.shape[-1]
    flat_rows = inputs.reshape(-1, model_width)
    gate_rows = jnp.dot(flat_rows, w_gate[0], preferred_element_type=jnp.float32)
    up_rows = jnp.dot(flat_rows, w_up[0], preferred_element_type=jnp.float32)
    hidden = (jax.nn.silu(gate_rows) * up_rows).astype(jnp.bfloat16)
    result = jnp.dot(hidden, w_down[0], preferred_element_type=jnp.float32).astype(jnp.bfloat16)
    return result.reshape(inputs.shape[:-1] + (result.shape[-1],))


def slot_table(pair_ids, pair_slots, experts, capacity):
    pair_count = pair_ids.shape[0]
    expert_match = pair_ids[None, None, :] == jnp.arange(experts, dtype=jnp.int32)[:, None, None]
    slot_match = pair_slots[None, None, :] == jnp.arange(capacity, dtype=jnp.int32)[None, :, None]
    pair_match = expert_match & slot_match
    token_of = jnp.arange(pair_count, dtype=jnp.int32) // TOPK
    source = jnp.sum(jnp.where(pair_match, token_of[None, None, :], 0), axis=2)
    filled = jnp.any(pair_match, axis=2)
    return (source, filled)


def dispatch_rows(normed, source, filled):
    gathered = jnp.take(normed, source.reshape(-1), axis=0).reshape(
        source.shape + (normed.shape[-1],)
    )
    return jnp.where(filled[:, :, None], gathered, jnp.zeros_like(gathered))


def local_sparse(
    qkv,
    kv_cache,
    residual,
    out_weight,
    moe_gain,
    w_gate,
    w_up,
    w_down,
    seg_ids,
    prefix_blocks,
    owners,
    slot_ids,
    expert_ids,
    gate_weights,
):
    groups = lax.axis_size("dp")
    shards = lax.axis_size("section") * lax.axis_size("mp")
    group_index = lax.axis_index("dp")
    shard_index = lax.axis_index("section") * lax.axis_size("mp") + lax.axis_index("mp")
    mb_rows = seg_ids.shape[2]
    quarter_rows = mb_rows // shards
    model_width = residual.shape[1]
    part_cols = model_width // shards
    head_cols = out_weight.shape[0]
    heads_local = head_cols // HEAD_DIM
    cache_cols = kv_cache.shape[2]
    quarter_cap = min(quarter_rows, max(2, 2 * quarter_rows * TOPK // groups))
    capacity = shards * quarter_cap
    owner_cap = max(3, 3 * PREF // groups)
    score_scale = 1.0 / math.sqrt(HEAD_DIM)
    own_table = owners[:, 0, :, 0]
    slot_table_m = slot_ids[:, 0, :]
    owned_here = own_table == group_index
    local_order = jnp.cumsum(owned_here.astype(jnp.int32), axis=1) - 1
    wanted = owned_here[:, None, :] & (
        local_order[:, None, :] == jnp.arange(owner_cap, dtype=jnp.int32)[None, :, None]
    )
    slot_pick = jnp.sum(jnp.where(wanted, slot_table_m[:, None, :], 0), axis=2)
    filled = jnp.any(wanted, axis=2)
    chosen = jnp.take(kv_cache, slot_pick.reshape(-1), axis=0).reshape(
        groups, owner_cap, BLK, cache_cols
    )
    chosen = jnp.where(filled[:, :, None, None], chosen, jnp.zeros_like(chosen))
    arrived = lax.all_to_all(chosen, "dp", split_axis=0, concat_axis=0, tiled=True)
    my_owner = lax.dynamic_index_in_dim(own_table, group_index, 0, keepdims=False)
    block_index = jnp.arange(PREF, dtype=jnp.int32)
    earlier = (my_owner[None, :] == my_owner[:, None]) & (
        block_index[None, :] < block_index[:, None]
    )
    my_rank = jnp.sum(earlier.astype(jnp.int32), axis=1)
    where_from = my_owner * owner_cap + my_rank
    prefix = jnp.take(arrived.reshape(groups * owner_cap, BLK, cache_cols), where_from, axis=0)
    prefix = prefix.reshape(PREF * BLK, heads_local, 2, HEAD_DIM)
    tokens = qkv
    tokens = tokens.reshape(mb_rows, heads_local, 3, HEAD_DIM)
    query_rows = tokens[:, :, 0]
    key_rows = jnp.concatenate([prefix[:, :, 0], tokens[:, :, 1]], axis=0)
    value_rows = jnp.concatenate([prefix[:, :, 1], tokens[:, :, 2]], axis=0)
    segments = seg_ids[0, 0]
    block_ends = jnp.cumsum(prefix_blocks[0, 0])
    block_seg = jnp.sum((block_ends[None, :] <= block_index[:, None]).astype(jnp.int32), axis=1)
    prefix_seg = jnp.repeat(block_seg, BLK)
    position = jnp.arange(mb_rows, dtype=jnp.int32)
    same_prefix = prefix_seg[None, :] == segments[:, None]
    same_new = (segments[None, :] == segments[:, None]) & (position[None, :] <= position[:, None])
    visible = jnp.concatenate([same_prefix, same_new], axis=1)
    scores = (
        jnp.einsum("qhd,khd->hqk", query_rows, key_rows, preferred_element_type=jnp.float32)
        * score_scale
    )
    scores = jnp.where(visible[None], scores, -jnp.inf)
    row_max = jnp.max(scores, axis=2, keepdims=True)
    weights = jnp.exp(scores - row_max)
    attention = (weights / jnp.sum(weights, axis=2, keepdims=True)).astype(jnp.bfloat16)
    combined = jnp.einsum("hqk,khd->qhd", attention, value_rows, preferred_element_type=jnp.float32)
    attended_now = combined.astype(jnp.bfloat16).reshape(mb_rows, head_cols)
    stream = residual.astype(jnp.float32)
    projected = jnp.dot(attended_now, out_weight, preferred_element_type=jnp.float32)
    quarter_ids = expert_ids.reshape(shards, quarter_rows * TOPK)
    one_hot = (
        quarter_ids[:, :, None] == jnp.arange(groups, dtype=jnp.int32)[None, None, :]
    ).astype(jnp.int32)
    quarter_rank = jnp.sum((jnp.cumsum(one_hot, axis=1) - one_hot) * one_hot, axis=2)
    flat_ids = expert_ids.reshape(-1)
    flat_slot = (quarter_rank + jnp.arange(shards, dtype=jnp.int32)[:, None] * quarter_cap).reshape(
        -1
    )
    mixed_in = stream + lax.psum(projected, ("section", "mp"))
    normed = normalize(mixed_in, moe_gain)
    source, filled = slot_table(flat_ids, flat_slot, groups, capacity)
    outgoing = dispatch_rows(normed, source, filled)
    incoming = lax.all_to_all(outgoing, "dp", split_axis=0, concat_axis=0, tiled=True)
    produced = expert_rows(incoming, w_gate, w_up, w_down)
    returned = lax.all_to_all(produced, "dp", split_axis=0, concat_axis=0, tiled=True)
    position = flat_ids * capacity + flat_slot
    picked = jnp.take(returned.reshape(groups * capacity, model_width), position, axis=0)
    picked = picked.reshape(mb_rows, TOPK, model_width)
    weighted = jnp.einsum("tk,tkd->td", gate_weights, picked.astype(jnp.float32))
    moe_full = lax.psum(weighted.astype(jnp.bfloat16), ("section", "mp")).astype(jnp.float32)
    finished = (mixed_in + moe_full).astype(jnp.bfloat16).reshape(mb_rows, shards, part_cols)
    return lax.dynamic_index_in_dim(finished, shard_index, 1, keepdims=False)


def remote(src, dst, send, recv, device):
    return pltpu.make_async_remote_copy(
        src_ref=src, dst_ref=dst, send_sem=send, recv_sem=recv, device_id=device, device_id_type=MESH
    )


def contract_last(a, b):
    return lax.dot_general(a, b, (((1,), (1,)), ((), ())), preferred_element_type=jnp.float32)


def layer_kernel(
    groups,
    qkv_hbm,
    kv_hbm,
    res_hbm,
    ow_hbm,
    gain_ref,
    wg_hbm,
    wu_hbm,
    wd_hbm,
    seg_ref,
    count_ref,
    owner_ref,
    slot_ref,
    ids_ref,
    gates_ref,
    out_ref,
    qkv_ref,
    kv_ref,
    res_ref,
    ow_ref,
    wg,
    wu,
    wd,
    qb,
    mb,
    os,
    orv,
    mls,
    mlr,
    ps,
    pr,
    ss,
    nb,
    xb,
    yown,
    ys,
    yr,
    rs,
    rb,
    mixed,
    in_sem,
    w_local,
    w_send,
    w_recv,
    q_send,
    q_recv,
    m_send,
    m_recv,
    o_send,
    o_recv,
    l_send,
    l_recv,
    p_send,
    p_recv,
    s_send,
    s_recv,
    n_send,
    x_send,
    x_recv,
    f_send,
    y_send,
    y_recv,
    r_send,
    r_recv,
):
    loads = []
    for i, (hbm, vmem) in enumerate(((qkv_hbm, qkv_ref), (kv_hbm, kv_ref), (ow_hbm, ow_ref), (res_hbm, res_ref))):
        loads.append(pltpu.make_async_copy(hbm, vmem, in_sem.at[i]))
        loads[-1].start()
    s = lax.axis_index("section")
    g = lax.axis_index("dp")
    m = lax.axis_index("mp")
    q = s * 2 + m
    z, y = g // 2, lax.rem(g, 2)
    across = g + 1 - 2 * y
    rows = qkv_ref.shape[0]
    wide = out_ref.shape[1]
    half = groups // 2
    half_line = half // 2
    scale = 1.0 / math.sqrt(HEAD_DIM)
    core_peer = (1 - s, g, m)
    x_peer = (s, g, 1 - m)

    barrier = pltpu.get_barrier_semaphore()

    def greet(k, carry):
        other = lax.rem(s * groups + g + k, 2 * groups)
        pl.semaphore_signal(
            barrier, inc=1, device_id=(other // groups, lax.rem(other, groups), m), device_id_type=MESH
        )
        return carry

    lax.fori_loop(1, 2 * groups, greet, 0)
    pl.semaphore_signal(barrier, inc=1, device_id=x_peer, device_id_type=MESH)
    pl.semaphore_signal(barrier, inc=1, device_id=(1 - s, g, 1 - m), device_id_type=MESH)

    def near(i):
        upper = z // half_line
        edge = z + upper * (3 - 2 * z)
        pick = (i // 2) * i + (1 - i // 2) * lax.rem(i + edge, 2)
        return pick + upper * (3 - 2 * pick)

    def relay(at, piece, sends, recv, sec, mine):
        @pl.when((at <= z) & (z < half - 1))
        def _():
            remote(piece, piece, sends.at[0], recv, (sec, g + 2, mine)).start()

        @pl.when((at >= z) & (z > 0))
        def _():
            remote(piece, piece, sends.at[1], recv, (sec, g - 2, mine)).start()

        remote(piece, piece, sends.at[2], recv, (sec, across, mine)).start()

    def relay_done(at, piece, sends, recv):
        @pl.when((at <= z) & (z < half - 1))
        def _():
            remote(piece, piece, sends.at[0], recv, x_peer).wait_send()

        @pl.when((at >= z) & (z > 0))
        def _():
            remote(piece, piece, sends.at[1], recv, x_peer).wait_send()

        remote(piece, piece, sends.at[2], recv, x_peer).wait_send()

    lane = lax.broadcasted_iota(jnp.int32, (rows, HEAD_DIM), 1)
    row = lax.broadcasted_iota(jnp.int32, (rows, HEAD_DIM), 0)
    ends = count_ref[0, 0]
    block_seg = jnp.zeros((8, HEAD_DIM), jnp.int32)
    for r in range(count_ref.shape[1] - 1):
        block_seg += jnp.where(lane[0:8] >= ends, 1, 0)
        ends = ends + count_ref[0, r + 1]
    meta = jnp.where(row[0:8] == 0, jnp.broadcast_to(seg_ref[...], (8, HEAD_DIM)), block_seg)
    mb[g] = meta
    loads[0].wait()
    for h in range(2):
        qb[g, :, h * HEAD_DIM : (h + 1) * HEAD_DIM] = qkv_ref[:, h * 3 * HEAD_DIM : h * 3 * HEAD_DIM + HEAD_DIM]
    pl.semaphore_wait(barrier, 2 * groups + 1)

    def take_query(src):
        remote(mb.at[src], mb.at[src], m_send.at[src, 0], m_recv.at[src], x_peer).wait_recv()
        remote(qb.at[src], qb.at[src], q_send.at[src, 0], q_recv.at[src], x_peer).wait_recv()

    def forward_query(i):
        at = near(i)
        src = at * 2 + y

        @pl.when(at != z)
        def _():
            take_query(src)

        relay(at, mb.at[src], m_send.at[src], m_recv.at[src], s, m)
        relay(at, qb.at[src], q_send.at[src], q_recv.at[src], s, m)

    forward_query(0)

    hid = wg_hbm.shape[1]
    own_hidden = pl.ds(pl.multiple_of(s * hid, 16), hid)
    peer_hidden = pl.ds(pl.multiple_of((1 - s) * hid, 16), hid)
    weights = ((wg_hbm, wg), (wu_hbm, wu), (wd_hbm, wd))
    for i, (hbm, vmem) in enumerate(weights):
        pltpu.make_async_copy(hbm.at[0], vmem.at[own_hidden], w_local.at[i]).start()

    key_slot = lax.broadcasted_iota(jnp.int32, (kv_ref.shape[0], PREF), 0) // BLK

    def same_request(meta, line):
        own = jnp.broadcast_to(meta[0:1, :], (rows, HEAD_DIM)).T
        return own == jnp.broadcast_to(meta[line : line + 1, :], (rows, HEAD_DIM))

    def serve(asker):
        back = (s, asker, m)
        seen = same_request(mb[asker].astype(jnp.float32), 1)
        seen = jnp.where(seen, 1.0, 0.0).astype(jnp.bfloat16)[:, :PREF]
        held = jnp.where(owner_ref[pl.ds(asker, 1), :] == g, slot_ref[pl.ds(asker, 1), :], -1)
        held = jnp.broadcast_to(held, key_slot.shape) == key_slot
        count = contract_last(seen, jnp.where(held, 1.0, 0.0).astype(jnp.bfloat16))
        bias = jnp.where(count > 0.0, jnp.log(jnp.maximum(count, 1.0)), NEG)
        facts = jnp.zeros((rows, HEAD_DIM), jnp.float32)
        for h in range(2):
            query = qb[asker, :, h * HEAD_DIM : (h + 1) * HEAD_DIM]
            key = kv_ref[:, h * 2 * HEAD_DIM : h * 2 * HEAD_DIM + HEAD_DIM]
            value = kv_ref[:, h * 2 * HEAD_DIM + HEAD_DIM : (h + 1) * 2 * HEAD_DIM]
            scores = contract_last(query, key) * scale + bias
            top = jnp.max(scores, axis=1, keepdims=True)
            weight = jnp.exp(scores - top)
            total = jnp.sum(weight, axis=1, keepdims=True)
            part = jnp.dot(weight.astype(jnp.bfloat16), value, preferred_element_type=jnp.float32)
            os[asker, :, h * HEAD_DIM : (h + 1) * HEAD_DIM] = part.astype(jnp.bfloat16)
            facts = jnp.where(lane == 2 * h, top, jnp.where(lane == 2 * h + 1, total, facts))
        mls[asker] = facts.T[0:8, :]

        @pl.when(asker != g)
        def _():
            remote(mls.at[asker], mlr.at[g], l_send.at[asker], l_recv.at[g], back).start()
            remote(os.at[asker], orv.at[g], o_send.at[asker], o_recv.at[g], back).start()

        @pl.when(asker == g)
        def _():
            mlr[g] = mls[g]
            orv[g] = os[g]

    loads[1].wait()

    def attend_step(t, carry):
        @pl.when(t < half)
        def _():
            forward_query(t)

        @pl.when(t <= half)
        def _():
            serve(near(t - 1) * 2 + y)

        @pl.when(t >= 2)
        def _():
            src = near(t - 2) * 2 + 1 - y
            take_query(src)
            serve(src)

        for i, (hbm, vmem) in enumerate(weights):

            @pl.when(t == i + 2)
            def _():
                remote(hbm.at[0], vmem.at[own_hidden], w_send.at[i], w_recv.at[i], core_peer).start()

        return carry

    lax.fori_loop(1, half + 2, attend_step, 0)

    visible = same_request(meta.astype(jnp.float32), 0) & (lane <= row)
    fresh = []
    for h in range(2):
        base = h * 3 * HEAD_DIM
        scores = contract_last(qkv_ref[:, base : base + HEAD_DIM], qkv_ref[:, base + HEAD_DIM : base + 2 * HEAD_DIM])
        scores = jnp.where(visible, scores * scale, NEG)
        top = jnp.max(scores, axis=1, keepdims=True)
        weight = jnp.where(visible, jnp.exp(scores - top), 0.0)
        total = jnp.sum(weight, axis=1, keepdims=True)
        part = jnp.dot(
            weight.astype(jnp.bfloat16),
            qkv_ref[:, base + 2 * HEAD_DIM : base + 3 * HEAD_DIM],
            preferred_element_type=jnp.float32,
        )
        fresh.append((top, total, part))

    def arrive_part(k, carry):
        owner = lax.rem(g + k, groups)
        back = (s, owner, m)
        remote(mls.at[owner], mlr.at[owner], l_send.at[owner], l_recv.at[owner], back).wait_recv()
        remote(os.at[owner], orv.at[owner], o_send.at[owner], o_recv.at[owner], back).wait_recv()
        return carry

    lax.fori_loop(1, groups, arrive_part, 0)

    facts = mlr[...].reshape(groups * 8, HEAD_DIM)
    facts = jnp.concatenate([facts, jnp.zeros((HEAD_DIM - groups * 8, HEAD_DIM), jnp.float32)], axis=0).T
    attended = []
    for h in range(2):
        top, total, part = fresh[h]
        best = top
        for e in range(groups):
            best = jnp.maximum(best, facts[:, e * 8 + 2 * h : e * 8 + 2 * h + 1])
        factor = jnp.exp(top - best)
        factors = jnp.exp(facts - best)
        mass = factor * total
        mix = factor * part
        for e in range(groups):
            factor = factors[:, e * 8 + 2 * h : e * 8 + 2 * h + 1]
            mass = mass + factor * facts[:, e * 8 + 2 * h + 1 : e * 8 + 2 * h + 2]
            mix = mix + factor * orv[e, :, h * HEAD_DIM : (h + 1) * HEAD_DIM].astype(jnp.float32)
        attended.append((mix / mass).astype(jnp.bfloat16))
    attended = jnp.concatenate(attended, axis=1)

    loads[2].wait()

    def project(to):
        cols = pl.ds(pl.multiple_of(to * wide, wide), wide)
        return jnp.dot(attended, ow_ref[:, cols], preferred_element_type=jnp.float32)

    for j in (1, 3, 2):
        to = lax.rem(q + j, 4)
        ps[to] = project(to).astype(jnp.bfloat16)
        remote(ps.at[to], pr.at[q], p_send.at[j], p_recv.at[q], (to // 2, g, lax.rem(to, 2))).start()
    mine = pl.ds(pl.multiple_of(q * wide, wide), wide)
    loads[3].wait()
    stream = res_ref[:, mine].astype(jnp.float32) + project(q)
    for j in (1, 3, 2):
        at = lax.rem(q + j, 4)
        remote(ps.at[at], pr.at[at], p_send.at[j], p_recv.at[at], (at // 2, g, lax.rem(at, 2))).wait_recv()
        stream = stream + pr[at].astype(jnp.float32)
    mixed[...] = stream

    square = jnp.sum(stream * stream, axis=1, keepdims=True)
    ss[q] = jnp.broadcast_to(square, (rows, HEAD_DIM)).T[0:8, :]
    for j in (1, 2, 3):
        to = lax.rem(q + j, 4)
        remote(ss.at[q], ss.at[q], s_send.at[j], s_recv.at[q], (to // 2, g, lax.rem(to, 2))).start()
    for j in (1, 2, 3):
        at = lax.rem(q + j, 4)
        remote(ss.at[at], ss.at[at], s_send.at[j], s_recv.at[at], (at // 2, g, lax.rem(at, 2))).wait_recv()
    square = ss[0] + ss[1] + ss[2] + ss[3]
    square = jnp.broadcast_to(square[0:1, :], (rows, HEAD_DIM)).T[:, 0:1]
    inverse = lax.rsqrt(square * (1.0 / (4 * wide)) + 1e-06)
    nb[...] = (stream * inverse * gain_ref[:, mine]).astype(jnp.bfloat16)

    @pl.when(s == y)
    def _():
        xb[z, q] = nb[...]

    @pl.when(s != y)
    def _():
        remote(nb, xb.at[z, q], n_send.at[0], x_recv.at[z, q], core_peer).start()

    @pl.when(s == 1)
    def _():
        remote(nb, xb.at[z, q], n_send.at[1], x_recv.at[z, q], (y, g, 1 - m)).start()

    for i, (hbm, vmem) in enumerate(weights):
        pltpu.make_async_copy(hbm.at[0], vmem.at[own_hidden], w_local.at[i]).wait()
        remote(hbm.at[0], vmem.at[peer_hidden], w_send.at[i], w_recv.at[i], core_peer).wait()

    def slot_of(i):
        at = near(i)
        return at * 2 + s, at

    def take_tokens(at, piece):
        remote(nb, xb.at[at, piece], n_send.at[0], x_recv.at[at, piece], x_peer).wait_recv()

    def forward(i):
        asker, at = slot_of(i)
        for piece in (m, 2, 3):

            @pl.when((asker != g) | (piece != q))
            def _():
                take_tokens(at, piece)

            if piece is m:
                remote(xb.at[at, m], xb.at[at, m], f_send.at[at], x_recv.at[at, m], x_peer).start()

            @pl.when(s == y)
            def _():
                relay(at, xb.at[at, piece], x_send.at[at, piece], x_recv.at[at, piece], s, m)


    def compute(i):
        asker, at = slot_of(i)
        take_tokens(at, 1 - m)
        tokens = jnp.concatenate([xb[at, piece] for piece in range(4)], axis=1)
        gate = contract_last(tokens, wg[...])
        up = contract_last(tokens, wu[...])
        hidden = (gate / (1.0 + jnp.exp(-gate)) * up).astype(jnp.bfloat16)

        def down(piece):
            cols = pl.ds(pl.multiple_of(piece * wide, wide), wide)
            return jnp.dot(hidden, wd[:, cols], preferred_element_type=jnp.float32)

        for c in range(2):
            ys[at, c] = down(2 * c + 1 - m).astype(jnp.bfloat16)
            remote(ys.at[at, c], yr.at[at, c], y_send.at[at, c], y_recv.at[at, c], x_peer).start()
        for c in range(2):
            yown[at, c] = down(2 * c + m)

    def give_back(i):
        asker, at = slot_of(i)
        for c in range(2):
            remote(ys.at[at, c], yr.at[at, c], y_send.at[at, c], y_recv.at[at, c], x_peer).wait_recv()
            rs[at, c] = (yown[at, c] + yr[at, c].astype(jnp.float32)).astype(jnp.bfloat16)
            is_mine = (asker == g) & (c == s)

            @pl.when(is_mine)
            def _():
                rb[g] = rs[at, c]

            @pl.when(jnp.logical_not(is_mine))
            def _():
                remote(rs.at[at, c], rb.at[g], r_send.at[at, c], r_recv.at[g], (c, asker, m)).start()

    def step(t, carry):
        @pl.when(t < half)
        def _():
            forward(t)

        @pl.when((t >= 1) & (t <= half))
        def _():
            compute(t - 1)

        @pl.when(t >= 2)
        def _():
            give_back(t - 2)

        return carry

    lax.fori_loop(0, half + 2, step, 0)

    share = jnp.zeros((groups, rows), jnp.float32)
    expert = lax.broadcasted_iota(jnp.int32, (groups, rows), 0)
    for k in range(TOPK):
        named = jnp.broadcast_to(ids_ref[k : k + 1, :], (groups, rows)) == expert
        share += jnp.where(named, jnp.broadcast_to(gates_ref[k : k + 1, :], (groups, rows)), 0.0)
    share = jnp.concatenate([share, jnp.zeros((HEAD_DIM - groups, rows), jnp.float32)], axis=0).T
    stream = mixed[...]
    for e in range(groups):

        @pl.when((e != g) | (s != y))
        def _():
            remote(rs.at[0, 0], rb.at[e], r_send.at[0, 0], r_recv.at[e], core_peer).wait_recv()

        stream = stream + share[:, e : e + 1] * rb[e].astype(jnp.float32)
    out_ref[...] = stream.astype(jnp.bfloat16)

    def drain(k, carry):
        other = lax.rem(g + k, groups)
        remote(mls.at[0], mlr.at[g], l_send.at[other], l_recv.at[g], x_peer).wait_send()
        remote(os.at[0], orv.at[g], o_send.at[other], o_recv.at[g], x_peer).wait_send()
        return carry

    lax.fori_loop(1, groups, drain, 0)

    @pl.when(s != y)
    def _():
        remote(nb, xb.at[z, q], n_send.at[0], x_recv.at[z, q], core_peer).wait_send()

    @pl.when(s == 1)
    def _():
        remote(nb, xb.at[z, q], n_send.at[1], x_recv.at[z, q], x_peer).wait_send()

    for j in (1, 2, 3):
        remote(ps.at[0], pr.at[q], p_send.at[j], p_recv.at[q], core_peer).wait_send()
        remote(ss.at[q], ss.at[q], s_send.at[j], s_recv.at[q], core_peer).wait_send()

    def drain_slot(i, carry):
        asker, at = slot_of(i)
        src = at * 2 + y
        relay_done(at, mb.at[src], m_send.at[src], m_recv.at[src])
        relay_done(at, qb.at[src], q_send.at[src], q_recv.at[src])
        for piece in (m, 2, 3):

            @pl.when(s == y)
            def _():
                relay_done(at, xb.at[at, piece], x_send.at[at, piece], x_recv.at[at, piece])

        remote(xb.at[at, m], xb.at[at, m], f_send.at[at], x_recv.at[at, m], x_peer).wait_send()
        for c in range(2):
            remote(ys.at[at, c], yr.at[at, c], y_send.at[at, c], y_recv.at[at, c], x_peer).wait_send()

            @pl.when((asker != g) | (c != s))
            def _():
                remote(rs.at[at, c], rb.at[g], r_send.at[at, c], r_recv.at[g], core_peer).wait_send()

        return carry

    lax.fori_loop(0, half, drain_slot, 0)


def local_dense(
    qkv,
    kv_cache,
    residual,
    out_weight,
    moe_gain,
    w_gate,
    w_up,
    w_down,
    seg_ids,
    prefix_blocks,
    owners,
    slot_ids,
    expert_ids,
    gate_weights,
):
    groups = lax.axis_size("dp")
    rows = qkv.shape[0]
    model_width = residual.shape[1]
    wide = model_width // 4
    half = groups // 2
    hid = w_gate.shape[2]
    slots = kv_cache.shape[0]
    kv = kv_cache.reshape(slots * BLK, kv_cache.shape[2])
    bf, f32 = jnp.bfloat16, jnp.float32
    dma = pltpu.SemaphoreType.DMA
    vmem = pl.BlockSpec(memory_space=pltpu.VMEM)
    smem = pl.BlockSpec(memory_space=pltpu.SMEM)
    anywhere = pl.BlockSpec(memory_space=pl.ANY)
    return pl.pallas_call(
        partial(layer_kernel, groups),
        out_shape=jax.ShapeDtypeStruct((rows, wide), bf),
        in_specs=[anywhere] * 4 + [vmem] + [anywhere] * 3 + [vmem, smem, vmem, vmem, vmem, vmem],
        out_specs=vmem,
        scratch_shapes=[
            pltpu.VMEM(qkv.shape, bf),
            pltpu.VMEM(kv.shape, bf),
            pltpu.VMEM(residual.shape, bf),
            pltpu.VMEM(out_weight.shape, bf),
            pltpu.VMEM((2 * hid, model_width), bf),
            pltpu.VMEM((2 * hid, model_width), bf),
            pltpu.VMEM((2 * hid, model_width), bf),
            pltpu.VMEM((groups, rows, 2 * HEAD_DIM), bf),
            pltpu.VMEM((groups, 8, HEAD_DIM), jnp.int32),
            pltpu.VMEM((groups, rows, 2 * HEAD_DIM), bf),
            pltpu.VMEM((groups, rows, 2 * HEAD_DIM), bf),
            pltpu.VMEM((groups, 8, HEAD_DIM), f32),
            pltpu.VMEM((groups, 8, HEAD_DIM), f32),
            pltpu.VMEM((4, rows, wide), bf),
            pltpu.VMEM((4, rows, wide), bf),
            pltpu.VMEM((4, 8, HEAD_DIM), f32),
            pltpu.VMEM((rows, wide), bf),
            pltpu.VMEM((half, 4, rows, wide), bf),
            pltpu.VMEM((half, 2, rows, wide), f32),
            pltpu.VMEM((half, 2, rows, wide), bf),
            pltpu.VMEM((half, 2, rows, wide), bf),
            pltpu.VMEM((half, 2, rows, wide), bf),
            pltpu.VMEM((groups, rows, wide), bf),
            pltpu.VMEM((rows, wide), f32),
            dma((4,)),
            dma((3,)),
            dma((3,)),
            dma((3,)),
            dma((groups, 3)),
            dma((groups,)),
            dma((groups, 3)),
            dma((groups,)),
            dma((groups,)),
            dma((groups,)),
            dma((groups,)),
            dma((groups,)),
            dma((4,)),
            dma((4,)),
            dma((4,)),
            dma((4,)),
            dma((2,)),
            dma((half, 4, 3)),
            dma((half, 4)),
            dma((half,)),
            dma((half, 2)),
            dma((half, 2)),
            dma((half, 2)),
            dma((groups,)),
        ],
        compiler_params=pltpu.CompilerParams(
            collective_id=0, has_side_effects=True, vmem_limit_bytes=60 * 1024 * 1024
        ),
    )(
        qkv,
        kv,
        residual,
        out_weight,
        moe_gain.reshape(1, -1),
        jnp.swapaxes(w_gate, 1, 2),
        jnp.swapaxes(w_up, 1, 2),
        w_down,
        seg_ids[0],
        prefix_blocks[0],
        owners[:, 0, :, 0],
        slot_ids[:, 0, :],
        expert_ids.T,
        gate_weights.T,
    )


def solution(mesh):
    dense = mesh.shape["dp"] <= DENSE_GROUPS
    return jax.shard_map(
        local_dense if dense else local_sparse,
        mesh=mesh,
        in_specs=(
            P("dp", ("section", "mp")),
            P("dp", None, ("section", "mp")),
            P("dp", None),
            P(("section", "mp"), None),
            P(),
            P("dp", None, ("section", "mp")),
            P("dp", None, ("section", "mp")),
            P("dp", ("section", "mp"), None),
            P("dp", None, None),
            P("dp", None, None),
            P(),
            P(),
            P("dp", None),
            P("dp", None),
        ),
        out_specs=P("dp", ("section", "mp")),
        check_vma=False,
    )
```
